32 devices in a mesh: groups: 2 (over y), blk: 4 (over z), leaf: 2 (over x), rhs: 2 (over core).
Axes of the slice: x: 2, y: 2, z: 4, core: 2. Of those that a mesh axis runs over, the one named last changes fastest.
Arguments:
- points: float32 [3, 32768], P(None, 'groups'), parts along dimension 1, may hold values from -1 to 1
- charges: bfloat16 [32768, 64], P(('groups', 'blk'), 'rhs'), parts along dimension 0, may hold values from -6 to 6
- basis: bfloat16 [32, 32768], P(None, ('groups', 'blk')), parts along dimension 1, may hold values from -0.5 to 0.5
- couplings: bfloat16 [256, 32, 32, 32], P(('groups', 'blk', 'leaf')), parts along dimension 0, may hold values from -0.1875 to 0.1875
- near_src: int32 [256, 27], P(('groups', 'blk', 'leaf')), parts along dimension 0, may hold values from 0 to 127, as said below
- far_src: int32 [256, 32], P('groups'), parts along dimension 0, may hold values from 0 to 127, as said below
Outputs:
- potential: bfloat16 [32768, 64], P(('groups', 'blk', 'leaf'), 'rhs'), parts along dimension 0
The draws below stay inside these ranges and needn't reach their ends.
There are 2 independent parts, one for each index of `groups`. The reference program is written for one: setup_inputs(seed, part) draws one part's arguments, and reference() takes and returns one part's arrays. A program takes and returns all parts, laid end to end along the dimension named above; each array names one. Nothing has to cross between parts.
Inputs may be any that keep to these rules, and one draw needn't show every extreme that they name: `near_src`: target cluster t lies in segment t // 32; every near cluster of t lies in that segment or in the one before or after it, cyclically over the 4 segments. `far_src`: the target clusters 16 * d to 16 * d + 15 form one group; among that group's 16 * 32 list entries at most 128 name clusters of one segment, and in every group some segment is named exactly 128 times.
All inputs are finite; a program needn't handle non-finite values.
Results may differ from the reference program's by a relative error of at most 0.0055.
Values may be sent and summed in bfloat16 or wider, within the bound.
No kernel may reach another device: no remote copies, remote signals or barrier semaphores. Data moves between devices by JAX's collectives and lax.ppermute only.
A program may use at most 128 MiB of HBM per device.

```python
import jax
import jax.numpy as jnp
from jax import lax

LEAF = 128
K = 32
R = 64
NNEAR = 27
NFAR = 32
C_DEV = 16
SEG = 32
NCL = 128
P_SIZE = 16384
CAP = 128


def draw_near_src(key, part):
    key = jax.random.fold_in(key, 11)
    key_step, key_local = jax.random.split(key)
    segment_total = NCL // SEG
    own_segment = jnp.arange(NCL, dtype=jnp.int32)[:, None] // SEG
    offset = jax.random.randint(key_step, (NCL, NNEAR), -1, 2)
    local = jax.random.randint(key_local, (NCL, NNEAR), 0, SEG)
    segment = (own_segment + offset + segment_total) % segment_total
    return (segment * SEG + local).astype(jnp.int32)


def group_entries(key):
    segment_total = NCL // SEG
    entry_total = C_DEV * NFAR
    key_star, key_order, key_mix, key_local = jax.random.split(key, 4)
    star = jax.random.randint(key_star, (), 0, segment_total)
    cells = jnp.arange(segment_total * CAP, dtype=jnp.int32)
    owner = cells // CAP
    shuffled = jax.random.permutation(key_order, segment_total * CAP).astype(jnp.int32)
    priority = jnp.where(owner == star, cells % CAP - CAP, shuffled)
    chosen = jnp.argsort(priority, stable=True)[:entry_total]
    owners = owner[chosen]
    owners = owners[jax.random.permutation(key_mix, entry_total)]
    local = jax.random.randint(key_local, (entry_total,), 0, SEG)
    return owners * SEG + local


def draw_far_src(key, part):
    key = jax.random.fold_in(key, 23)
    group_keys = jax.random.split(key, NCL // C_DEV)
    entries = jax.vmap(group_entries)(group_keys)
    return entries.reshape(NCL, NFAR).astype(jnp.int32)


def steps_of(own_key, dims, cuts, least, high):
    gain = 1.0
    for dim, shards_of in cuts:
        heights = jax.random.uniform(jax.random.fold_in(jax.random.fold_in(own_key, 6), dim), (shards_of,), jnp.float32, least / len(cuts), high / len(cuts))
        gain = gain * jnp.repeat(jnp.exp(heights), dims[dim] // shards_of).reshape((-1,) + (1,) * (len(dims) - 1 - dim))
    return gain


def scatter_about(own_key, shape, spread, bound, shards=(), kind=jnp.bfloat16):
    values = jax.random.normal(own_key, shape, jnp.float32) * spread
    if len(shards) > 0:
        values = steps_of(own_key, shape, shards, -0.22, 0.18) * values
    return jnp.clip(values, min=-bound, max=bound).astype(kind)


def setup_inputs(seed: int = 0, part: int = 0) -> dict:
    keys = jax.random.split(jax.random.key(seed), 7)
    own_keys = jax.random.split(jax.random.fold_in(keys[6], part), 7)
    return {
        "points": jnp.clip(jax.random.uniform(own_keys[0], (3, P_SIZE), jnp.float32, -1.0, 1.0), -1.0, 1.0),
        "charges": scatter_about(own_keys[1], (P_SIZE, R), 1.0, 6.0, ((0, 4), (1, 2))),
        "basis": scatter_about(own_keys[2], (K, P_SIZE), LEAF ** -0.5, 0.5, ((1, 4),)),
        "couplings": scatter_about(own_keys[3], (NCL, NFAR, K, K), (K * NFAR) ** -0.5, 0.1875, ((0, 8),)),
        "near_src": draw_near_src(jax.random.fold_in(jax.random.fold_in(keys[6], part), 71), part),
        "far_src": draw_far_src(jax.random.fold_in(jax.random.fold_in(keys[6], part), 71), part),
    }


kernel_scale = 0.0625 / (4.0 * 3.141592653589793)
soften = 0.001

def near_kernel(target_coords, source_coords):
    diff_zero = target_coords[0][None, :, None] - source_coords[0][:, None, :]
    diff_one = target_coords[1][None, :, None] - source_coords[1][:, None, :]
    diff_two = target_coords[2][None, :, None] - source_coords[2][:, None, :]
    radius_sq = diff_zero * diff_zero + diff_one * diff_one + diff_two * diff_two
    return (kernel_scale * lax.rsqrt(radius_sq + soften)).astype(jnp.bfloat16)

def reference(points, charges, basis, couplings, near_src, far_src):
    cluster_total = near_src.shape[0]
    coords = points.reshape(3, cluster_total, LEAF)
    charge_blocks = charges.reshape(cluster_total, LEAF, R)
    basis_blocks = basis.reshape(K, cluster_total, LEAF)
    skeleton = jnp.einsum('ksl,slr->skr', basis_blocks.astype(jnp.float32), charge_blocks.astype(jnp.float32)).astype(jnp.bfloat16)

    def one_target(target):
        near_ids = near_src[target]
        kernel = near_kernel(coords[:, target, :], coords[:, near_ids, :])
        near = jnp.einsum('jts,jsr->tr', kernel.astype(jnp.float32), charge_blocks[near_ids].astype(jnp.float32))
        coefficient = jnp.einsum('fkl,flr->kr', couplings[target].astype(jnp.float32), skeleton[far_src[target]].astype(jnp.float32)).astype(jnp.bfloat16)
        far = jnp.einsum('kt,kr->tr', basis_blocks[:, target, :].astype(jnp.float32), coefficient.astype(jnp.float32))
        return (near + far).astype(jnp.bfloat16)
    result = lax.map(one_target, jnp.arange(cluster_total, dtype=jnp.int32))
    return result.reshape(cluster_total * LEAF, R)
```

```python
import functools

import jax
import jax.numpy as jnp
from jax import lax
from jax.experimental import pallas as pl
from jax.experimental.pallas import tpu as pltpu
from jax.sharding import PartitionSpec as P

LEAF = 128
BATCH = 12
DEPTH = 48

kernel_scale = 0.0625 / (4.0 * 3.141592653589793)
soften = 0.001
inverse_sq = 1.0 / (kernel_scale * kernel_scale)

bf16 = jnp.bfloat16
f32 = jnp.float32
VMEM = pl.BlockSpec(memory_space=pltpu.VMEM)
SMEM = pl.BlockSpec(memory_space=pltpu.SMEM)
PARAMS = pltpu.CompilerParams(vmem_limit_bytes=48 * 2**20)


def shifted(block, axis, shift):
    count = lax.axis_size(axis)
    return lax.ppermute(block, axis, [(i, (i + shift) % count) for i in range(count)])


def cluster(index):
    return pl.ds(pl.multiple_of(index * LEAF, LEAF), LEAF)


def list_kernel(seg_size, near_ref, basis_ref, charges_ref, own_ref, prev_ref, next_ref, skel_ref):
    targets = near_ref.shape[0] // 2
    near_count = near_ref.shape[1]
    blk_count = lax.axis_size("blk")
    blk = lax.axis_index("blk")
    before = lax.rem(blk + blk_count - 1, blk_count)
    row = lax.axis_index("rhs") * targets
    last = own_ref.shape[0] - 1
    zero = jnp.int32(0)

    def one_target(target, counts):
        own, prev, after = counts
        for j in range(near_count):
            source = near_ref[row + target, j]
            segment = lax.div(source, seg_size)
            code = target * 256 + (source - segment * seg_size)
            is_own = (segment == blk).astype(jnp.int32)
            is_prev = (segment == before).astype(jnp.int32) * (1 - is_own)
            own_ref[own] = code
            prev_ref[prev] = code
            next_ref[after] = code
            own = own + is_own
            prev = prev + is_prev
            after = after + (1 - is_own - is_prev)
        return own, prev, after

    own, prev, after = lax.fori_loop(0, targets, one_target, (zero, zero, zero))
    own_ref[last] = own
    prev_ref[last] = prev
    next_ref[last] = after

    columns = charges_ref.shape[0]
    rank = basis_ref.shape[0]
    pack = LEAF // columns
    for group in range(seg_size // pack):
        rows = []
        for i in range(pack):
            at = (group * pack + i) * LEAF
            parts = [jnp.zeros((columns, LEAF), bf16)] * pack
            parts[i] = charges_ref[:, at : at + LEAF]
            rows.append(jnp.concatenate(parts, axis=1))
        spread = jnp.concatenate(rows, axis=0)
        at = group * pack * LEAF
        block = lax.dot_general(
            basis_ref[:, at : at + pack * LEAF],
            spread,
            (((1,), (1,)), ((), ())),
            preferred_element_type=f32,
        )
        skel_ref[group * rank : (group + 1) * rank, :] = block.astype(bf16)


def split(value):
    high = value.astype(bf16).astype(f32)
    rest = value - high
    middle = rest.astype(bf16).astype(f32)
    return high, middle, rest - middle


def coords_of(points_ref, at):
    block = points_ref[:, cluster(at)]
    zero, one, two = block[0:1, :], block[1:2, :], block[2:3, :]
    return zero, one, two, zero * zero + one * one + two * two


def rows_of(values):
    row = lax.broadcasted_iota(jnp.int32, (8, LEAF), 0)
    out = jnp.zeros((8, LEAF), f32)
    for i, value in enumerate(values):
        out = jnp.where(row == i, value, out)
    return out


def target_features(points_ref, at):
    zero, one, two, norm = coords_of(points_ref, at)
    slope = -2.0 * inverse_sq
    rows = rows_of((zero * slope, one * slope, two * slope, (norm + soften) * inverse_sq, 1.0))
    high, middle, low = split(rows)
    return jnp.concatenate([high, high, middle, middle, high, low], axis=0).astype(bf16)


def source_features(points_ref, at):
    zero, one, two, norm = coords_of(points_ref, at)
    rows = rows_of((zero, one, two, 1.0, norm * inverse_sq))
    high, middle, low = split(rows)
    stacked = jnp.concatenate([high, middle, high, middle, low, high], axis=0)
    return jnp.transpose(stacked).astype(bf16)


def feature_kernel(seg_size, targets, leaf_clusters, points_ref, target_ref, source_ref):
    blk_count = lax.axis_size("blk")
    blk = lax.axis_index("blk")
    first = lax.axis_index("leaf") * leaf_clusters + lax.axis_index("rhs") * targets
    for which in range(3):
        segment = lax.rem(blk + which + blk_count - 1, blk_count)
        for i in range(targets):
            target_ref[which * targets + i] = target_features(
                points_ref, segment * seg_size + first + i
            )
    target_ref[3 * targets] = jnp.zeros((DEPTH, LEAF), bf16)

    def some_sources(step, carry):
        for u in range(8):
            at = step * 8 + u
            source_ref[at] = source_features(points_ref, blk * seg_size + at)
        return carry

    lax.fori_loop(0, seg_size // 8, some_sources, 0)


def near_kernel(base, list_ref, target_ref, source_ref, mine_ref, other_ref, out_ref, total, even, odd):
    targets = total.shape[0] - 1
    length = list_ref[list_ref.shape[0] - 1]
    batches = lax.div(length + (BATCH - 1), BATCH)
    total[...] = jnp.zeros_like(total)

    def pair(batch, u):
        at = batch * BATCH + u
        code = jnp.where(at < length, list_ref[at], targets * 256)
        return lax.shift_right_logical(code, 8), lax.bitwise_and(code, 255)

    def make(batch, slot):
        for u in range(BATCH):
            target, source = pair(batch, u)
            square = jnp.dot(source_ref[source], target_ref[base + target], preferred_element_type=f32)
            slot[u] = lax.rsqrt(square).astype(bf16)

    def use(batch, slot):
        sums = []
        for u in range(BATCH):
            target, source = pair(batch, u)
            charges = jnp.concatenate([mine_ref[:, cluster(source)], other_ref[:, cluster(source)]], axis=0)
            sums.append((target, jnp.dot(charges, slot[u], preferred_element_type=f32)))
        for target, value in sums:
            total[target] += value

    make(0, even)

    def body(step, carry):
        make(2 * step + 1, odd)
        use(2 * step, even)
        make(2 * step + 2, even)
        use(2 * step + 1, odd)
        return carry

    lax.fori_loop(0, lax.div(batches + 1, 2), body, 0)
    for i in range(targets):
        out_ref[:, i * LEAF : (i + 1) * LEAF] = total[i].astype(out_ref.dtype)


def near_sum(base, targets, pairs, target_rows, source_rows, mine, other, dtype):
    columns = 2 * mine.shape[0]
    return pl.pallas_call(
        functools.partial(near_kernel, base),
        out_shape=jax.ShapeDtypeStruct((columns, targets * LEAF), dtype),
        in_specs=[SMEM] + [VMEM] * 4,
        out_specs=VMEM,
        scratch_shapes=[
            pltpu.VMEM((targets + 1, columns, LEAF), f32),
            pltpu.VMEM((BATCH, LEAF, LEAF), bf16),
            pltpu.VMEM((BATCH, LEAF, LEAF), bf16),
        ],
        compiler_params=PARAMS,
    )(pairs, target_rows, source_rows, mine, other)


def far_kernel(seg_size, far_ref, couplings_ref, basis_ref, *refs):
    parts, (out_ref, skel) = refs[:-2], refs[-2:]
    clusters = couplings_ref.shape[0]
    far_count = couplings_ref.shape[1]
    rank = couplings_ref.shape[2]
    columns = out_ref.shape[0]
    pack = LEAF // columns
    leaf = lax.axis_index("leaf") * clusters
    for order, part in enumerate(parts):
        def unpack(group, carry, order=order, part=part):
            block = part[pl.ds(pl.multiple_of(group * rank, rank), rank), :]
            for i in range(pack):
                skel[order * seg_size + group * pack + i] = block[:, i * columns : (i + 1) * columns]
            return carry
        groups = part.shape[0] // rank
        lax.fori_loop(0, groups, unpack, 0)

    for target in range(clusters):
        coefficient = jnp.zeros((rank, columns), f32)
        step = 256 // rank
        for at in range(0, far_count, step):
            left = jnp.concatenate([couplings_ref[target, at + i] for i in range(step)], axis=1)
            rows = []
            for i in range(step):
                rows.append(skel[far_ref[target, at + i]])
            coefficient = coefficient + jnp.dot(
                left, jnp.concatenate(rows, axis=0), preferred_element_type=f32
            )
        own_basis = basis_ref[:, cluster(leaf + target)]
        out_ref[:, target * LEAF : (target + 1) * LEAF] = lax.dot_general(
            coefficient.astype(bf16),
            own_basis,
            (((0,), (0,)), ((), ())),
            preferred_element_type=f32,
        )


def on_device(points, charges, basis, couplings, near_src, far_src):
    blk_count = lax.axis_size("blk")
    mine = charges.T
    columns, seg_rows = mine.shape
    seg_size = seg_rows // LEAF
    rank = basis.shape[0]
    own_clusters, near_count = near_src.shape
    targets = own_clusters // 2
    cluster_total = seg_size * blk_count
    other = shifted(mine, "rhs", 1)

    list_size = -(-(targets * near_count + 4 * BATCH + 1) // 128) * 128
    pack = LEAF // columns
    own_list, prev_list, next_list, skeleton = pl.pallas_call(
        functools.partial(list_kernel, seg_size),
        out_shape=[jax.ShapeDtypeStruct((list_size,), jnp.int32)] * 3
        + [jax.ShapeDtypeStruct((seg_size // pack * rank, LEAF), bf16)],
        in_specs=[SMEM, VMEM, VMEM],
        out_specs=[SMEM, SMEM, SMEM, VMEM],
        compiler_params=PARAMS,
    )(near_src, basis, mine)

    after_list = shifted(prev_list, "blk", -1)
    before_list = shifted(next_list, "blk", 1)
    if blk_count == 4:
        skeletons = [skeleton] + [shifted(skeleton, "blk", -i) for i in range(1, blk_count)]
    else:
        skeletons = [lax.all_gather(skeleton, "blk", axis=0, tiled=True)]

    target_rows, source_rows = pl.pallas_call(
        functools.partial(feature_kernel, seg_size, targets, own_clusters),
        out_shape=[
            jax.ShapeDtypeStruct((3 * targets + 1, DEPTH, LEAF), bf16),
            jax.ShapeDtypeStruct((seg_size, LEAF, DEPTH), bf16),
        ],
        in_specs=[VMEM],
        out_specs=[VMEM, VMEM],
        compiler_params=PARAMS,
    )(points)
    own_near = near_sum(targets, targets, own_list, target_rows, source_rows, mine, other, f32)
    to_before = near_sum(0, targets, before_list, target_rows, source_rows, mine, other, bf16)
    from_after = shifted(to_before, "blk", -1)
    to_after = near_sum(2 * targets, targets, after_list, target_rows, source_rows, mine, other, bf16)
    from_before = shifted(to_after, "blk", 1)

    blk = lax.axis_index("blk")
    first = blk * seg_size + lax.axis_index("leaf") * own_clusters
    entries = lax.dynamic_slice_in_dim(far_src, first, own_clusters, 0)
    if len(skeletons) > 1:
        entries = lax.rem(entries + (blk_count - blk) * seg_size, cluster_total)
    far = pl.pallas_call(
        functools.partial(far_kernel, seg_size),
        out_shape=jax.ShapeDtypeStruct((columns, own_clusters * LEAF), f32),
        in_specs=[SMEM] + [VMEM] * (2 + len(skeletons)),
        out_specs=VMEM,
        scratch_shapes=[pltpu.VMEM((cluster_total, rank, columns), bf16)],
        compiler_params=PARAMS,
    )(entries, couplings, basis, *skeletons)

    near = own_near + from_before.astype(f32) + from_after.astype(f32)
    keep = near[:columns]
    got = shifted(near[columns:], "rhs", 1)
    even = lax.axis_index("rhs") == 0
    whole = jnp.concatenate([jnp.where(even, keep, got), jnp.where(even, got, keep)], axis=1)
    return (whole + far).astype(bf16).T


def solution(mesh):
    in_specs = (
        P(None, "groups"),
        P(("groups", "blk"), "rhs"),
        P(None, ("groups", "blk")),
        P(("groups", "blk", "leaf"), None, None, None),
        P(("groups", "blk", "leaf"), None),
        P("groups", None),
    )
    out_specs = P(("groups", "blk", "leaf"), "rhs")
    return jax.shard_map(
        on_device, mesh=mesh, in_specs=in_specs, out_specs=out_specs, check_vma=False
    )
```

```python
import functools

import jax
import jax.numpy as jnp
from jax import lax
from jax.experimental import pallas as pl
from jax.experimental.pallas import tpu as pltpu
from jax.sharding import PartitionSpec as P

LEAF = 128
BATCH = 12
DEPTH = 48

kernel_scale = 0.0625 / (4.0 * 3.141592653589793)
soften = 0.001
inverse_sq = 1.0 / (kernel_scale * kernel_scale)

bf16 = jnp.bfloat16
f32 = jnp.float32
VMEM = pl.BlockSpec(memory_space=pltpu.VMEM)
ANY = pl.BlockSpec(memory_space=pl.ANY)
SMEM = pl.BlockSpec(memory_space=pltpu.SMEM)
PARAMS = pltpu.CompilerParams(vmem_limit_bytes=48 * 2**20)


def cost(microseconds):
    return pl.CostEstimate(flops=int(microseconds * 1e9), bytes_accessed=0, transcendentals=0)


def shifted(block, axis, shift):
    count = lax.axis_size(axis)
    return lax.ppermute(block, axis, [(i, (i + shift) % count) for i in range(count)])


def cluster(index):
    return pl.ds(pl.multiple_of(index * LEAF, LEAF), LEAF)


def list_kernel(seg_size, near_hbm, basis_hbm, charges_hbm, own_ref, prev_ref, next_ref, near_ref, basis_ref, charges_ref, sems):
    copies = [
        pltpu.make_async_copy(near_hbm, near_ref, sems.at[0]),
        pltpu.make_async_copy(basis_hbm, basis_ref, sems.at[1]),
        pltpu.make_async_copy(charges_hbm, charges_ref, sems.at[2]),
    ]
    for copy in copies:
        copy.start()
    targets = near_ref.shape[0] // 2
    near_count = near_ref.shape[1]
    blk_count = lax.axis_size("blk")
    blk = lax.axis_index("blk")
    before = lax.rem(blk + blk_count - 1, blk_count)
    row = lax.axis_index("rhs") * targets
    place = lax.broadcasted_iota(jnp.int32, (8, LEAF), 0) * LEAF + lax.broadcasted_iota(jnp.int32, (8, LEAF), 1)
    zero = jnp.int32(0)
    blank = jnp.zeros((8, LEAF), jnp.int32)
    copies[0].wait()

    def one_target(target, carry):
        own, prev, after, prev_list, next_list = carry
        for j in range(near_count):
            source = near_ref[row + target, j]
            segment = lax.div(source, seg_size)
            code = target * 256 + (source - segment * seg_size)
            is_own = segment == blk
            is_prev = jnp.logical_and(segment == before, jnp.logical_not(is_own))
            is_next = jnp.logical_not(jnp.logical_or(is_own, is_prev))
            own_ref[lax.shift_right_logical(own, 7), lax.bitwise_and(own, 127)] = code
            prev_list = jnp.where(place == jnp.where(is_prev, prev, -1), code, prev_list)
            next_list = jnp.where(place == jnp.where(is_next, after, -1), code, next_list)
            own = own + is_own.astype(jnp.int32)
            prev = prev + is_prev.astype(jnp.int32)
            after = after + is_next.astype(jnp.int32)
        return own, prev, after, prev_list, next_list

    own, prev, after, prev_list, next_list = lax.fori_loop(
        0, targets, one_target, (zero, zero, zero, blank, blank)
    )
    own_ref[7, LEAF - 1] = own
    columns = charges_ref.shape[0]
    rank = basis_ref.shape[0]
    pack = LEAF // columns
    rows_end = seg_size // pack * rank
    for out, count, entries in ((prev_ref, prev, prev_list), (next_ref, after, next_list)):
        entries = jnp.where(place == 8 * LEAF - 1, count, entries)
        both = jnp.concatenate([lax.bitwise_and(entries, 255), lax.shift_right_logical(entries, 8)], axis=0)
        out[rows_end : rows_end + 16, :] = both.astype(f32).astype(bf16)

    copies[1].wait()
    copies[2].wait()
    for group in range(seg_size // pack):
        rows = []
        for i in range(pack):
            at = (group * pack + i) * LEAF
            parts = [jnp.zeros((columns, LEAF), bf16)] * pack
            parts[i] = charges_ref[:, at : at + LEAF]
            rows.append(jnp.concatenate(parts, axis=1))
        spread = jnp.concatenate(rows, axis=0)
        at = group * pack * LEAF
        block = lax.dot_general(
            basis_ref[:, at : at + pack * LEAF],
            spread,
            (((1,), (1,)), ((), ())),
            preferred_element_type=f32,
        ).astype(bf16)
        prev_ref[group * rank : (group + 1) * rank, :] = block
        next_ref[group * rank : (group + 1) * rank, :] = block


def split(value):
    high = value.astype(bf16).astype(f32)
    rest = value - high
    middle = rest.astype(bf16).astype(f32)
    return high, middle, rest - middle


def coords_of(points_ref, at):
    block = points_ref[:, cluster(at)]
    zero, one, two = block[0:1, :], block[1:2, :], block[2:3, :]
    return zero, one, two, zero * zero + one * one + two * two


def rows_of(values):
    row = lax.broadcasted_iota(jnp.int32, (8, LEAF), 0)
    out = jnp.zeros((8, LEAF), f32)
    for i, value in enumerate(values):
        out = jnp.where(row == i, value, out)
    return out


def target_features(points_ref, at):
    zero, one, two, norm = coords_of(points_ref, at)
    slope = -2.0 * inverse_sq
    rows = rows_of((zero * slope, one * slope, two * slope, (norm + soften) * inverse_sq, 1.0))
    high, middle, low = split(rows)
    return jnp.concatenate([high, high, middle, middle, high, low], axis=0).astype(bf16)


def source_features(points_ref, at):
    zero, one, two, norm = coords_of(points_ref, at)
    rows = rows_of((zero, one, two, 1.0, norm * inverse_sq))
    high, middle, low = split(rows)
    stacked = jnp.concatenate([high, middle, high, middle, low, high], axis=0)
    return jnp.transpose(stacked).astype(bf16)


def feature_kernel(seg_size, targets, leaf_clusters, points_ref, target_ref, source_ref):
    blk_count = lax.axis_size("blk")
    blk = lax.axis_index("blk")
    first = lax.axis_index("leaf") * leaf_clusters + lax.axis_index("rhs") * targets
    for which in range(3):
        segment = lax.rem(blk + which + blk_count - 1, blk_count)
        for i in range(targets):
            target_ref[which * targets + i] = target_features(
                points_ref, segment * seg_size + first + i
            )
    target_ref[3 * targets] = jnp.zeros((DEPTH, LEAF), bf16)

    def some_sources(step, carry):
        for u in range(8):
            at = step * 8 + u
            source_ref[at] = source_features(points_ref, blk * seg_size + at)
        return carry

    lax.fori_loop(0, seg_size // 8, some_sources, 0)


def near_kernel(base, list_ref, target_ref, source_ref, mine_ref, other_ref, out_ref, total, held):
    targets = total.shape[0] - 1
    length = list_ref[7, LEAF - 1]
    batches = lax.div(length + (BATCH - 1), BATCH)
    total[...] = jnp.zeros_like(total)

    def pair(batch, u):
        at = batch * BATCH + u
        code = list_ref[lax.shift_right_logical(at, 7), lax.bitwise_and(at, 127)]
        code = jnp.where(at < length, code, targets * 256)
        return lax.shift_right_logical(code, 8), lax.bitwise_and(code, 255)

    def make(batch, u):
        target, source = pair(batch, u)
        square = jnp.dot(source_ref[source], target_ref[base + target], preferred_element_type=f32)
        held[u] = lax.rsqrt(square).astype(bf16)

    def use(batch, u):
        target, source = pair(batch, u)
        charges = jnp.concatenate([mine_ref[:, cluster(source)], other_ref[:, cluster(source)]], axis=0)
        return target, jnp.dot(charges, held[u], preferred_element_type=f32)

    def body(batch, carry):
        values = []
        for u in range(BATCH):
            values.append(use(batch, u))
            make(batch + 1, u)
        for target, value in values:
            total[target] += value
        return carry

    for u in range(BATCH):
        make(0, u)
    lax.fori_loop(0, batches - 1, body, 0)
    final = jnp.maximum(batches - 1, 0)
    values = [use(final, u) for u in range(BATCH)]
    for target, value in values:
        total[target] += value
    for i in range(targets):
        out_ref[:, i * LEAF : (i + 1) * LEAF] = total[i].astype(out_ref.dtype)


def near_sum(base, targets, pairs, target_rows, source_rows, mine, other, dtype):
    columns = 2 * mine.shape[0]
    return pl.pallas_call(
        functools.partial(near_kernel, base),
        out_shape=jax.ShapeDtypeStruct((columns, targets * LEAF), dtype),
        in_specs=[SMEM] + [VMEM] * 4,
        out_specs=VMEM,
        scratch_shapes=[
            pltpu.VMEM((targets + 1, columns, LEAF), f32),
            pltpu.VMEM((BATCH, LEAF, LEAF), bf16),
        ],
        compiler_params=PARAMS,
        cost_estimate=cost(2.5),
    )(pairs, target_rows, source_rows, mine, other)


def far_sum(out_ref, basis_ref, target, at, coefficient):
    out_ref[:, target * LEAF : (target + 1) * LEAF] = lax.dot_general(
        coefficient.astype(bf16),
        basis_ref[:, cluster(at)],
        (((0,), (0,)), ((), ())),
        preferred_element_type=f32,
    )


def far_kernel(seg_size, far_ref, couplings_ref, basis_ref, part, out_ref, skel):
    leaf = lax.axis_index("leaf") * couplings_ref.shape[0]
    clusters, far_count, rank, _ = couplings_ref.shape
    columns = out_ref.shape[0]
    pack = LEAF // columns

    def unpack(group, carry):
        block = part[pl.ds(pl.multiple_of(group * rank, rank), rank), :]
        for i in range(pack):
            skel[group * pack + i] = block[:, i * columns : (i + 1) * columns]
        return carry

    lax.fori_loop(0, part.shape[0] // rank, unpack, 0)
    for target in range(clusters):
        coefficient = jnp.zeros((rank, columns), f32)
        step = 256 // rank
        for at in range(0, far_count, step):
            left = jnp.concatenate([couplings_ref[target, at + i] for i in range(step)], axis=1)
            rows = [skel[far_ref[target, at + i]] for i in range(step)]
            coefficient = coefficient + jnp.dot(
                left, jnp.concatenate(rows, axis=0), preferred_element_type=f32
            )
        far_sum(out_ref, basis_ref, target, leaf + target, coefficient)


def far_kernel_wide(seg_size, far_ref, couplings_hbm, basis_ref, *refs):
    parts, (out_ref, skel, couplings_ref, sems) = refs[:-4], refs[-4:]
    clusters, far_count, rank, _ = couplings_ref.shape
    columns = out_ref.shape[0]
    pack = LEAF // columns
    leaf = lax.axis_index("leaf") * clusters
    copies = [
        pltpu.make_async_copy(couplings_hbm.at[t], couplings_ref.at[t], sems.at[t]) for t in range(clusters)
    ]
    for copy in copies:
        copy.start()
    lane_block = lax.broadcasted_iota(jnp.int32, (rank, LEAF), 1) // columns
    for order, part in enumerate(parts):
        def unpack(group, carry, order=order, part=part):
            block = part[pl.ds(pl.multiple_of(group * rank, rank), rank), :].astype(f32)
            turned = [block] + [pltpu.roll(block, k * columns, 1) for k in range(1, pack)]
            for i in range(pack):
                for j in range(pack):
                    value = jnp.where(lane_block == j, turned[(j - i) % pack], 0.0)
                    skel[j, order * seg_size + group * pack + i] = value.astype(bf16)
            return carry
        lax.fori_loop(0, seg_size // pack, unpack, 0, unroll=2)

    for target in range(clusters):
        copies[target].wait()
        wide = jnp.zeros((rank, LEAF), f32)
        for at in range(0, far_count, pack):
            right = skel[0, far_ref[target, at]]
            for i in range(1, pack):
                right = right + skel[i, far_ref[target, at + i]]
            left = couplings_ref[target, at : at + pack].reshape(pack * rank, rank)
            product = jnp.dot(left, right, preferred_element_type=f32)
            chosen = product[:rank]
            for i in range(1, pack):
                chosen = jnp.where(lane_block == i, product[i * rank : (i + 1) * rank], chosen)
            wide = wide + chosen
        turn = columns
        while turn < LEAF:
            wide = wide + pltpu.roll(wide, turn, 1)
            turn *= 2
        far_sum(out_ref, basis_ref, target, leaf + target, wide[:, :columns])


def on_device(points, charges, basis, couplings, near_src, far_src):
    blk_count = lax.axis_size("blk")
    mine = charges.T
    columns, seg_rows = mine.shape
    seg_size = seg_rows // LEAF
    rank = basis.shape[0]
    own_clusters, near_count = near_src.shape
    targets = own_clusters // 2
    cluster_total = seg_size * blk_count
    pack = LEAF // columns
    skel_rows = seg_size // pack * rank
    other = shifted(mine, "rhs", 1)

    own_list, prev_load, next_load = pl.pallas_call(
        functools.partial(list_kernel, seg_size),
        out_shape=[jax.ShapeDtypeStruct((8, LEAF), jnp.int32)]
        + [jax.ShapeDtypeStruct((skel_rows + 16, LEAF), bf16)] * 2,
        in_specs=[ANY] * 3,
        out_specs=[SMEM, VMEM, VMEM],
        scratch_shapes=[
            pltpu.SMEM(near_src.shape, jnp.int32),
            pltpu.VMEM(basis.shape, bf16),
            pltpu.VMEM(mine.shape, bf16),
            pltpu.SemaphoreType.DMA((3,)),
        ],
        compiler_params=PARAMS,
        cost_estimate=cost(3.0),
    )(near_src, basis, mine)

    after_load = shifted(prev_load, "blk", -1)
    before_load = shifted(next_load, "blk", 1)

    def list_of(load):
        entries = load[skel_rows:].astype(jnp.int32)
        return entries[:8] + 256 * entries[8:]

    target_rows, source_rows = pl.pallas_call(
        functools.partial(feature_kernel, seg_size, targets, own_clusters),
        out_shape=[
            jax.ShapeDtypeStruct((3 * targets + 1, DEPTH, LEAF), bf16),
            jax.ShapeDtypeStruct((seg_size, LEAF, DEPTH), bf16),
        ],
        in_specs=[VMEM],
        out_specs=[VMEM, VMEM],
        compiler_params=PARAMS,
        cost_estimate=cost(0.7),
    )(points)
    args = (target_rows, source_rows, mine, other)
    own_near = near_sum(targets, targets, own_list, *args, f32)
    to_before = near_sum(0, targets, list_of(before_load), *args, bf16)
    from_after = shifted(to_before, "blk", -1)
    to_after = near_sum(2 * targets, targets, list_of(after_load), *args, bf16)
    from_before = shifted(to_after, "blk", 1)

    blk = lax.axis_index("blk")
    first = blk * seg_size + lax.axis_index("leaf") * own_clusters
    entries = lax.dynamic_slice_in_dim(far_src, first, own_clusters, 0)
    far_shape = jax.ShapeDtypeStruct((columns, own_clusters * LEAF), f32)
    if blk_count == 4 and cluster_total <= 256:
        middle_load = shifted(prev_load, "blk", 2)
        entries = lax.rem(entries + (blk_count - blk) * seg_size, cluster_total)
        far = pl.pallas_call(
            functools.partial(far_kernel_wide, seg_size),
            out_shape=far_shape,
            in_specs=[SMEM, ANY] + [VMEM] * 5,
            out_specs=VMEM,
            scratch_shapes=[
                pltpu.VMEM((pack, cluster_total, rank, LEAF), bf16),
                pltpu.VMEM(couplings.shape, bf16),
                pltpu.SemaphoreType.DMA((own_clusters,)),
            ],
            compiler_params=PARAMS,
            cost_estimate=cost(3.0),
        )(entries, couplings, basis, prev_load, after_load, middle_load, before_load)
    else:
        far = pl.pallas_call(
            functools.partial(far_kernel, seg_size),
            out_shape=far_shape,
            in_specs=[SMEM] + [VMEM] * 3,
            out_specs=VMEM,
            scratch_shapes=[pltpu.VMEM((cluster_total, rank, columns), bf16)],
            compiler_params=PARAMS,
        )(entries, couplings, basis, lax.all_gather(prev_load[:skel_rows], "blk", axis=0, tiled=True))

    near = own_near + from_before.astype(f32) + from_after.astype(f32)
    keep = near[:columns]
    got = shifted(near[columns:], "rhs", 1)
    even = lax.axis_index("rhs") == 0
    whole = jnp.concatenate([jnp.where(even, keep, got), jnp.where(even, got, keep)], axis=1)
    return (whole + far).astype(bf16).T


def solution(mesh):
    in_specs = (
        P(None, "groups"),
        P(("groups", "blk"), "rhs"),
        P(None, ("groups", "blk")),
        P(("groups", "blk", "leaf"), None, None, None),
        P(("groups", "blk", "leaf"), None),
        P("groups", None),
    )
    out_specs = P(("groups", "blk", "leaf"), "rhs")
    return jax.shard_map(
        on_device, mesh=mesh, in_specs=in_specs, out_specs=out_specs, check_vma=False
    )
```

```python
import functools

import jax
import jax.numpy as jnp
from jax import lax
from jax.experimental import pallas as pl
from jax.experimental.pallas import tpu as pltpu
from jax.sharding import PartitionSpec as P

LEAF = 128
BATCH = 12
DEPTH = 48

kernel_scale = 0.0625 / (4.0 * 3.141592653589793)
soften = 0.001
inverse_sq = 1.0 / (kernel_scale * kernel_scale)

bf16 = jnp.bfloat16
f32 = jnp.float32
VMEM = pl.BlockSpec(memory_space=pltpu.VMEM)
HBM = pl.BlockSpec(memory_space=pltpu.HBM)
SMEM = pl.BlockSpec(memory_space=pltpu.SMEM)
PARAMS = pltpu.CompilerParams(vmem_limit_bytes=48 * 2**20)


def cost(microseconds):
    return pl.CostEstimate(flops=int(microseconds * 1e9), bytes_accessed=0, transcendentals=0)


def shifted(block, axis, shift):
    count = lax.axis_size(axis)
    return lax.ppermute(block, axis, [(i, (i + shift) % count) for i in range(count)])


def cluster(index):
    return pl.ds(pl.multiple_of(index * LEAF, LEAF), LEAF)


def list_kernel(seg_size, near_hbm, basis_hbm, charges_hbm, own_ref, prev_ref, next_ref, near_ref, basis_ref, charges_ref, sems):
    copies = [
        pltpu.make_async_copy(near_hbm, near_ref, sems.at[0]),
        pltpu.make_async_copy(basis_hbm, basis_ref, sems.at[1]),
        pltpu.make_async_copy(charges_hbm, charges_ref, sems.at[2]),
    ]
    for copy in copies:
        copy.start()
    targets = near_ref.shape[0] // 2
    near_count = near_ref.shape[1]
    blk_count = lax.axis_size("blk")
    blk = lax.axis_index("blk")
    before = lax.rem(blk + blk_count - 1, blk_count)
    half = lax.axis_index("rhs")
    columns = charges_ref.shape[0]
    rank = basis_ref.shape[0]
    pack = LEAF // columns
    rows_end = seg_size // pack * rank

    def iota(shape, dim):
        return lax.broadcasted_iota(jnp.int32, shape, dim)

    def ones(condition):
        return jnp.where(condition, 1.0, 0.0).astype(bf16)

    lane = iota((targets, LEAF), 1)
    earlier = ones(iota((LEAF, LEAF), 0) < iota((LEAF, LEAF), 1))
    above = ones(iota((targets, targets), 1) < iota((targets, targets), 0))
    row = iota((8, LEAF), 0)
    lower = iota((LEAF, LEAF), 0)
    copies[0].wait()
    sources = jnp.where(half == 0, near_ref[:targets, :], near_ref[targets:, :])
    sources = jnp.concatenate(
        [sources, jnp.full((targets, LEAF - near_count), -1, jnp.int32)], axis=1
    )
    segment = jnp.zeros((targets, LEAF), jnp.int32)
    if seg_size & (seg_size - 1) == 0:
        segment = lax.shift_right_arithmetic(sources, seg_size.bit_length() - 1)
    else:
        segment = lax.div(sources, seg_size)
    local = (sources - segment * seg_size).astype(f32)
    is_own = segment == blk
    is_prev = jnp.logical_and(segment == before, jnp.logical_not(is_own))
    is_next = jnp.logical_and(lane < near_count, jnp.logical_not(jnp.logical_or(is_own, is_prev)))
    masks = (is_own, is_prev, is_next)
    place = jnp.zeros((targets, LEAF), f32)
    totals = []
    for mask in masks:
        within = jnp.dot(ones(mask), earlier, preferred_element_type=f32)
        count = jnp.broadcast_to(within[:, LEAF - 1 :], (targets, LEAF))
        start = jnp.dot(above, count.astype(bf16), preferred_element_type=f32)
        place = jnp.where(mask, start + within, place)
        totals.append(start[targets - 1 :, :] + count[targets - 1 :, :])
    place = place.astype(jnp.int32)
    left, right = [], []
    for target in range(targets):
        at = place[target : target + 1, :]
        here = lax.shift_right_logical(at, 7) == row
        rows = []
        for mask in masks:
            chosen = jnp.logical_and(here, jnp.where(mask[target : target + 1, :], 1, 0) == 1)
            rows.append(jnp.where(chosen, local[target : target + 1, :], 0.0))
            rows.append(jnp.where(chosen, float(target), 0.0))
        left.append(jnp.concatenate(rows, axis=0).astype(bf16))
        right.append(ones(lax.bitwise_and(at, LEAF - 1) == lower))
    lists = lax.dot_general(
        jnp.concatenate(left, axis=1),
        jnp.concatenate(right, axis=1),
        (((1,), (1,)), ((), ())),
        preferred_element_type=f32,
    )
    last = row * LEAF + iota((8, LEAF), 1) == 8 * LEAF - 1
    finished = []
    for i, total in enumerate(totals):
        high = jnp.floor(total * (1.0 / 256.0))
        finished.append(jnp.where(last, total - 256.0 * high, lists[16 * i : 16 * i + 8]))
        finished.append(jnp.where(last, high, lists[16 * i + 8 : 16 * i + 16]))
    own_ref[...] = finished[0].astype(jnp.int32) + 256 * finished[1].astype(jnp.int32)
    prev_ref[rows_end : rows_end + 16, :] = jnp.concatenate(finished[2:4], axis=0).astype(bf16)
    next_ref[rows_end : rows_end + 16, :] = jnp.concatenate(finished[4:6], axis=0).astype(bf16)

    copies[1].wait()
    copies[2].wait()
    blocks = []
    for group in range(seg_size // pack):
        rows = []
        for i in range(pack):
            at = (group * pack + i) * LEAF
            parts = [jnp.zeros((columns, LEAF), bf16)] * pack
            parts[i] = charges_ref[:, at : at + LEAF]
            rows.append(jnp.concatenate(parts, axis=1))
        at = group * pack * LEAF
        blocks.append(
            lax.dot_general(
                basis_ref[:, at : at + pack * LEAF],
                jnp.concatenate(rows, axis=0),
                (((1,), (1,)), ((), ())),
                preferred_element_type=f32,
            )
        )
    for group, block in enumerate(blocks):
        prev_ref[group * rank : (group + 1) * rank, :] = block.astype(bf16)
        next_ref[group * rank : (group + 1) * rank, :] = block.astype(bf16)


def split(value):
    high = value.astype(bf16).astype(f32)
    rest = value - high
    middle = rest.astype(bf16).astype(f32)
    return high, middle, rest - middle


def coords_of(points_ref, at):
    block = points_ref[:, cluster(at)]
    zero, one, two = block[0:1, :], block[1:2, :], block[2:3, :]
    return zero, one, two, zero * zero + one * one + two * two


def rows_of(values):
    row = lax.broadcasted_iota(jnp.int32, (8, LEAF), 0)
    out = jnp.zeros((8, LEAF), f32)
    for i, value in enumerate(values):
        out = jnp.where(row == i, value, out)
    return out


def target_features(points_ref, at):
    zero, one, two, norm = coords_of(points_ref, at)
    slope = -2.0 * inverse_sq
    rows = rows_of((zero * slope, one * slope, two * slope, (norm + soften) * inverse_sq, 1.0))
    high, middle, low = split(rows)
    return jnp.concatenate([high, high, middle, middle, high, low], axis=0).astype(bf16)


def source_features(points_ref, at):
    zero, one, two, norm = coords_of(points_ref, at)
    rows = rows_of((zero, one, two, 1.0, norm * inverse_sq))
    high, middle, low = split(rows)
    stacked = jnp.concatenate([high, middle, high, middle, low, high], axis=0)
    return jnp.transpose(stacked).astype(bf16)


def feature_kernel(seg_size, targets, leaf_clusters, points_ref, target_ref, source_ref):
    blk_count = lax.axis_size("blk")
    blk = lax.axis_index("blk")
    first = lax.axis_index("leaf") * leaf_clusters + lax.axis_index("rhs") * targets
    for which in range(3):
        segment = lax.rem(blk + which + blk_count - 1, blk_count)
        for i in range(targets):
            target_ref[which * targets + i] = target_features(
                points_ref, segment * seg_size + first + i
            )
    target_ref[3 * targets] = jnp.zeros((DEPTH, LEAF), bf16)

    def some_sources(step, carry):
        for u in range(8):
            at = step * 8 + u
            source_ref[at] = source_features(points_ref, blk * seg_size + at)
        return carry

    lax.fori_loop(0, seg_size // 8, some_sources, 0)


def near_kernel(bases, targets, *refs):
    count = len(bases)
    lists = refs[:count]
    target_ref, source_ref, mine_ref, other_ref = refs[count : count + 4]
    outs = refs[count + 4 : 2 * count + 4]
    total, even, odd = refs[2 * count + 4 :]
    lengths = [ref[7, LEAF - 1] for ref in lists]
    length = sum(lengths)
    batches = lax.div(length + (BATCH - 1), BATCH)
    total[...] = jnp.zeros_like(total)

    def pair(batch, u):
        at = batch * BATCH + u
        code = jnp.int32(3 * targets * 256)
        for i in reversed(range(count)):
            start = sum(lengths[:i])
            place = jnp.maximum(at - start, 0)
            entry = lists[i][lax.shift_right_logical(place, 7), lax.bitwise_and(place, 127)]
            code = jnp.where(at < start + lengths[i], entry + bases[i] * 256, code)
        return lax.shift_right_logical(code, 8), lax.bitwise_and(code, 255)

    def make(batch, slot):
        for u in range(BATCH):
            target, source = pair(batch, u)
            square = jnp.dot(source_ref[source], target_ref[target], preferred_element_type=f32)
            slot[u] = lax.rsqrt(square).astype(bf16)

    def use(batch, slot):
        sums = []
        for u in range(BATCH):
            target, source = pair(batch, u)
            charges = jnp.concatenate([mine_ref[:, cluster(source)], other_ref[:, cluster(source)]], axis=0)
            sums.append((target, jnp.dot(charges, slot[u], preferred_element_type=f32)))
        for target, value in sums:
            total[target] += value

    make(0, even)

    def body(step, carry):
        make(2 * step + 1, odd)
        use(2 * step, even)
        make(2 * step + 2, even)
        use(2 * step + 1, odd)
        return carry

    lax.fori_loop(0, lax.div(batches + 1, 2), body, 0)
    for base, out in zip(bases, outs):
        for i in range(targets):
            out[:, i * LEAF : (i + 1) * LEAF] = total[base + i].astype(out.dtype)


def near_sums(bases, targets, lists, target_rows, source_rows, mine, other, dtype, microseconds):
    columns = 2 * mine.shape[0]
    return pl.pallas_call(
        functools.partial(near_kernel, bases, targets),
        out_shape=[jax.ShapeDtypeStruct((columns, targets * LEAF), dtype)] * len(bases),
        in_specs=[SMEM] * len(bases) + [VMEM] * 4,
        out_specs=[VMEM] * len(bases),
        scratch_shapes=[
            pltpu.VMEM((3 * targets + 1, columns, LEAF), f32),
            pltpu.VMEM((BATCH, LEAF, LEAF), bf16),
            pltpu.VMEM((BATCH, LEAF, LEAF), bf16),
        ],
        compiler_params=PARAMS,
        cost_estimate=cost(microseconds),
    )(*lists, target_rows, source_rows, mine, other)


def far_sum(out_ref, basis_ref, target, at, coefficient):
    out_ref[:, target * LEAF : (target + 1) * LEAF] = lax.dot_general(
        coefficient.astype(bf16),
        basis_ref[:, cluster(at)],
        (((0,), (0,)), ((), ())),
        preferred_element_type=f32,
    )


def far_kernel(seg_size, far_ref, couplings_ref, basis_ref, part, out_ref, skel):
    leaf = lax.axis_index("leaf") * couplings_ref.shape[0]
    clusters, far_count, rank, _ = couplings_ref.shape
    columns = out_ref.shape[0]
    pack = LEAF // columns

    def unpack(group, carry):
        block = part[pl.ds(pl.multiple_of(group * rank, rank), rank), :]
        for i in range(pack):
            skel[group * pack + i] = block[:, i * columns : (i + 1) * columns]
        return carry

    lax.fori_loop(0, part.shape[0] // rank, unpack, 0)
    for target in range(clusters):
        coefficient = jnp.zeros((rank, columns), f32)
        step = 256 // rank
        for at in range(0, far_count, step):
            left = jnp.concatenate([couplings_ref[target, at + i] for i in range(step)], axis=1)
            rows = [skel[far_ref[target, at + i]] for i in range(step)]
            coefficient = coefficient + jnp.dot(
                left, jnp.concatenate(rows, axis=0), preferred_element_type=f32
            )
        far_sum(out_ref, basis_ref, target, leaf + target, coefficient)


def far_kernel_phased(seg_size, far_ref, couplings_ref, basis_ref, *refs):
    parts, (out_ref, skel, side, held) = refs[:-4], refs[-4:]
    clusters, far_count, rank, _ = couplings_ref.shape
    columns = out_ref.shape[0]
    pack = LEAF // columns
    leaf = lax.axis_index("leaf") * clusters
    for target in range(clusters):
        for at in range(0, far_count, pack):
            side[target, :, at * rank : (at + pack) * rank] = jnp.concatenate(
                [couplings_ref[target, at + i] for i in range(pack)], axis=1
            )
    for order, part in enumerate(parts):
        for group in range(seg_size // pack):
            block = part[group * rank : (group + 1) * rank, :]
            for i in range(pack):
                skel[order * seg_size + group * pack + i] = block[:, i * columns : (i + 1) * columns]
    step = 256 // rank
    for target in range(clusters):
        coefficient = jnp.zeros((rank, columns), f32)
        for at in range(0, far_count, step):
            rows = [skel[far_ref[target, at + i]] for i in range(step)]
            coefficient = coefficient + jnp.dot(
                side[target, :, at * rank : (at + step) * rank],
                jnp.concatenate(rows, axis=0),
                preferred_element_type=f32,
            )
        held[target] = coefficient.astype(bf16)
    for target in range(clusters):
        far_sum(out_ref, basis_ref, target, leaf + target, held[target])


def on_device(points, charges, basis, couplings, near_src, far_src):
    blk_count = lax.axis_size("blk")
    mine = charges.T
    columns, seg_rows = mine.shape
    seg_size = seg_rows // LEAF
    rank = basis.shape[0]
    own_clusters, near_count = near_src.shape
    targets = own_clusters // 2
    cluster_total = seg_size * blk_count
    pack = LEAF // columns
    skel_rows = seg_size // pack * rank
    other = shifted(mine, "rhs", 1)

    own_list, prev_load, next_load = pl.pallas_call(
        functools.partial(list_kernel, seg_size),
        out_shape=[jax.ShapeDtypeStruct((8, LEAF), jnp.int32)]
        + [jax.ShapeDtypeStruct((skel_rows + 16, LEAF), bf16)] * 2,
        in_specs=[HBM] * 3,
        out_specs=[VMEM] * 3,
        scratch_shapes=[
            pltpu.VMEM(near_src.shape, jnp.int32),
            pltpu.VMEM(basis.shape, bf16),
            pltpu.VMEM(mine.shape, bf16),
            pltpu.SemaphoreType.DMA((3,)),
        ],
        compiler_params=pltpu.CompilerParams(vmem_limit_bytes=63 * 2**20),
        cost_estimate=cost(3.0),
    )(near_src, basis, mine)

    after_load = shifted(prev_load, "blk", -1)
    before_load = shifted(next_load, "blk", 1)

    def list_of(load):
        entries = load[skel_rows:].astype(jnp.int32)
        return entries[:8] + 256 * entries[8:]

    target_rows, source_rows = pl.pallas_call(
        functools.partial(feature_kernel, seg_size, targets, own_clusters),
        out_shape=[
            jax.ShapeDtypeStruct((3 * targets + 1, DEPTH, LEAF), bf16),
            jax.ShapeDtypeStruct((seg_size, LEAF, DEPTH), bf16),
        ],
        in_specs=[VMEM],
        out_specs=[VMEM, VMEM],
        compiler_params=PARAMS,
        cost_estimate=cost(0.7),
    )(points)
    args = (target_rows, source_rows, mine, other)
    (own_near,) = near_sums((targets,), targets, (own_list,), *args, f32, 2.6)
    own_near, before_load, after_load = lax.optimization_barrier((own_near, before_load, after_load))
    lists = (list_of(before_load), list_of(after_load))
    to_before, to_after = near_sums((0, 2 * targets), targets, lists, *args, bf16, 4.0)
    from_after = shifted(to_before, "blk", -1)
    from_before = shifted(to_after, "blk", 1)

    blk = lax.axis_index("blk")
    first = blk * seg_size + lax.axis_index("leaf") * own_clusters
    entries = lax.dynamic_slice_in_dim(far_src, first, own_clusters, 0)
    far_shape = jax.ShapeDtypeStruct((columns, own_clusters * LEAF), f32)
    if blk_count == 4 and cluster_total <= 256:
        middle_load = shifted(prev_load, "blk", 2)
        entries = lax.rem(entries + (blk_count - blk) * seg_size, cluster_total)
        far = pl.pallas_call(
            functools.partial(far_kernel_phased, seg_size),
            out_shape=far_shape,
            in_specs=[SMEM] + [VMEM] * 6,
            out_specs=VMEM,
            scratch_shapes=[
                pltpu.VMEM((cluster_total, rank, columns), bf16),
                pltpu.VMEM((own_clusters, rank, far_src.shape[1] * rank), bf16),
                pltpu.VMEM((own_clusters, rank, columns), bf16),
            ],
            compiler_params=PARAMS,
            cost_estimate=cost(3.0),
        )(entries, couplings, basis, prev_load, after_load, middle_load, before_load)
    else:
        far = pl.pallas_call(
            functools.partial(far_kernel, seg_size),
            out_shape=far_shape,
            in_specs=[SMEM] + [VMEM] * 3,
            out_specs=VMEM,
            scratch_shapes=[pltpu.VMEM((cluster_total, rank, columns), bf16)],
            compiler_params=PARAMS,
        )(entries, couplings, basis, lax.all_gather(prev_load[:skel_rows], "blk", axis=0, tiled=True))

    far, from_before, from_after = lax.optimization_barrier((far, from_before, from_after))
    near = own_near + from_before.astype(f32) + from_after.astype(f32)
    keep = near[:columns]
    got = shifted(near[columns:], "rhs", 1)
    even = lax.axis_index("rhs") == 0
    whole = jnp.concatenate([jnp.where(even, keep, got), jnp.where(even, got, keep)], axis=1)
    return (whole + far).astype(bf16).T


def solution(mesh):
    in_specs = (
        P(None, "groups"),
        P(("groups", "blk"), "rhs"),
        P(None, ("groups", "blk")),
        P(("groups", "blk", "leaf"), None, None, None),
        P(("groups", "blk", "leaf"), None),
        P("groups", None),
    )
    out_specs = P(("groups", "blk", "leaf"), "rhs")
    return jax.shard_map(
        on_device, mesh=mesh, in_specs=in_specs, out_specs=out_specs, check_vma=False
    )
```

```python
import functools

import jax
import jax.numpy as jnp
from jax import lax
from jax.experimental import pallas as pl
from jax.experimental.pallas import tpu as pltpu
from jax.sharding import PartitionSpec as P

LEAF = 128
BATCH = 12
DEPTH = 48

kernel_scale = 0.0625 / (4.0 * 3.141592653589793)
soften = 0.001
inverse_sq = 1.0 / (kernel_scale * kernel_scale)

bf16 = jnp.bfloat16
f32 = jnp.float32
VMEM = pl.BlockSpec(memory_space=pltpu.VMEM)
HBM = pl.BlockSpec(memory_space=pltpu.HBM)
SMEM = pl.BlockSpec(memory_space=pltpu.SMEM)
PARAMS = pltpu.CompilerParams(vmem_limit_bytes=48 * 2**20)


def cost(microseconds):
    return pl.CostEstimate(flops=int(microseconds * 1e9), bytes_accessed=0, transcendentals=0)


def shifted(block, axis, shift):
    count = lax.axis_size(axis)
    return lax.ppermute(block, axis, [(i, (i + shift) % count) for i in range(count)])


def cluster(index):
    return pl.ds(pl.multiple_of(index * LEAF, LEAF), LEAF)


def list_kernel(seg_size, near_hbm, basis_hbm, charges_hbm, own_ref, prev_ref, next_ref, near_ref, basis_ref, charges_ref, sems):
    copies = [
        pltpu.make_async_copy(near_hbm, near_ref, sems.at[0]),
        pltpu.make_async_copy(basis_hbm, basis_ref, sems.at[1]),
        pltpu.make_async_copy(charges_hbm, charges_ref, sems.at[2]),
    ]
    for copy in copies:
        copy.start()
    targets = near_ref.shape[0] // 2
    near_count = near_ref.shape[1]
    blk_count = lax.axis_size("blk")
    blk = lax.axis_index("blk")
    before = lax.rem(blk + blk_count - 1, blk_count)
    half = lax.axis_index("rhs")
    columns = charges_ref.shape[0]
    rank = basis_ref.shape[0]
    pack = LEAF // columns
    rows_end = seg_size // pack * rank

    def iota(shape, dim):
        return lax.broadcasted_iota(jnp.int32, shape, dim)

    def ones(condition):
        return jnp.where(condition, 1.0, 0.0).astype(bf16)

    lane = iota((targets, LEAF), 1)
    earlier = ones(iota((LEAF, LEAF), 0) < iota((LEAF, LEAF), 1))
    above = ones(iota((targets, targets), 1) < iota((targets, targets), 0))
    row = iota((8, LEAF), 0)
    lower = iota((LEAF, LEAF), 0)
    copies[0].wait()
    sources = jnp.where(half == 0, near_ref[:targets, :], near_ref[targets:, :])
    sources = jnp.concatenate(
        [sources, jnp.full((targets, LEAF - near_count), -1, jnp.int32)], axis=1
    )
    segment = jnp.zeros((targets, LEAF), jnp.int32)
    if seg_size & (seg_size - 1) == 0:
        segment = lax.shift_right_arithmetic(sources, seg_size.bit_length() - 1)
    else:
        segment = lax.div(sources, seg_size)
    local = (sources - segment * seg_size).astype(f32)
    is_own = segment == blk
    is_prev = jnp.logical_and(segment == before, jnp.logical_not(is_own))
    is_next = jnp.logical_and(lane < near_count, jnp.logical_not(jnp.logical_or(is_own, is_prev)))
    masks = (is_own, is_prev, is_next)
    place = jnp.zeros((targets, LEAF), f32)
    totals = []
    for mask in masks:
        within = jnp.dot(ones(mask), earlier, preferred_element_type=f32)
        count = jnp.broadcast_to(within[:, LEAF - 1 :], (targets, LEAF))
        start = jnp.dot(above, count.astype(bf16), preferred_element_type=f32)
        place = jnp.where(mask, start + within, place)
        totals.append(start[targets - 1 :, :] + count[targets - 1 :, :])
    place = place.astype(jnp.int32)
    left, right = [], []
    for target in range(targets):
        at = place[target : target + 1, :]
        here = lax.shift_right_logical(at, 7) == row
        rows = []
        for mask in masks:
            chosen = jnp.logical_and(here, jnp.where(mask[target : target + 1, :], 1, 0) == 1)
            rows.append(jnp.where(chosen, local[target : target + 1, :], 0.0))
            rows.append(jnp.where(chosen, float(target), 0.0))
        left.append(jnp.concatenate(rows, axis=0).astype(bf16))
        right.append(ones(lax.bitwise_and(at, LEAF - 1) == lower))
    lists = lax.dot_general(
        jnp.concatenate(left, axis=1),
        jnp.concatenate(right, axis=1),
        (((1,), (1,)), ((), ())),
        preferred_element_type=f32,
    )
    last = row * LEAF + iota((8, LEAF), 1) == 8 * LEAF - 1
    finished = []
    for i, total in enumerate(totals):
        high = jnp.floor(total * (1.0 / 256.0))
        finished.append(jnp.where(last, total - 256.0 * high, lists[16 * i : 16 * i + 8]))
        finished.append(jnp.where(last, high, lists[16 * i + 8 : 16 * i + 16]))
    own_ref[...] = finished[0].astype(jnp.int32) + 256 * finished[1].astype(jnp.int32)
    prev_ref[rows_end : rows_end + 16, :] = jnp.concatenate(finished[2:4], axis=0).astype(bf16)
    next_ref[rows_end : rows_end + 16, :] = jnp.concatenate(finished[4:6], axis=0).astype(bf16)

    copies[1].wait()
    copies[2].wait()
    blocks = []
    for group in range(seg_size // pack):
        rows = []
        for i in range(pack):
            at = (group * pack + i) * LEAF
            parts = [jnp.zeros((columns, LEAF), bf16)] * pack
            parts[i] = charges_ref[:, at : at + LEAF]
            rows.append(jnp.concatenate(parts, axis=1))
        at = group * pack * LEAF
        blocks.append(
            lax.dot_general(
                basis_ref[:, at : at + pack * LEAF],
                jnp.concatenate(rows, axis=0),
                (((1,), (1,)), ((), ())),
                preferred_element_type=f32,
            )
        )
    for group, block in enumerate(blocks):
        prev_ref[group * rank : (group + 1) * rank, :] = block.astype(bf16)
        next_ref[group * rank : (group + 1) * rank, :] = block.astype(bf16)


def split(value):
    high = value.astype(bf16).astype(f32)
    rest = value - high
    middle = rest.astype(bf16).astype(f32)
    return high, middle, rest - middle


def coords_of(points_ref, at):
    block = points_ref[:, cluster(at)]
    zero, one, two = block[0:1, :], block[1:2, :], block[2:3, :]
    return zero, one, two, zero * zero + one * one + two * two


def rows_of(values):
    row = lax.broadcasted_iota(jnp.int32, (8, LEAF), 0)
    out = jnp.zeros((8, LEAF), f32)
    for i, value in enumerate(values):
        out = jnp.where(row == i, value, out)
    return out


def target_features(points_ref, at):
    zero, one, two, norm = coords_of(points_ref, at)
    slope = -2.0 * inverse_sq
    rows = rows_of((zero * slope, one * slope, two * slope, (norm + soften) * inverse_sq, 1.0))
    high, middle, low = split(rows)
    return jnp.concatenate([high, high, middle, middle, high, low], axis=0).astype(bf16)


def source_features(points_ref, at):
    zero, one, two, norm = coords_of(points_ref, at)
    rows = rows_of((zero, one, two, 1.0, norm * inverse_sq))
    high, middle, low = split(rows)
    stacked = jnp.concatenate([high, middle, high, middle, low, high], axis=0)
    return jnp.transpose(stacked).astype(bf16)


def feature_kernel(seg_size, targets, leaf_clusters, points_ref, target_ref, source_ref):
    blk_count = lax.axis_size("blk")
    blk = lax.axis_index("blk")
    first = lax.axis_index("leaf") * leaf_clusters + lax.axis_index("rhs") * targets
    for which in range(3):
        segment = lax.rem(blk + which + blk_count - 1, blk_count)
        for i in range(targets):
            target_ref[which * targets + i] = target_features(
                points_ref, segment * seg_size + first + i
            )
    target_ref[3 * targets] = jnp.zeros((DEPTH, LEAF), bf16)

    def some_sources(step, carry):
        for u in range(8):
            at = step * 8 + u
            source_ref[at] = source_features(points_ref, blk * seg_size + at)
        return carry

    lax.fori_loop(0, seg_size // 8, some_sources, 0)


def near_kernel(bases, targets, *refs):
    count = len(bases)
    lists = refs[:count]
    target_ref, source_ref, mine_ref, other_ref = refs[count : count + 4]
    outs = refs[count + 4 : 2 * count + 4]
    total, even, odd = refs[2 * count + 4 :]
    lengths = [ref[7, LEAF - 1] for ref in lists]
    length = sum(lengths)
    batches = lax.div(length + (BATCH - 1), BATCH)
    total[...] = jnp.zeros_like(total)

    def pair(batch, u):
        at = batch * BATCH + u
        code = jnp.int32(3 * targets * 256)
        for i in reversed(range(count)):
            start = sum(lengths[:i])
            place = jnp.maximum(at - start, 0)
            entry = lists[i][lax.shift_right_logical(place, 7), lax.bitwise_and(place, 127)]
            code = jnp.where(at < start + lengths[i], entry + bases[i] * 256, code)
        return lax.shift_right_logical(code, 8), lax.bitwise_and(code, 255)

    def make(batch, slot):
        for u in range(BATCH):
            target, source = pair(batch, u)
            square = jnp.dot(source_ref[source], target_ref[target], preferred_element_type=f32)
            slot[u] = lax.rsqrt(square).astype(bf16)

    def use(batch, slot):
        sums = []
        for u in range(BATCH):
            target, source = pair(batch, u)
            charges = jnp.concatenate([mine_ref[:, cluster(source)], other_ref[:, cluster(source)]], axis=0)
            sums.append((target, jnp.dot(charges, slot[u], preferred_element_type=f32)))
        for target, value in sums:
            total[target] += value

    make(0, even)

    def body(step, carry):
        make(2 * step + 1, odd)
        use(2 * step, even)
        make(2 * step + 2, even)
        use(2 * step + 1, odd)
        return carry

    lax.fori_loop(0, lax.div(batches, 2), body, 0)

    @pl.when(lax.rem(batches, 2) == 1)
    def _():
        use(batches - 1, even)

    for base, out in zip(bases, outs):
        for i in range(targets):
            out[:, i * LEAF : (i + 1) * LEAF] = total[base + i].astype(out.dtype)


def near_sums(bases, targets, lists, target_rows, source_rows, mine, other, dtype, microseconds):
    columns = 2 * mine.shape[0]
    return pl.pallas_call(
        functools.partial(near_kernel, bases, targets),
        out_shape=[jax.ShapeDtypeStruct((columns, targets * LEAF), dtype)] * len(bases),
        in_specs=[SMEM] * len(bases) + [VMEM] * 4,
        out_specs=[VMEM] * len(bases),
        scratch_shapes=[
            pltpu.VMEM((3 * targets + 1, columns, LEAF), f32),
            pltpu.VMEM((BATCH, LEAF, LEAF), bf16),
            pltpu.VMEM((BATCH, LEAF, LEAF), bf16),
        ],
        compiler_params=PARAMS,
        cost_estimate=cost(microseconds),
    )(*lists, target_rows, source_rows, mine, other)


def far_sum(out_ref, basis_ref, target, at, coefficient):
    out_ref[:, target * LEAF : (target + 1) * LEAF] = lax.dot_general(
        coefficient.astype(bf16),
        basis_ref[:, cluster(at)],
        (((0,), (0,)), ((), ())),
        preferred_element_type=f32,
    )


def far_kernel(seg_size, far_ref, couplings_ref, basis_ref, part, out_ref, skel):
    leaf = lax.axis_index("leaf") * couplings_ref.shape[0]
    clusters, far_count, rank, _ = couplings_ref.shape
    columns = out_ref.shape[0]
    pack = LEAF // columns

    def unpack(group, carry):
        block = part[pl.ds(pl.multiple_of(group * rank, rank), rank), :]
        for i in range(pack):
            skel[group * pack + i] = block[:, i * columns : (i + 1) * columns]
        return carry

    lax.fori_loop(0, part.shape[0] // rank, unpack, 0)
    for target in range(clusters):
        coefficient = jnp.zeros((rank, columns), f32)
        step = 256 // rank
        for at in range(0, far_count, step):
            left = jnp.concatenate([couplings_ref[target, at + i] for i in range(step)], axis=1)
            rows = [skel[far_ref[target, at + i]] for i in range(step)]
            coefficient = coefficient + jnp.dot(
                left, jnp.concatenate(rows, axis=0), preferred_element_type=f32
            )
        far_sum(out_ref, basis_ref, target, leaf + target, coefficient)


def far_kernel_phased(seg_size, far_ref, couplings_ref, basis_ref, *refs):
    parts, (out_ref, skel, side, held) = refs[:-4], refs[-4:]
    clusters, far_count, rank, _ = couplings_ref.shape
    columns = out_ref.shape[0]
    pack = LEAF // columns
    leaf = lax.axis_index("leaf") * clusters
    for target in range(clusters):
        for at in range(0, far_count, pack):
            side[target, :, at * rank : (at + pack) * rank] = jnp.concatenate(
                [couplings_ref[target, at + i] for i in range(pack)], axis=1
            )
    for order, part in enumerate(parts):
        for group in range(seg_size // pack):
            block = part[group * rank : (group + 1) * rank, :]
            for i in range(pack):
                skel[order * seg_size + group * pack + i] = block[:, i * columns : (i + 1) * columns]
    step = 256 // rank
    for target in range(clusters):
        coefficient = jnp.zeros((rank, columns), f32)
        for at in range(0, far_count, step):
            rows = [skel[far_ref[target, at + i]] for i in range(step)]
            coefficient = coefficient + jnp.dot(
                side[target, :, at * rank : (at + step) * rank],
                jnp.concatenate(rows, axis=0),
                preferred_element_type=f32,
            )
        held[target] = coefficient.astype(bf16)
    for target in range(clusters):
        far_sum(out_ref, basis_ref, target, leaf + target, held[target])


def on_device(points, charges, basis, couplings, near_src, far_src):
    blk_count = lax.axis_size("blk")
    mine = charges.T
    columns, seg_rows = mine.shape
    seg_size = seg_rows // LEAF
    rank = basis.shape[0]
    own_clusters, near_count = near_src.shape
    targets = own_clusters // 2
    cluster_total = seg_size * blk_count
    pack = LEAF // columns
    skel_rows = seg_size // pack * rank
    other = shifted(mine, "rhs", 1)

    own_list, prev_load, next_load = pl.pallas_call(
        functools.partial(list_kernel, seg_size),
        out_shape=[jax.ShapeDtypeStruct((8, LEAF), jnp.int32)]
        + [jax.ShapeDtypeStruct((skel_rows + 16, LEAF), bf16)] * 2,
        in_specs=[HBM] * 3,
        out_specs=[VMEM] * 3,
        scratch_shapes=[
            pltpu.VMEM(near_src.shape, jnp.int32),
            pltpu.VMEM(basis.shape, bf16),
            pltpu.VMEM(mine.shape, bf16),
            pltpu.SemaphoreType.DMA((3,)),
        ],
        compiler_params=pltpu.CompilerParams(vmem_limit_bytes=63 * 2**20),
        cost_estimate=cost(3.0),
    )(near_src, basis, mine)

    after_load = shifted(prev_load, "blk", -1)
    before_load = shifted(next_load, "blk", 1)

    def list_of(load):
        entries = load[skel_rows:].astype(jnp.int32)
        return entries[:8] + 256 * entries[8:]

    target_rows, source_rows = pl.pallas_call(
        functools.partial(feature_kernel, seg_size, targets, own_clusters),
        out_shape=[
            jax.ShapeDtypeStruct((3 * targets + 1, DEPTH, LEAF), bf16),
            jax.ShapeDtypeStruct((seg_size, LEAF, DEPTH), bf16),
        ],
        in_specs=[VMEM],
        out_specs=[VMEM, VMEM],
        compiler_params=PARAMS,
        cost_estimate=cost(0.7),
    )(points)
    args = (target_rows, source_rows, mine, other)
    (own_near,) = near_sums((targets,), targets, (own_list,), *args, f32, 2.6)
    own_near, before_load, after_load, later_load = lax.optimization_barrier(
        (own_near, before_load, after_load, prev_load)
    )
    lists = (list_of(before_load), list_of(after_load))
    to_before, to_after = near_sums((0, 2 * targets), targets, lists, *args, bf16, 4.0)
    from_after = shifted(to_before, "blk", -1)
    from_before = shifted(to_after, "blk", 1)

    blk = lax.axis_index("blk")
    first = blk * seg_size + lax.axis_index("leaf") * own_clusters
    entries = lax.dynamic_slice_in_dim(far_src, first, own_clusters, 0)
    far_shape = jax.ShapeDtypeStruct((columns, own_clusters * LEAF), f32)
    if blk_count == 4 and cluster_total <= 256:
        middle_load = shifted(later_load, "blk", 2)
        entries = lax.rem(entries + (blk_count - blk) * seg_size, cluster_total)
        far = pl.pallas_call(
            functools.partial(far_kernel_phased, seg_size),
            out_shape=far_shape,
            in_specs=[SMEM] + [VMEM] * 6,
            out_specs=VMEM,
            scratch_shapes=[
                pltpu.VMEM((cluster_total, rank, columns), bf16),
                pltpu.VMEM((own_clusters, rank, far_src.shape[1] * rank), bf16),
                pltpu.VMEM((own_clusters, rank, columns), bf16),
            ],
            compiler_params=PARAMS,
            cost_estimate=cost(3.0),
        )(entries, couplings, basis, prev_load, after_load, middle_load, before_load)
    else:
        far = pl.pallas_call(
            functools.partial(far_kernel, seg_size),
            out_shape=far_shape,
            in_specs=[SMEM] + [VMEM] * 3,
            out_specs=VMEM,
            scratch_shapes=[pltpu.VMEM((cluster_total, rank, columns), bf16)],
            compiler_params=PARAMS,
        )(entries, couplings, basis, lax.all_gather(prev_load[:skel_rows], "blk", axis=0, tiled=True))

    far, from_before, from_after = lax.optimization_barrier((far, from_before, from_after))
    near = own_near + from_before.astype(f32) + from_after.astype(f32)
    keep = near[:columns]
    got = shifted(near[columns:], "rhs", 1)
    even = lax.axis_index("rhs") == 0
    whole = jnp.concatenate([jnp.where(even, keep, got), jnp.where(even, got, keep)], axis=1)
    return (whole + far).astype(bf16).T


def solution(mesh):
    in_specs = (
        P(None, "groups"),
        P(("groups", "blk"), "rhs"),
        P(None, ("groups", "blk")),
        P(("groups", "blk", "leaf"), None, None, None),
        P(("groups", "blk", "leaf"), None),
        P("groups", None),
    )
    out_specs = P(("groups", "blk", "leaf"), "rhs")
    return jax.shard_map(
        on_device, mesh=mesh, in_specs=in_specs, out_specs=out_specs, check_vma=False
    )
```

```python
import functools

import jax
import jax.numpy as jnp
from jax import lax
from jax.experimental import pallas as pl
from jax.experimental.pallas import tpu as pltpu
from jax.sharding import PartitionSpec as P

LEAF = 128
BATCH = 12
DEPTH = 48

kernel_scale = 0.0625 / (4.0 * 3.141592653589793)
soften = 0.001
inverse_sq = 1.0 / (kernel_scale * kernel_scale)

bf16 = jnp.bfloat16
f32 = jnp.float32
VMEM = pl.BlockSpec(memory_space=pltpu.VMEM)
HBM = pl.BlockSpec(memory_space=pltpu.HBM)
SMEM = pl.BlockSpec(memory_space=pltpu.SMEM)
PARAMS = pltpu.CompilerParams(vmem_limit_bytes=48 * 2**20)


def cost(microseconds):
    return pl.CostEstimate(flops=int(microseconds * 1e9), bytes_accessed=0, transcendentals=0)


def shifted(block, axis, shift):
    count = lax.axis_size(axis)
    return lax.ppermute(block, axis, [(i, (i + shift) % count) for i in range(count)])


def cluster(index):
    return pl.ds(pl.multiple_of(index * LEAF, LEAF), LEAF)


def list_kernel(seg_size, near_hbm, basis_hbm, charges_hbm, own_ref, prev_ref, next_ref, near_ref, basis_ref, charges_ref, sems):
    copies = [
        pltpu.make_async_copy(near_hbm, near_ref, sems.at[0]),
        pltpu.make_async_copy(basis_hbm, basis_ref, sems.at[1]),
        pltpu.make_async_copy(charges_hbm, charges_ref, sems.at[2]),
    ]
    for copy in copies:
        copy.start()
    targets = near_ref.shape[0] // 2
    near_count = near_ref.shape[1]
    blk_count = lax.axis_size("blk")
    blk = lax.axis_index("blk")
    before = lax.rem(blk + blk_count - 1, blk_count)
    half = lax.axis_index("rhs")
    columns = charges_ref.shape[0]
    rank = basis_ref.shape[0]
    pack = LEAF // columns
    rows_end = seg_size // pack * rank

    def iota(shape, dim):
        return lax.broadcasted_iota(jnp.int32, shape, dim)

    def ones(condition):
        return jnp.where(condition, 1.0, 0.0).astype(bf16)

    lane = iota((targets, LEAF), 1)
    earlier = ones(iota((LEAF, LEAF), 0) < iota((LEAF, LEAF), 1))
    above = ones(iota((targets, targets), 1) < iota((targets, targets), 0))
    row = iota((8, LEAF), 0)
    lower = iota((LEAF, LEAF), 0)
    copies[0].wait()
    sources = jnp.where(half == 0, near_ref[:targets, :], near_ref[targets:, :])
    sources = jnp.concatenate(
        [sources, jnp.full((targets, LEAF - near_count), -1, jnp.int32)], axis=1
    )
    segment = jnp.zeros((targets, LEAF), jnp.int32)
    if seg_size & (seg_size - 1) == 0:
        segment = lax.shift_right_arithmetic(sources, seg_size.bit_length() - 1)
    else:
        segment = lax.div(sources, seg_size)
    local = (sources - segment * seg_size).astype(f32)
    is_own = segment == blk
    is_prev = jnp.logical_and(segment == before, jnp.logical_not(is_own))
    is_next = jnp.logical_and(lane < near_count, jnp.logical_not(jnp.logical_or(is_own, is_prev)))
    masks = (is_own, is_prev, is_next)
    place = jnp.zeros((targets, LEAF), f32)
    totals = []
    for mask in masks:
        within = jnp.dot(ones(mask), earlier, preferred_element_type=f32)
        count = jnp.broadcast_to(within[:, LEAF - 1 :], (targets, LEAF))
        start = jnp.dot(above, count.astype(bf16), preferred_element_type=f32)
        place = jnp.where(mask, start + within, place)
        totals.append(start[targets - 1 :, :] + count[targets - 1 :, :])
    place = place.astype(jnp.int32)
    left, right = [], []
    for target in range(targets):
        at = place[target : target + 1, :]
        here = lax.shift_right_logical(at, 7) == row
        rows = []
        for mask in masks:
            chosen = jnp.logical_and(here, jnp.where(mask[target : target + 1, :], 1, 0) == 1)
            rows.append(jnp.where(chosen, local[target : target + 1, :], 0.0))
            rows.append(jnp.where(chosen, float(target), 0.0))
        left.append(jnp.concatenate(rows, axis=0).astype(bf16))
        right.append(ones(lax.bitwise_and(at, LEAF - 1) == lower))
    lists = lax.dot_general(
        jnp.concatenate(left, axis=1),
        jnp.concatenate(right, axis=1),
        (((1,), (1,)), ((), ())),
        preferred_element_type=f32,
    )
    last = row * LEAF + iota((8, LEAF), 1) == 8 * LEAF - 1
    finished = []
    for i, total in enumerate(totals):
        high = jnp.floor(total * (1.0 / 256.0))
        finished.append(jnp.where(last, total - 256.0 * high, lists[16 * i : 16 * i + 8]))
        finished.append(jnp.where(last, high, lists[16 * i + 8 : 16 * i + 16]))
    own_ref[...] = finished[0].astype(jnp.int32) + 256 * finished[1].astype(jnp.int32)
    prev_ref[rows_end : rows_end + 16, :] = jnp.concatenate(finished[2:4], axis=0).astype(bf16)
    next_ref[rows_end : rows_end + 16, :] = jnp.concatenate(finished[4:6], axis=0).astype(bf16)

    copies[1].wait()
    copies[2].wait()
    blocks = []
    for group in range(seg_size // pack):
        rows = []
        for i in range(pack):
            at = (group * pack + i) * LEAF
            parts = [jnp.zeros((columns, LEAF), bf16)] * pack
            parts[i] = charges_ref[:, at : at + LEAF]
            rows.append(jnp.concatenate(parts, axis=1))
        at = group * pack * LEAF
        blocks.append(
            lax.dot_general(
                basis_ref[:, at : at + pack * LEAF],
                jnp.concatenate(rows, axis=0),
                (((1,), (1,)), ((), ())),
                preferred_element_type=f32,
            )
        )
    for group, block in enumerate(blocks):
        prev_ref[group * rank : (group + 1) * rank, :] = block.astype(bf16)
        next_ref[group * rank : (group + 1) * rank, :] = block.astype(bf16)


def split(value):
    high = value.astype(bf16).astype(f32)
    rest = value - high
    middle = rest.astype(bf16).astype(f32)
    return high, middle, rest - middle


def coords_of(points_ref, at):
    block = points_ref[:, cluster(at)]
    zero, one, two = block[0:1, :], block[1:2, :], block[2:3, :]
    return zero, one, two, zero * zero + one * one + two * two


def rows_of(values):
    row = lax.broadcasted_iota(jnp.int32, (8, LEAF), 0)
    out = jnp.zeros((8, LEAF), f32)
    for i, value in enumerate(values):
        out = jnp.where(row == i, value, out)
    return out


def target_features(points_ref, at):
    zero, one, two, norm = coords_of(points_ref, at)
    slope = -2.0 * inverse_sq
    rows = rows_of((zero * slope, one * slope, two * slope, (norm + soften) * inverse_sq, 1.0))
    high, middle, low = split(rows)
    return jnp.concatenate([high, high, middle, middle, high, low], axis=0).astype(bf16)


def source_features(points_ref, at):
    zero, one, two, norm = coords_of(points_ref, at)
    rows = rows_of((zero, one, two, 1.0, norm * inverse_sq))
    high, middle, low = split(rows)
    stacked = jnp.concatenate([high, middle, high, middle, low, high], axis=0)
    return jnp.transpose(stacked).astype(bf16)


def feature_kernel(seg_size, targets, leaf_clusters, points_ref, target_ref, source_ref):
    blk_count = lax.axis_size("blk")
    blk = lax.axis_index("blk")
    first = lax.axis_index("leaf") * leaf_clusters + lax.axis_index("rhs") * targets
    for which in range(3):
        segment = lax.rem(blk + which + blk_count - 1, blk_count)
        for i in range(targets):
            target_ref[which * targets + i] = target_features(
                points_ref, segment * seg_size + first + i
            )
    target_ref[3 * targets] = jnp.zeros((DEPTH, LEAF), bf16)

    def some_sources(step, carry):
        for u in range(8):
            at = step * 8 + u
            source_ref[at] = source_features(points_ref, blk * seg_size + at)
        return carry

    lax.fori_loop(0, seg_size // 8, some_sources, 0)


def near_kernel(bases, targets, *refs):
    count = len(bases)
    lists = refs[:count]
    target_ref, source_ref, mine_ref, other_ref = refs[count : count + 4]
    outs = refs[count + 4 : 2 * count + 4]
    total, even, odd = refs[2 * count + 4 :]
    lengths = [ref[7, LEAF - 1] for ref in lists]
    length = sum(lengths)
    batches = lax.div(length + (BATCH - 1), BATCH)
    total[...] = jnp.zeros_like(total)

    def pair(batch, u):
        at = batch * BATCH + u
        code = jnp.int32(3 * targets * 256)
        for i in reversed(range(count)):
            start = sum(lengths[:i])
            place = jnp.maximum(at - start, 0)
            entry = lists[i][lax.shift_right_logical(place, 7), lax.bitwise_and(place, 127)]
            code = jnp.where(at < start + lengths[i], entry + bases[i] * 256, code)
        return lax.shift_right_logical(code, 8), lax.bitwise_and(code, 255)

    def make(batch, slot):
        for u in range(BATCH):
            target, source = pair(batch, u)
            square = jnp.dot(source_ref[source], target_ref[target], preferred_element_type=f32)
            slot[u] = lax.rsqrt(square).astype(bf16)

    def use(batch, slot):
        sums = []
        for u in range(BATCH):
            target, source = pair(batch, u)
            charges = jnp.concatenate([mine_ref[:, cluster(source)], other_ref[:, cluster(source)]], axis=0)
            sums.append((target, jnp.dot(charges, slot[u], preferred_element_type=f32)))
        for target, value in sums:
            total[target] += value

    make(0, even)

    def body(step, carry):
        make(2 * step + 1, odd)
        use(2 * step, even)
        make(2 * step + 2, even)
        use(2 * step + 1, odd)
        return carry

    lax.fori_loop(0, lax.div(batches, 2), body, 0)

    @pl.when(lax.rem(batches, 2) == 1)
    def _():
        use(batches - 1, even)

    for base, out in zip(bases, outs):
        for i in range(targets):
            out[:, i * LEAF : (i + 1) * LEAF] = total[base + i].astype(out.dtype)


def near_sums(bases, targets, lists, target_rows, source_rows, mine, other, dtype, microseconds):
    columns = 2 * mine.shape[0]
    return pl.pallas_call(
        functools.partial(near_kernel, bases, targets),
        out_shape=[jax.ShapeDtypeStruct((columns, targets * LEAF), dtype)] * len(bases),
        in_specs=[SMEM] * len(bases) + [VMEM] * 4,
        out_specs=[VMEM] * len(bases),
        scratch_shapes=[
            pltpu.VMEM((3 * targets + 1, columns, LEAF), f32),
            pltpu.VMEM((BATCH, LEAF, LEAF), bf16),
            pltpu.VMEM((BATCH, LEAF, LEAF), bf16),
        ],
        compiler_params=PARAMS,
        cost_estimate=cost(microseconds),
    )(*lists, target_rows, source_rows, mine, other)


def far_sum(out_ref, basis_ref, target, at, coefficient):
    out_ref[:, target * LEAF : (target + 1) * LEAF] = lax.dot_general(
        coefficient.astype(bf16),
        basis_ref[:, cluster(at)],
        (((0,), (0,)), ((), ())),
        preferred_element_type=f32,
    )


def far_kernel(seg_size, far_ref, couplings_ref, basis_ref, part, out_ref, skel):
    leaf = lax.axis_index("leaf") * couplings_ref.shape[0]
    clusters, far_count, rank, _ = couplings_ref.shape
    columns = out_ref.shape[0]
    pack = LEAF // columns

    def unpack(group, carry):
        block = part[pl.ds(pl.multiple_of(group * rank, rank), rank), :]
        for i in range(pack):
            skel[group * pack + i] = block[:, i * columns : (i + 1) * columns]
        return carry

    lax.fori_loop(0, part.shape[0] // rank, unpack, 0)
    for target in range(clusters):
        coefficient = jnp.zeros((rank, columns), f32)
        step = 256 // rank
        for at in range(0, far_count, step):
            left = jnp.concatenate([couplings_ref[target, at + i] for i in range(step)], axis=1)
            rows = [skel[far_ref[target, at + i]] for i in range(step)]
            coefficient = coefficient + jnp.dot(
                left, jnp.concatenate(rows, axis=0), preferred_element_type=f32
            )
        far_sum(out_ref, basis_ref, target, leaf + target, coefficient)


def far_kernel_phased(seg_size, far_ref, couplings_ref, basis_ref, *refs):
    parts, (out_ref, skel, side, held) = refs[:-4], refs[-4:]
    clusters, far_count, rank, _ = couplings_ref.shape
    columns = out_ref.shape[0]
    pack = LEAF // columns
    leaf = lax.axis_index("leaf") * clusters
    for target in range(clusters):
        for at in range(0, far_count, pack):
            side[target, :, at * rank : (at + pack) * rank] = jnp.concatenate(
                [couplings_ref[target, at + i] for i in range(pack)], axis=1
            )
    for order, part in enumerate(parts):
        for group in range(seg_size // pack):
            block = part[group * rank : (group + 1) * rank, :]
            for i in range(pack):
                skel[order * seg_size + group * pack + i] = block[:, i * columns : (i + 1) * columns]
    step = 256 // rank
    for target in range(clusters):
        coefficient = jnp.zeros((rank, columns), f32)
        for at in range(0, far_count, step):
            rows = [skel[far_ref[target, at + i]] for i in range(step)]
            coefficient = coefficient + jnp.dot(
                side[target, :, at * rank : (at + step) * rank],
                jnp.concatenate(rows, axis=0),
                preferred_element_type=f32,
            )
        held[target] = coefficient.astype(bf16)
    for target in range(clusters):
        far_sum(out_ref, basis_ref, target, leaf + target, held[target])


def on_device(points, charges, basis, couplings, near_src, far_src):
    blk_count = lax.axis_size("blk")
    mine = charges.T
    columns, seg_rows = mine.shape
    seg_size = seg_rows // LEAF
    rank = basis.shape[0]
    own_clusters, near_count = near_src.shape
    targets = own_clusters // 2
    cluster_total = seg_size * blk_count
    pack = LEAF // columns
    skel_rows = seg_size // pack * rank
    own_list, prev_load, next_load = pl.pallas_call(
        functools.partial(list_kernel, seg_size),
        out_shape=[jax.ShapeDtypeStruct((8, LEAF), jnp.int32)]
        + [jax.ShapeDtypeStruct((skel_rows + 16, LEAF), bf16)] * 2,
        in_specs=[HBM] * 3,
        out_specs=[VMEM] * 3,
        scratch_shapes=[
            pltpu.VMEM(near_src.shape, jnp.int32),
            pltpu.VMEM(basis.shape, bf16),
            pltpu.VMEM(mine.shape, bf16),
            pltpu.SemaphoreType.DMA((3,)),
        ],
        compiler_params=pltpu.CompilerParams(vmem_limit_bytes=63 * 2**20),
        cost_estimate=cost(3.0),
    )(near_src, basis, mine)

    later_charges, prev_load = lax.optimization_barrier((mine, prev_load))
    other = shifted(later_charges, "rhs", 1)
    after_load = shifted(prev_load, "blk", -1)
    before_load = shifted(next_load, "blk", 1)

    def list_of(load):
        entries = load[skel_rows:].astype(jnp.int32)
        return entries[:8] + 256 * entries[8:]

    target_rows, source_rows = pl.pallas_call(
        functools.partial(feature_kernel, seg_size, targets, own_clusters),
        out_shape=[
            jax.ShapeDtypeStruct((3 * targets + 1, DEPTH, LEAF), bf16),
            jax.ShapeDtypeStruct((seg_size, LEAF, DEPTH), bf16),
        ],
        in_specs=[VMEM],
        out_specs=[VMEM, VMEM],
        compiler_params=PARAMS,
        cost_estimate=cost(0.7),
    )(points)
    target_rows, later_load = lax.optimization_barrier((target_rows, prev_load))
    args = (target_rows, source_rows, mine, other)
    (own_near,) = near_sums((targets,), targets, (own_list,), *args, f32, 2.6)
    own_near, before_load, after_load = lax.optimization_barrier((own_near, before_load, after_load))
    lists = (list_of(before_load), list_of(after_load))
    to_before, to_after = near_sums((0, 2 * targets), targets, lists, *args, bf16, 0.2)
    from_after = shifted(to_before, "blk", -1)
    from_before = shifted(to_after, "blk", 1)

    blk = lax.axis_index("blk")
    first = blk * seg_size + lax.axis_index("leaf") * own_clusters
    entries = lax.dynamic_slice_in_dim(far_src, first, own_clusters, 0)
    far_shape = jax.ShapeDtypeStruct((columns, own_clusters * LEAF), f32)
    if blk_count == 4 and cluster_total <= 256:
        middle_load = shifted(later_load, "blk", 2)
        entries = lax.rem(entries + (blk_count - blk) * seg_size, cluster_total)
        far = pl.pallas_call(
            functools.partial(far_kernel_phased, seg_size),
            out_shape=far_shape,
            in_specs=[SMEM] + [VMEM] * 6,
            out_specs=VMEM,
            scratch_shapes=[
                pltpu.VMEM((cluster_total, rank, columns), bf16),
                pltpu.VMEM((own_clusters, rank, far_src.shape[1] * rank), bf16),
                pltpu.VMEM((own_clusters, rank, columns), bf16),
            ],
            compiler_params=PARAMS,
            cost_estimate=cost(3.0),
        )(entries, couplings, basis, prev_load, after_load, middle_load, before_load)
    else:
        far = pl.pallas_call(
            functools.partial(far_kernel, seg_size),
            out_shape=far_shape,
            in_specs=[SMEM] + [VMEM] * 3,
            out_specs=VMEM,
            scratch_shapes=[pltpu.VMEM((cluster_total, rank, columns), bf16)],
            compiler_params=PARAMS,
        )(entries, couplings, basis, lax.all_gather(prev_load[:skel_rows], "blk", axis=0, tiled=True))

    far, from_before, from_after = lax.optimization_barrier((far, from_before, from_after))
    near = own_near + from_before.astype(f32) + from_after.astype(f32)
    keep = near[:columns]
    got = shifted(near[columns:], "rhs", 1)
    even = lax.axis_index("rhs") == 0
    whole = jnp.concatenate([jnp.where(even, keep, got), jnp.where(even, got, keep)], axis=1)
    return (whole + far).astype(bf16).T


def solution(mesh):
    in_specs = (
        P(None, "groups"),
        P(("groups", "blk"), "rhs"),
        P(None, ("groups", "blk")),
        P(("groups", "blk", "leaf"), None, None, None),
        P(("groups", "blk", "leaf"), None),
        P("groups", None),
    )
    out_specs = P(("groups", "blk", "leaf"), "rhs")
    return jax.shard_map(
        on_device, mesh=mesh, in_specs=in_specs, out_specs=out_specs, check_vma=False
    )
```

```python
import functools

import jax
import jax.numpy as jnp
from jax import lax
from jax.experimental import pallas as pl
from jax.experimental.pallas import tpu as pltpu
from jax.sharding import PartitionSpec as P

LEAF = 128
BATCH = 12
DEPTH = 48

kernel_scale = 0.0625 / (4.0 * 3.141592653589793)
soften = 0.001
inverse_sq = 1.0 / (kernel_scale * kernel_scale)

bf16 = jnp.bfloat16
f32 = jnp.float32
VMEM = pl.BlockSpec(memory_space=pltpu.VMEM)
HBM = pl.BlockSpec(memory_space=pltpu.HBM)
SMEM = pl.BlockSpec(memory_space=pltpu.SMEM)
PARAMS = pltpu.CompilerParams(vmem_limit_bytes=48 * 2**20)


def cost(microseconds):
    return pl.CostEstimate(flops=int(microseconds * 1e9), bytes_accessed=0, transcendentals=0)


def shifted(block, axis, shift):
    count = lax.axis_size(axis)
    return lax.ppermute(block, axis, [(i, (i + shift) % count) for i in range(count)])


def cluster(index):
    return pl.ds(pl.multiple_of(index * LEAF, LEAF), LEAF)


def list_kernel(seg_size, near_hbm, basis_hbm, charges_hbm, own_ref, prev_ref, next_ref, skel_ref, near_ref, basis_ref, charges_ref, sems):
    copies = [
        pltpu.make_async_copy(near_hbm, near_ref, sems.at[0]),
        pltpu.make_async_copy(basis_hbm, basis_ref, sems.at[1]),
        pltpu.make_async_copy(charges_hbm, charges_ref, sems.at[2]),
    ]
    for copy in copies:
        copy.start()
    targets = near_ref.shape[0] // 2
    near_count = near_ref.shape[1]
    blk_count = lax.axis_size("blk")
    blk = lax.axis_index("blk")
    before = lax.rem(blk + blk_count - 1, blk_count)
    half = lax.axis_index("rhs")
    columns = charges_ref.shape[0]
    rank = basis_ref.shape[0]
    pack = LEAF // columns

    def iota(shape, dim):
        return lax.broadcasted_iota(jnp.int32, shape, dim)

    def ones(condition):
        return jnp.where(condition, 1.0, 0.0).astype(bf16)

    lane = iota((targets, LEAF), 1)
    earlier = ones(iota((LEAF, LEAF), 0) < iota((LEAF, LEAF), 1))
    above = ones(iota((targets, targets), 1) < iota((targets, targets), 0))
    row = iota((8, LEAF), 0)
    lower = iota((LEAF, LEAF), 0)
    copies[0].wait()
    sources = jnp.where(half == 0, near_ref[:targets, :], near_ref[targets:, :])
    sources = jnp.concatenate(
        [sources, jnp.full((targets, LEAF - near_count), -1, jnp.int32)], axis=1
    )
    segment = jnp.zeros((targets, LEAF), jnp.int32)
    if seg_size & (seg_size - 1) == 0:
        segment = lax.shift_right_arithmetic(sources, seg_size.bit_length() - 1)
    else:
        segment = lax.div(sources, seg_size)
    local = (sources - segment * seg_size).astype(f32)
    is_own = segment == blk
    is_prev = jnp.logical_and(segment == before, jnp.logical_not(is_own))
    is_next = jnp.logical_and(lane < near_count, jnp.logical_not(jnp.logical_or(is_own, is_prev)))
    masks = (is_own, is_prev, is_next)
    place = jnp.zeros((targets, LEAF), f32)
    totals = []
    for mask in masks:
        within = jnp.dot(ones(mask), earlier, preferred_element_type=f32)
        count = jnp.broadcast_to(within[:, LEAF - 1 :], (targets, LEAF))
        start = jnp.dot(above, count.astype(bf16), preferred_element_type=f32)
        place = jnp.where(mask, start + within, place)
        totals.append(start[targets - 1 :, :] + count[targets - 1 :, :])
    place = place.astype(jnp.int32)
    left, right = [], []
    for target in range(targets):
        at = place[target : target + 1, :]
        here = lax.shift_right_logical(at, 7) == row
        rows = []
        for mask in masks:
            chosen = jnp.logical_and(here, jnp.where(mask[target : target + 1, :], 1, 0) == 1)
            rows.append(jnp.where(chosen, local[target : target + 1, :], 0.0))
            rows.append(jnp.where(chosen, float(target), 0.0))
        left.append(jnp.concatenate(rows, axis=0).astype(bf16))
        right.append(ones(lax.bitwise_and(at, LEAF - 1) == lower))
    lists = lax.dot_general(
        jnp.concatenate(left, axis=1),
        jnp.concatenate(right, axis=1),
        (((1,), (1,)), ((), ())),
        preferred_element_type=f32,
    )
    last = row * LEAF + iota((8, LEAF), 1) == 8 * LEAF - 1
    for i, out in enumerate((own_ref, prev_ref, next_ref)):
        codes = lists[16 * i : 16 * i + 8] + 256.0 * lists[16 * i + 8 : 16 * i + 16]
        out[...] = jnp.where(last, totals[i], codes).astype(jnp.int32)

    copies[1].wait()
    copies[2].wait()
    blocks = []
    for group in range(seg_size // pack):
        rows = []
        for i in range(pack):
            at = (group * pack + i) * LEAF
            parts = [jnp.zeros((columns, LEAF), bf16)] * pack
            parts[i] = charges_ref[:, at : at + LEAF]
            rows.append(jnp.concatenate(parts, axis=1))
        at = group * pack * LEAF
        blocks.append(
            lax.dot_general(
                basis_ref[:, at : at + pack * LEAF],
                jnp.concatenate(rows, axis=0),
                (((1,), (1,)), ((), ())),
                preferred_element_type=f32,
            )
        )
    for group, block in enumerate(blocks):
        skel_ref[group * rank : (group + 1) * rank, :] = block.astype(bf16)


def split(value):
    high = value.astype(bf16).astype(f32)
    rest = value - high
    middle = rest.astype(bf16).astype(f32)
    return high, middle, rest - middle


def coords_of(points_ref, at):
    block = points_ref[:, cluster(at)]
    zero, one, two = block[0:1, :], block[1:2, :], block[2:3, :]
    return zero, one, two, zero * zero + one * one + two * two


def rows_of(values):
    row = lax.broadcasted_iota(jnp.int32, (8, LEAF), 0)
    out = jnp.zeros((8, LEAF), f32)
    for i, value in enumerate(values):
        out = jnp.where(row == i, value, out)
    return out


def target_features(points_ref, at):
    zero, one, two, norm = coords_of(points_ref, at)
    slope = -2.0 * inverse_sq
    rows = rows_of((zero * slope, one * slope, two * slope, (norm + soften) * inverse_sq, 1.0))
    high, middle, low = split(rows)
    return jnp.concatenate([high, high, middle, middle, high, low], axis=0).astype(bf16)


def source_features(points_ref, at):
    zero, one, two, norm = coords_of(points_ref, at)
    rows = rows_of((zero, one, two, 1.0, norm * inverse_sq))
    high, middle, low = split(rows)
    stacked = jnp.concatenate([high, middle, high, middle, low, high], axis=0)
    return jnp.transpose(stacked).astype(bf16)


def feature_kernel(seg_size, targets, leaf_clusters, points_ref, target_ref, source_ref):
    blk_count = lax.axis_size("blk")
    blk = lax.axis_index("blk")
    first = lax.axis_index("leaf") * leaf_clusters + lax.axis_index("rhs") * targets
    for which in range(3):
        segment = lax.rem(blk + which + blk_count - 1, blk_count)
        for i in range(targets):
            target_ref[which * targets + i] = target_features(
                points_ref, segment * seg_size + first + i
            )
    target_ref[3 * targets] = jnp.zeros((DEPTH, LEAF), bf16)

    def some_sources(step, carry):
        for u in range(8):
            at = step * 8 + u
            source_ref[at] = source_features(points_ref, blk * seg_size + at)
        return carry

    lax.fori_loop(0, seg_size // 8, some_sources, 0)


def near_kernel(bases, targets, *refs):
    count = len(bases)
    lists = refs[:count]
    target_ref, source_ref, mine_ref, other_ref = refs[count : count + 4]
    outs = refs[count + 4 : 2 * count + 4]
    total, even, odd = refs[2 * count + 4 :]
    lengths = [ref[7, LEAF - 1] for ref in lists]
    length = sum(lengths)
    batches = lax.div(length + (BATCH - 1), BATCH)
    total[...] = jnp.zeros_like(total)

    def pair(batch, u):
        at = batch * BATCH + u
        code = jnp.int32(3 * targets * 256)
        for i in reversed(range(count)):
            start = sum(lengths[:i])
            place = jnp.maximum(at - start, 0)
            entry = lists[i][lax.shift_right_logical(place, 7), lax.bitwise_and(place, 127)]
            code = jnp.where(at < start + lengths[i], entry + bases[i] * 256, code)
        return lax.shift_right_logical(code, 8), lax.bitwise_and(code, 255)

    def make(batch, slot):
        for u in range(BATCH):
            target, source = pair(batch, u)
            square = jnp.dot(source_ref[source], target_ref[target], preferred_element_type=f32)
            slot[u] = lax.rsqrt(square).astype(bf16)

    def use(batch, slot):
        sums = []
        for u in range(BATCH):
            target, source = pair(batch, u)
            charges = jnp.concatenate([mine_ref[:, cluster(source)], other_ref[:, cluster(source)]], axis=0)
            sums.append((target, jnp.dot(charges, slot[u], preferred_element_type=f32)))
        for target, value in sums:
            total[target] += value

    make(0, even)

    def body(step, carry):
        make(2 * step + 1, odd)
        use(2 * step, even)
        make(2 * step + 2, even)
        use(2 * step + 1, odd)
        return carry

    lax.fori_loop(0, lax.div(batches, 2), body, 0)

    @pl.when(lax.rem(batches, 2) == 1)
    def _():
        use(batches - 1, even)

    for base, out in zip(bases, outs):
        for i in range(targets):
            out[:, i * LEAF : (i + 1) * LEAF] = total[base + i].astype(out.dtype)


def near_sums(bases, targets, lists, target_rows, source_rows, mine, other, dtype, microseconds):
    columns = 2 * mine.shape[0]
    return pl.pallas_call(
        functools.partial(near_kernel, bases, targets),
        out_shape=[jax.ShapeDtypeStruct((columns, targets * LEAF), dtype)] * len(bases),
        in_specs=[SMEM] * len(bases) + [VMEM] * 4,
        out_specs=[VMEM] * len(bases),
        scratch_shapes=[
            pltpu.VMEM((3 * targets + 1, columns, LEAF), f32),
            pltpu.VMEM((BATCH, LEAF, LEAF), bf16),
            pltpu.VMEM((BATCH, LEAF, LEAF), bf16),
        ],
        compiler_params=PARAMS,
        cost_estimate=cost(microseconds),
    )(*lists, target_rows, source_rows, mine, other)


def far_sum(out_ref, basis_ref, target, at, coefficient):
    out_ref[:, target * LEAF : (target + 1) * LEAF] = lax.dot_general(
        coefficient.astype(bf16),
        basis_ref[:, cluster(at)],
        (((0,), (0,)), ((), ())),
        preferred_element_type=f32,
    )


def far_kernel(seg_size, far_ref, couplings_ref, basis_ref, part, out_ref, skel):
    leaf = lax.axis_index("leaf") * couplings_ref.shape[0]
    clusters, far_count, rank, _ = couplings_ref.shape
    columns = out_ref.shape[0]
    pack = LEAF // columns

    def unpack(group, carry):
        block = part[pl.ds(pl.multiple_of(group * rank, rank), rank), :]
        for i in range(pack):
            skel[group * pack + i] = block[:, i * columns : (i + 1) * columns]
        return carry

    lax.fori_loop(0, part.shape[0] // rank, unpack, 0)
    for target in range(clusters):
        coefficient = jnp.zeros((rank, columns), f32)
        step = 256 // rank
        for at in range(0, far_count, step):
            left = jnp.concatenate([couplings_ref[target, at + i] for i in range(step)], axis=1)
            rows = [skel[far_ref[target, at + i]] for i in range(step)]
            coefficient = coefficient + jnp.dot(
                left, jnp.concatenate(rows, axis=0), preferred_element_type=f32
            )
        far_sum(out_ref, basis_ref, target, leaf + target, coefficient)


def far_kernel_phased(seg_size, far_ref, couplings_ref, basis_ref, *refs):
    parts, (out_ref, skel, side, held) = refs[:-4], refs[-4:]
    clusters, far_count, rank, _ = couplings_ref.shape
    columns = out_ref.shape[0]
    pack = LEAF // columns
    leaf = lax.axis_index("leaf") * clusters
    for target in range(clusters):
        for at in range(0, far_count, pack):
            side[target, :, at * rank : (at + pack) * rank] = jnp.concatenate(
                [couplings_ref[target, at + i] for i in range(pack)], axis=1
            )
    for order, part in enumerate(parts):
        for group in range(seg_size // pack):
            block = part[group * rank : (group + 1) * rank, :]
            for i in range(pack):
                skel[order * seg_size + group * pack + i] = block[:, i * columns : (i + 1) * columns]
    step = 256 // rank
    for target in range(clusters):
        coefficient = jnp.zeros((rank, columns), f32)
        for at in range(0, far_count, step):
            rows = [skel[far_ref[target, at + i]] for i in range(step)]
            coefficient = coefficient + jnp.dot(
                side[target, :, at * rank : (at + step) * rank],
                jnp.concatenate(rows, axis=0),
                preferred_element_type=f32,
            )
        held[target] = coefficient.astype(bf16)
    for target in range(clusters):
        far_sum(out_ref, basis_ref, target, leaf + target, held[target])


def on_device(points, charges, basis, couplings, near_src, far_src):
    blk_count = lax.axis_size("blk")
    mine = charges.T
    columns, seg_rows = mine.shape
    seg_size = seg_rows // LEAF
    rank = basis.shape[0]
    own_clusters, near_count = near_src.shape
    targets = own_clusters // 2
    cluster_total = seg_size * blk_count
    pack = LEAF // columns
    own_list, prev_list, next_list, skeleton = pl.pallas_call(
        functools.partial(list_kernel, seg_size),
        out_shape=[jax.ShapeDtypeStruct((8, LEAF), jnp.int32)] * 3
        + [jax.ShapeDtypeStruct((seg_size // pack * rank, LEAF), bf16)],
        in_specs=[HBM] * 3,
        out_specs=[VMEM] * 4,
        scratch_shapes=[
            pltpu.VMEM(near_src.shape, jnp.int32),
            pltpu.VMEM(basis.shape, bf16),
            pltpu.VMEM(mine.shape, bf16),
            pltpu.SemaphoreType.DMA((3,)),
        ],
        compiler_params=pltpu.CompilerParams(vmem_limit_bytes=63 * 2**20),
        cost_estimate=cost(0.01),
    )(near_src, basis, mine)

    points, prev_list, next_list = lax.optimization_barrier((points, prev_list, next_list))
    after_list = shifted(prev_list, "blk", -1)
    before_list = shifted(next_list, "blk", 1)
    target_rows, source_rows = pl.pallas_call(
        functools.partial(feature_kernel, seg_size, targets, own_clusters),
        out_shape=[
            jax.ShapeDtypeStruct((3 * targets + 1, DEPTH, LEAF), bf16),
            jax.ShapeDtypeStruct((seg_size, LEAF, DEPTH), bf16),
        ],
        in_specs=[VMEM],
        out_specs=[VMEM, VMEM],
        compiler_params=PARAMS,
        cost_estimate=cost(0.01),
    )(points)
    later_charges, skeleton = lax.optimization_barrier((mine, skeleton))
    other = shifted(later_charges, "rhs", 1)
    narrow = blk_count == 4 and cluster_total <= 256
    if narrow:
        skeletons = [skeleton] + [shifted(skeleton, "blk", -i) for i in range(1, blk_count)]
    else:
        skeletons = [lax.all_gather(skeleton, "blk", axis=0, tiled=True)]
    args = (target_rows, source_rows, mine, other)
    lists = (before_list, after_list)
    to_before, to_after = near_sums((0, 2 * targets), targets, lists, *args, bf16, 20.0)
    to_before, to_after, own_list = lax.optimization_barrier((to_before, to_after, own_list))
    from_after = shifted(to_before, "blk", -1)
    from_before = shifted(to_after, "blk", 1)
    (own_near,) = near_sums((targets,), targets, (own_list,), *args, f32, 20.0)
    own_near, skeletons = lax.optimization_barrier((own_near, skeletons))

    blk = lax.axis_index("blk")
    first = blk * seg_size + lax.axis_index("leaf") * own_clusters
    entries = lax.dynamic_slice_in_dim(far_src, first, own_clusters, 0)
    far_shape = jax.ShapeDtypeStruct((columns, own_clusters * LEAF), f32)
    if narrow:
        entries = lax.rem(entries + (blk_count - blk) * seg_size, cluster_total)
        far = pl.pallas_call(
            functools.partial(far_kernel_phased, seg_size),
            out_shape=far_shape,
            in_specs=[SMEM] + [VMEM] * 6,
            out_specs=VMEM,
            scratch_shapes=[
                pltpu.VMEM((cluster_total, rank, columns), bf16),
                pltpu.VMEM((own_clusters, rank, far_src.shape[1] * rank), bf16),
                pltpu.VMEM((own_clusters, rank, columns), bf16),
            ],
            compiler_params=PARAMS,
            cost_estimate=cost(0.01),
        )(entries, couplings, basis, *skeletons)
    else:
        far = pl.pallas_call(
            functools.partial(far_kernel, seg_size),
            out_shape=far_shape,
            in_specs=[SMEM] + [VMEM] * 3,
            out_specs=VMEM,
            scratch_shapes=[pltpu.VMEM((cluster_total, rank, columns), bf16)],
            compiler_params=PARAMS,
        )(entries, couplings, basis, *skeletons)

    far, from_before, from_after = lax.optimization_barrier((far, from_before, from_after))
    near = own_near + from_before.astype(f32) + from_after.astype(f32)
    keep = near[:columns]
    got = shifted(near[columns:], "rhs", 1)
    even = lax.axis_index("rhs") == 0
    whole = jnp.concatenate([jnp.where(even, keep, got), jnp.where(even, got, keep)], axis=1)
    return (whole + far).astype(bf16).T


def solution(mesh):
    in_specs = (
        P(None, "groups"),
        P(("groups", "blk"), "rhs"),
        P(None, ("groups", "blk")),
        P(("groups", "blk", "leaf"), None, None, None),
        P(("groups", "blk", "leaf"), None),
        P("groups", None),
    )
    out_specs = P(("groups", "blk", "leaf"), "rhs")
    return jax.shard_map(
        on_device, mesh=mesh, in_specs=in_specs, out_specs=out_specs, check_vma=False
    )
```

```python
import functools

import jax
import jax.numpy as jnp
from jax import lax
from jax.experimental import pallas as pl
from jax.experimental.pallas import tpu as pltpu
from jax.sharding import PartitionSpec as P

LEAF = 128
BATCH = 12
DEPTH = 48

kernel_scale = 0.0625 / (4.0 * 3.141592653589793)
soften = 0.001
inverse_sq = 1.0 / (kernel_scale * kernel_scale)

bf16 = jnp.bfloat16
f32 = jnp.float32
VMEM = pl.BlockSpec(memory_space=pltpu.VMEM)
HBM = pl.BlockSpec(memory_space=pltpu.HBM)
SMEM = pl.BlockSpec(memory_space=pltpu.SMEM)
PARAMS = pltpu.CompilerParams(vmem_limit_bytes=48 * 2**20)


def cost(microseconds):
    return pl.CostEstimate(flops=int(microseconds * 1e9), bytes_accessed=0, transcendentals=0)


def shifted(block, axis, shift):
    count = lax.axis_size(axis)
    return lax.ppermute(block, axis, [(i, (i + shift) % count) for i in range(count)])


def crossed(block, shift):
    count = lax.axis_size("blk")
    pairs = []
    for i in range(count):
        pairs.append((2 * i, (i + shift) % count * 2))
        pairs.append((2 * i + 1, (i - shift) % count * 2 + 1))
    return lax.ppermute(block, ("blk", "rhs"), pairs)


def cluster(index):
    return pl.ds(pl.multiple_of(index * LEAF, LEAF), LEAF)


def list_kernel(seg_size, near_hbm, basis_hbm, charges_hbm, own_ref, away_ref, skel_ref, near_ref, basis_ref, charges_ref, sems):
    copies = [
        pltpu.make_async_copy(near_hbm, near_ref, sems.at[0]),
        pltpu.make_async_copy(basis_hbm, basis_ref, sems.at[1]),
        pltpu.make_async_copy(charges_hbm, charges_ref, sems.at[2]),
    ]
    for copy in copies:
        copy.start()
    targets, near_count = near_ref.shape
    blk_count = lax.axis_size("blk")
    blk = lax.axis_index("blk")
    before = lax.rem(blk + blk_count - 1, blk_count)
    half = lax.axis_index("rhs")
    columns = charges_ref.shape[0]
    rank = basis_ref.shape[0]
    pack = LEAF // columns

    def iota(shape, dim):
        return lax.broadcasted_iota(jnp.int32, shape, dim)

    def ones(condition):
        return jnp.where(condition, 1.0, 0.0).astype(bf16)

    lane = iota((targets, LEAF), 1)
    in_half = iota((targets, LEAF), 0) // (targets // 2) == half
    earlier = ones(iota((LEAF, LEAF), 0) < iota((LEAF, LEAF), 1))
    above = ones(iota((targets, targets), 1) < iota((targets, targets), 0))
    row = iota((8, LEAF), 0)
    lower = iota((LEAF, LEAF), 0)
    copies[0].wait()
    sources = jnp.concatenate(
        [near_ref[...], jnp.full((targets, LEAF - near_count), -1, jnp.int32)], axis=1
    )
    segment = jnp.zeros((targets, LEAF), jnp.int32)
    if seg_size & (seg_size - 1) == 0:
        segment = lax.shift_right_arithmetic(sources, seg_size.bit_length() - 1)
    else:
        segment = lax.div(sources, seg_size)
    local = (sources - segment * seg_size).astype(f32)
    is_own = segment == blk
    is_prev = jnp.logical_and(segment == before, jnp.logical_not(is_own))
    is_next = jnp.logical_and(lane < near_count, jnp.logical_not(jnp.logical_or(is_own, is_prev)))
    away = jnp.where(half == 0, jnp.where(is_next, 1, 0), jnp.where(is_prev, 1, 0))
    masks = (jnp.logical_and(is_own, in_half), away == 1)
    place = jnp.zeros((targets, LEAF), f32)
    totals = []
    for mask in masks:
        within = jnp.dot(ones(mask), earlier, preferred_element_type=f32)
        count = jnp.broadcast_to(within[:, LEAF - 1 :], (targets, LEAF))
        start = jnp.dot(above, count.astype(bf16), preferred_element_type=f32)
        place = jnp.where(mask, start + within, place)
        totals.append(start[targets - 1 :, :] + count[targets - 1 :, :])
    place = place.astype(jnp.int32)
    left, right = [], []
    for target in range(targets):
        at = place[target : target + 1, :]
        here = lax.shift_right_logical(at, 7) == row
        rows = []
        for mask in masks:
            chosen = jnp.logical_and(here, jnp.where(mask[target : target + 1, :], 1, 0) == 1)
            rows.append(jnp.where(chosen, local[target : target + 1, :], 0.0))
            rows.append(jnp.where(chosen, float(target), 0.0))
        left.append(jnp.concatenate(rows, axis=0).astype(bf16))
        right.append(ones(lax.bitwise_and(at, LEAF - 1) == lower))
    lists = lax.dot_general(
        jnp.concatenate(left, axis=1),
        jnp.concatenate(right, axis=1),
        (((1,), (1,)), ((), ())),
        preferred_element_type=f32,
    )
    last = row * LEAF + iota((8, LEAF), 1) == 8 * LEAF - 1
    for i, out in enumerate((own_ref, away_ref)):
        codes = lists[16 * i : 16 * i + 8] + 256.0 * lists[16 * i + 8 : 16 * i + 16]
        out[...] = jnp.where(last, totals[i], codes).astype(jnp.int32)

    copies[1].wait()
    copies[2].wait()
    blocks = []
    for group in range(seg_size // pack):
        rows = []
        for i in range(pack):
            at = (group * pack + i) * LEAF
            parts = [jnp.zeros((columns, LEAF), bf16)] * pack
            parts[i] = charges_ref[:, at : at + LEAF]
            rows.append(jnp.concatenate(parts, axis=1))
        at = group * pack * LEAF
        blocks.append(
            lax.dot_general(
                basis_ref[:, at : at + pack * LEAF],
                jnp.concatenate(rows, axis=0),
                (((1,), (1,)), ((), ())),
                preferred_element_type=f32,
            )
        )
    for group, block in enumerate(blocks):
        skel_ref[group * rank : (group + 1) * rank, :] = block.astype(bf16)


def split(value):
    high = value.astype(bf16).astype(f32)
    rest = value - high
    middle = rest.astype(bf16).astype(f32)
    return high, middle, rest - middle


def coords_of(points_ref, at):
    block = points_ref[:, cluster(at)]
    zero, one, two = block[0:1, :], block[1:2, :], block[2:3, :]
    return zero, one, two, zero * zero + one * one + two * two


def rows_of(values):
    row = lax.broadcasted_iota(jnp.int32, (8, LEAF), 0)
    out = jnp.zeros((8, LEAF), f32)
    for i, value in enumerate(values):
        out = jnp.where(row == i, value, out)
    return out


def target_features(points_ref, at):
    zero, one, two, norm = coords_of(points_ref, at)
    slope = -2.0 * inverse_sq
    rows = rows_of((zero * slope, one * slope, two * slope, (norm + soften) * inverse_sq, 1.0))
    high, middle, low = split(rows)
    return jnp.concatenate([high, high, middle, middle, high, low], axis=0).astype(bf16)


def source_features(points_ref, at):
    zero, one, two, norm = coords_of(points_ref, at)
    rows = rows_of((zero, one, two, 1.0, norm * inverse_sq))
    high, middle, low = split(rows)
    stacked = jnp.concatenate([high, middle, high, middle, low, high], axis=0)
    return jnp.transpose(stacked).astype(bf16)


def feature_kernel(seg_size, targets, points_ref, target_ref, source_ref):
    blk_count = lax.axis_size("blk")
    blk = lax.axis_index("blk")
    first = lax.axis_index("leaf") * targets
    away = lax.rem(blk + 2 * lax.axis_index("rhs") + blk_count - 1, blk_count)
    for which, segment in enumerate((away, blk)):
        for i in range(targets):
            target_ref[which * targets + i] = target_features(points_ref, segment * seg_size + first + i)
    target_ref[2 * targets] = jnp.zeros((DEPTH, LEAF), bf16)

    def some_sources(step, carry):
        for u in range(8):
            at = step * 8 + u
            source_ref[at] = source_features(points_ref, blk * seg_size + at)
        return carry

    lax.fori_loop(0, seg_size // 8, some_sources, 0)


def near_kernel(base, list_ref, target_ref, source_ref, mine_ref, other_ref, out_ref, total, even, odd):
    targets = total.shape[0] - 1
    blank = target_ref.shape[0] - 1
    length = list_ref[7, LEAF - 1]
    batches = lax.div(length + (BATCH - 1), BATCH)
    total[...] = jnp.zeros_like(total)

    def pair(batch, u):
        at = batch * BATCH + u
        code = list_ref[lax.shift_right_logical(at, 7), lax.bitwise_and(at, 127)]
        code = jnp.where(at < length, code, targets * 256)
        return lax.shift_right_logical(code, 8), lax.bitwise_and(code, 255)

    def make(batch, slot):
        for u in range(BATCH):
            target, source = pair(batch, u)
            square = jnp.dot(source_ref[source], target_ref[jnp.minimum(base + target, blank)], preferred_element_type=f32)
            slot[u] = lax.rsqrt(square).astype(bf16)

    def use(batch, slot):
        sums = []
        for u in range(BATCH):
            target, source = pair(batch, u)
            charges = jnp.concatenate([mine_ref[:, cluster(source)], other_ref[:, cluster(source)]], axis=0)
            sums.append((target, jnp.dot(charges, slot[u], preferred_element_type=f32)))
        for target, value in sums:
            total[target] += value

    make(0, even)

    def body(step, carry):
        make(2 * step + 1, odd)
        use(2 * step, even)
        make(2 * step + 2, even)
        use(2 * step + 1, odd)
        return carry

    lax.fori_loop(0, lax.div(batches, 2), body, 0)

    @pl.when(lax.rem(batches, 2) == 1)
    def _():
        use(batches - 1, even)

    for i in range(targets):
        out_ref[:, i * LEAF : (i + 1) * LEAF] = total[i].astype(out_ref.dtype)


def near_sum(base, targets, pairs, target_rows, source_rows, mine, other, dtype):
    columns = 2 * mine.shape[0]
    return pl.pallas_call(
        functools.partial(near_kernel, base),
        out_shape=jax.ShapeDtypeStruct((columns, targets * LEAF), dtype),
        in_specs=[SMEM] + [VMEM] * 4,
        out_specs=VMEM,
        scratch_shapes=[
            pltpu.VMEM((targets + 1, columns, LEAF), f32),
            pltpu.VMEM((BATCH, LEAF, LEAF), bf16),
            pltpu.VMEM((BATCH, LEAF, LEAF), bf16),
        ],
        compiler_params=PARAMS,
        cost_estimate=cost(20.0),
    )(pairs, target_rows, source_rows, mine, other)


def far_sum(out_ref, basis_ref, target, at, coefficient):
    out_ref[:, target * LEAF : (target + 1) * LEAF] = lax.dot_general(
        coefficient.astype(bf16),
        basis_ref[:, cluster(at)],
        (((0,), (0,)), ((), ())),
        preferred_element_type=f32,
    )


def far_kernel(seg_size, far_ref, couplings_ref, basis_ref, part, out_ref, skel):
    leaf = lax.axis_index("leaf") * couplings_ref.shape[0]
    clusters, far_count, rank, _ = couplings_ref.shape
    columns = out_ref.shape[0]
    pack = LEAF // columns

    def unpack(group, carry):
        block = part[pl.ds(pl.multiple_of(group * rank, rank), rank), :]
        for i in range(pack):
            skel[group * pack + i] = block[:, i * columns : (i + 1) * columns]
        return carry

    lax.fori_loop(0, part.shape[0] // rank, unpack, 0)
    for target in range(clusters):
        coefficient = jnp.zeros((rank, columns), f32)
        step = 256 // rank
        for at in range(0, far_count, step):
            left = jnp.concatenate([couplings_ref[target, at + i] for i in range(step)], axis=1)
            rows = [skel[far_ref[target, at + i]] for i in range(step)]
            coefficient = coefficient + jnp.dot(
                left, jnp.concatenate(rows, axis=0), preferred_element_type=f32
            )
        far_sum(out_ref, basis_ref, target, leaf + target, coefficient)


def far_kernel_phased(seg_size, far_ref, couplings_ref, basis_ref, *refs):
    parts, (out_ref, skel, side, held) = refs[:-4], refs[-4:]
    clusters, far_count, rank, _ = couplings_ref.shape
    columns = out_ref.shape[0]
    pack = LEAF // columns
    leaf = lax.axis_index("leaf") * clusters
    for target in range(clusters):
        for at in range(0, far_count, pack):
            side[target, :, at * rank : (at + pack) * rank] = jnp.concatenate(
                [couplings_ref[target, at + i] for i in range(pack)], axis=1
            )
    for order, part in enumerate(parts):
        for group in range(seg_size // pack):
            block = part[group * rank : (group + 1) * rank, :]
            for i in range(pack):
                skel[order * seg_size + group * pack + i] = block[:, i * columns : (i + 1) * columns]
    step = 256 // rank
    for target in range(clusters):
        coefficient = jnp.zeros((rank, columns), f32)
        for at in range(0, far_count, step):
            rows = [skel[far_ref[target, at + i]] for i in range(step)]
            coefficient = coefficient + jnp.dot(
                side[target, :, at * rank : (at + step) * rank],
                jnp.concatenate(rows, axis=0),
                preferred_element_type=f32,
            )
        held[target] = coefficient.astype(bf16)
    for target in range(clusters):
        far_sum(out_ref, basis_ref, target, leaf + target, held[target])


def on_device(points, charges, basis, couplings, near_src, far_src):
    blk_count = lax.axis_size("blk")
    mine = charges.T
    columns, seg_rows = mine.shape
    seg_size = seg_rows // LEAF
    rank = basis.shape[0]
    own_clusters, near_count = near_src.shape
    cluster_total = seg_size * blk_count
    pack = LEAF // columns
    own_list, away_list, skeleton = pl.pallas_call(
        functools.partial(list_kernel, seg_size),
        out_shape=[jax.ShapeDtypeStruct((8, LEAF), jnp.int32)] * 2
        + [jax.ShapeDtypeStruct((seg_size // pack * rank, LEAF), bf16)],
        in_specs=[HBM] * 3,
        out_specs=[VMEM] * 3,
        scratch_shapes=[
            pltpu.VMEM(near_src.shape, jnp.int32),
            pltpu.VMEM(basis.shape, bf16),
            pltpu.VMEM(mine.shape, bf16),
            pltpu.SemaphoreType.DMA((3,)),
        ],
        compiler_params=pltpu.CompilerParams(vmem_limit_bytes=63 * 2**20),
        cost_estimate=cost(3.0),
    )(near_src, basis, mine)

    points, away_list = lax.optimization_barrier((points, away_list))
    pairs = crossed(away_list, 1)
    target_rows, source_rows = pl.pallas_call(
        functools.partial(feature_kernel, seg_size, own_clusters),
        out_shape=[
            jax.ShapeDtypeStruct((2 * own_clusters + 1, DEPTH, LEAF), bf16),
            jax.ShapeDtypeStruct((seg_size, LEAF, DEPTH), bf16),
        ],
        in_specs=[VMEM],
        out_specs=[VMEM, VMEM],
        compiler_params=PARAMS,
        cost_estimate=cost(0.7),
    )(points)
    later_charges, skeleton = lax.optimization_barrier((mine, skeleton))
    other = shifted(later_charges, "rhs", 1)
    narrow = blk_count == 4 and cluster_total <= 256
    if narrow:
        skeletons = [skeleton] + [shifted(skeleton, "blk", -i) for i in range(1, blk_count)]
    else:
        skeletons = [lax.all_gather(skeleton, "blk", axis=0, tiled=True)]
    args = (target_rows, source_rows, mine, other)
    partial = near_sum(0, own_clusters, pairs, *args, bf16)
    partial, own_list = lax.optimization_barrier((partial, own_list))
    returned = crossed(partial, -1)
    own_near = near_sum(own_clusters, own_clusters, own_list, *args, f32)
    own_near, skeletons = lax.optimization_barrier((own_near, skeletons))

    blk = lax.axis_index("blk")
    first = blk * seg_size + lax.axis_index("leaf") * own_clusters
    entries = lax.dynamic_slice_in_dim(far_src, first, own_clusters, 0)
    far_shape = jax.ShapeDtypeStruct((columns, own_clusters * LEAF), f32)
    if narrow:
        entries = lax.rem(entries + (blk_count - blk) * seg_size, cluster_total)
        far = pl.pallas_call(
            functools.partial(far_kernel_phased, seg_size),
            out_shape=far_shape,
            in_specs=[SMEM] + [VMEM] * 6,
            out_specs=VMEM,
            scratch_shapes=[
                pltpu.VMEM((cluster_total, rank, columns), bf16),
                pltpu.VMEM((own_clusters, rank, far_src.shape[1] * rank), bf16),
                pltpu.VMEM((own_clusters, rank, columns), bf16),
            ],
            compiler_params=PARAMS,
            cost_estimate=cost(0.01),
        )(entries, couplings, basis, *skeletons)
    else:
        far = pl.pallas_call(
            functools.partial(far_kernel, seg_size),
            out_shape=far_shape,
            in_specs=[SMEM] + [VMEM] * 3,
            out_specs=VMEM,
            scratch_shapes=[pltpu.VMEM((cluster_total, rank, columns), bf16)],
            compiler_params=PARAMS,
        )(entries, couplings, basis, *skeletons)

    far, returned = lax.optimization_barrier((far, returned))
    near = own_near + returned.astype(f32)
    got = shifted(near[columns:].astype(bf16), "rhs", 1)
    return (near[:columns] + got.astype(f32) + far).astype(bf16).T


def solution(mesh):
    in_specs = (
        P(None, "groups"),
        P(("groups", "blk"), "rhs"),
        P(None, ("groups", "blk")),
        P(("groups", "blk", "leaf"), None, None, None),
        P(("groups", "blk", "leaf"), None),
        P("groups", None),
    )
    out_specs = P(("groups", "blk", "leaf"), "rhs")
    return jax.shard_map(
        on_device, mesh=mesh, in_specs=in_specs, out_specs=out_specs, check_vma=False
    )
```

```python
import functools

import jax
import jax.numpy as jnp
from jax import lax
from jax.experimental import pallas as pl
from jax.experimental.pallas import tpu as pltpu
from jax.sharding import PartitionSpec as P

LEAF = 128
BATCH = 12
DEPTH = 48

kernel_scale = 0.0625 / (4.0 * 3.141592653589793)
soften = 0.001
inverse_sq = 1.0 / (kernel_scale * kernel_scale)

bf16 = jnp.bfloat16
f32 = jnp.float32
VMEM = pl.BlockSpec(memory_space=pltpu.VMEM)
HBM = pl.BlockSpec(memory_space=pltpu.HBM)
SMEM = pl.BlockSpec(memory_space=pltpu.SMEM)
PARAMS = pltpu.CompilerParams(vmem_limit_bytes=48 * 2**20)


def cost(microseconds):
    return pl.CostEstimate(flops=int(microseconds * 1e9), bytes_accessed=0, transcendentals=0)


def shifted(block, axis, shift):
    count = lax.axis_size(axis)
    return lax.ppermute(block, axis, [(i, (i + shift) % count) for i in range(count)])


def crossed(block, shift):
    count = lax.axis_size("blk")
    pairs = []
    for i in range(count):
        pairs.append((2 * i, (i + shift) % count * 2))
        pairs.append((2 * i + 1, (i - shift) % count * 2 + 1))
    return lax.ppermute(block, ("blk", "rhs"), pairs)


def cluster(index):
    return pl.ds(pl.multiple_of(index * LEAF, LEAF), LEAF)


def list_kernel(seg_size, near_hbm, basis_hbm, charges_hbm, own_ref, load_ref, near_ref, basis_ref, charges_ref, sems):
    copies = [
        pltpu.make_async_copy(near_hbm, near_ref, sems.at[0]),
        pltpu.make_async_copy(basis_hbm, basis_ref, sems.at[1]),
        pltpu.make_async_copy(charges_hbm, charges_ref, sems.at[2]),
    ]
    for copy in copies:
        copy.start()
    targets, near_count = near_ref.shape
    blk_count = lax.axis_size("blk")
    blk = lax.axis_index("blk")
    before = lax.rem(blk + blk_count - 1, blk_count)
    half = lax.axis_index("rhs")
    columns = charges_ref.shape[0]
    rank = basis_ref.shape[0]
    pack = LEAF // columns

    def iota(shape, dim):
        return lax.broadcasted_iota(jnp.int32, shape, dim)

    def ones(condition):
        return jnp.where(condition, 1.0, 0.0).astype(bf16)

    lane = iota((targets, LEAF), 1)
    in_half = iota((targets, LEAF), 0) // (targets // 2) == half
    earlier = ones(iota((LEAF, LEAF), 0) < iota((LEAF, LEAF), 1))
    above = ones(iota((targets, targets), 1) < iota((targets, targets), 0))
    row = iota((8, LEAF), 0)
    lower = iota((LEAF, LEAF), 0)
    copies[0].wait()
    sources = jnp.concatenate(
        [near_ref[...], jnp.full((targets, LEAF - near_count), -1, jnp.int32)], axis=1
    )
    segment = jnp.zeros((targets, LEAF), jnp.int32)
    if seg_size & (seg_size - 1) == 0:
        segment = lax.shift_right_arithmetic(sources, seg_size.bit_length() - 1)
    else:
        segment = lax.div(sources, seg_size)
    local = (sources - segment * seg_size).astype(f32)
    is_own = segment == blk
    is_prev = jnp.logical_and(segment == before, jnp.logical_not(is_own))
    is_next = jnp.logical_and(lane < near_count, jnp.logical_not(jnp.logical_or(is_own, is_prev)))
    leaving = jnp.where(half == 0, jnp.where(is_next, 1, 0), jnp.where(is_prev, 1, 0))
    masks = (jnp.logical_and(is_own, in_half), leaving == 1)
    place = jnp.zeros((targets, LEAF), f32)
    totals = []
    for mask in masks:
        within = jnp.dot(ones(mask), earlier, preferred_element_type=f32)
        count = jnp.broadcast_to(within[:, LEAF - 1 :], (targets, LEAF))
        start = jnp.dot(above, count.astype(bf16), preferred_element_type=f32)
        place = jnp.where(mask, start + within, place)
        totals.append(start[targets - 1 :, :] + count[targets - 1 :, :])
    place = place.astype(jnp.int32)
    left, right = [], []
    for target in range(targets):
        at = place[target : target + 1, :]
        here = lax.shift_right_logical(at, 7) == row
        rows = []
        for mask in masks:
            chosen = jnp.logical_and(here, jnp.where(mask[target : target + 1, :], 1, 0) == 1)
            rows.append(jnp.where(chosen, local[target : target + 1, :], 0.0))
            rows.append(jnp.where(chosen, float(target), 0.0))
        left.append(jnp.concatenate(rows, axis=0).astype(bf16))
        right.append(ones(lax.bitwise_and(at, LEAF - 1) == lower))
    lists = lax.dot_general(
        jnp.concatenate(left, axis=1),
        jnp.concatenate(right, axis=1),
        (((1,), (1,)), ((), ())),
        preferred_element_type=f32,
    )
    last = row * LEAF + iota((8, LEAF), 1) == 8 * LEAF - 1
    own = lists[:8] + 256.0 * lists[8:16]
    own_ref[...] = jnp.where(last, totals[0], own).astype(jnp.int32)
    high = jnp.floor(totals[1] * (1.0 / 256.0))
    away = jnp.concatenate(
        [jnp.where(last, totals[1] - 256.0 * high, lists[16:24]), jnp.where(last, high, lists[24:32])], axis=0
    )
    rows_end = seg_size // pack * rank
    load_ref[rows_end : rows_end + 16, :] = away.astype(bf16)

    copies[1].wait()
    copies[2].wait()
    blocks = []
    for group in range(seg_size // pack):
        rows = []
        for i in range(pack):
            at = (group * pack + i) * LEAF
            parts = [jnp.zeros((columns, LEAF), bf16)] * pack
            parts[i] = charges_ref[:, at : at + LEAF]
            rows.append(jnp.concatenate(parts, axis=1))
        at = group * pack * LEAF
        blocks.append(
            lax.dot_general(
                basis_ref[:, at : at + pack * LEAF],
                jnp.concatenate(rows, axis=0),
                (((1,), (1,)), ((), ())),
                preferred_element_type=f32,
            )
        )
    for group, block in enumerate(blocks):
        load_ref[group * rank : (group + 1) * rank, :] = block.astype(bf16)


def split(value):
    high = value.astype(bf16).astype(f32)
    rest = value - high
    middle = rest.astype(bf16).astype(f32)
    return high, middle, rest - middle


def coords_of(points_ref, at):
    block = points_ref[:, cluster(at)]
    zero, one, two = block[0:1, :], block[1:2, :], block[2:3, :]
    return zero, one, two, zero * zero + one * one + two * two


def rows_of(values):
    row = lax.broadcasted_iota(jnp.int32, (8, LEAF), 0)
    out = jnp.zeros((8, LEAF), f32)
    for i, value in enumerate(values):
        out = jnp.where(row == i, value, out)
    return out


def target_features(points_ref, at):
    zero, one, two, norm = coords_of(points_ref, at)
    slope = -2.0 * inverse_sq
    rows = rows_of((zero * slope, one * slope, two * slope, (norm + soften) * inverse_sq, 1.0))
    high, middle, low = split(rows)
    return jnp.concatenate([high, high, middle, middle, high, low], axis=0).astype(bf16)


def source_features(points_ref, at):
    zero, one, two, norm = coords_of(points_ref, at)
    rows = rows_of((zero, one, two, 1.0, norm * inverse_sq))
    high, middle, low = split(rows)
    stacked = jnp.concatenate([high, middle, high, middle, low, high], axis=0)
    return jnp.transpose(stacked).astype(bf16)


def feature_kernel(seg_size, targets, points_ref, target_ref, source_ref):
    blk_count = lax.axis_size("blk")
    blk = lax.axis_index("blk")
    first = lax.axis_index("leaf") * targets
    away = lax.rem(blk + 2 * lax.axis_index("rhs") + blk_count - 1, blk_count)
    for which, segment in enumerate((away, blk)):
        for i in range(targets):
            target_ref[which * targets + i] = target_features(points_ref, segment * seg_size + first + i)
    target_ref[2 * targets] = jnp.zeros((DEPTH, LEAF), bf16)

    def some_sources(step, carry):
        for u in range(8):
            at = step * 8 + u
            source_ref[at] = source_features(points_ref, blk * seg_size + at)
        return carry

    lax.fori_loop(0, seg_size // 8, some_sources, 0)


def near_kernel(base, list_ref, target_ref, source_ref, mine_ref, other_ref, out_ref, total, even, odd):
    targets = total.shape[0] - 1
    blank = target_ref.shape[0] - 1
    length = list_ref[7, LEAF - 1]
    batches = lax.div(length + (BATCH - 1), BATCH)
    total[...] = jnp.zeros_like(total)

    def pair(batch, u):
        at = batch * BATCH + u
        code = list_ref[lax.shift_right_logical(at, 7), lax.bitwise_and(at, 127)]
        code = jnp.where(at < length, code, targets * 256)
        return lax.shift_right_logical(code, 8), lax.bitwise_and(code, 255)

    def make(batch, slot):
        for u in range(BATCH):
            target, source = pair(batch, u)
            square = jnp.dot(source_ref[source], target_ref[jnp.minimum(base + target, blank)], preferred_element_type=f32)
            slot[u] = lax.rsqrt(square).astype(bf16)

    def use(batch, slot):
        sums = []
        for u in range(BATCH):
            target, source = pair(batch, u)
            charges = jnp.concatenate([mine_ref[:, cluster(source)], other_ref[:, cluster(source)]], axis=0)
            sums.append((target, jnp.dot(charges, slot[u], preferred_element_type=f32)))
        for target, value in sums:
            total[target] += value

    make(0, even)

    def body(step, carry):
        make(2 * step + 1, odd)
        use(2 * step, even)
        make(2 * step + 2, even)
        use(2 * step + 1, odd)
        return carry

    lax.fori_loop(0, lax.div(batches, 2), body, 0)

    @pl.when(lax.rem(batches, 2) == 1)
    def _():
        use(batches - 1, even)

    for i in range(targets):
        out_ref[:, i * LEAF : (i + 1) * LEAF] = total[i].astype(out_ref.dtype)


def near_sum(base, targets, pairs, target_rows, source_rows, mine, other, dtype):
    columns = 2 * mine.shape[0]
    return pl.pallas_call(
        functools.partial(near_kernel, base),
        out_shape=jax.ShapeDtypeStruct((columns, targets * LEAF), dtype),
        in_specs=[SMEM] + [VMEM] * 4,
        out_specs=VMEM,
        scratch_shapes=[
            pltpu.VMEM((targets + 1, columns, LEAF), f32),
            pltpu.VMEM((BATCH, LEAF, LEAF), bf16),
            pltpu.VMEM((BATCH, LEAF, LEAF), bf16),
        ],
        compiler_params=PARAMS,
        cost_estimate=cost(20.0),
    )(pairs, target_rows, source_rows, mine, other)


def far_sum(out_ref, basis_ref, target, at, coefficient):
    out_ref[:, target * LEAF : (target + 1) * LEAF] = lax.dot_general(
        coefficient.astype(bf16),
        basis_ref[:, cluster(at)],
        (((0,), (0,)), ((), ())),
        preferred_element_type=f32,
    )


def far_kernel(seg_size, far_ref, couplings_ref, basis_ref, part, out_ref, skel):
    leaf = lax.axis_index("leaf") * couplings_ref.shape[0]
    clusters, far_count, rank, _ = couplings_ref.shape
    columns = out_ref.shape[0]
    pack = LEAF // columns

    def unpack(group, carry):
        block = part[pl.ds(pl.multiple_of(group * rank, rank), rank), :]
        for i in range(pack):
            skel[group * pack + i] = block[:, i * columns : (i + 1) * columns]
        return carry

    lax.fori_loop(0, part.shape[0] // rank, unpack, 0)
    for target in range(clusters):
        coefficient = jnp.zeros((rank, columns), f32)
        step = 256 // rank
        for at in range(0, far_count, step):
            left = jnp.concatenate([couplings_ref[target, at + i] for i in range(step)], axis=1)
            rows = [skel[far_ref[target, at + i]] for i in range(step)]
            coefficient = coefficient + jnp.dot(
                left, jnp.concatenate(rows, axis=0), preferred_element_type=f32
            )
        far_sum(out_ref, basis_ref, target, leaf + target, coefficient)


def far_kernel_phased(seg_size, far_ref, couplings_ref, basis_ref, *refs):
    parts, (out_ref, skel, side, held) = refs[:-4], refs[-4:]
    clusters, far_count, rank, _ = couplings_ref.shape
    columns = out_ref.shape[0]
    pack = LEAF // columns
    leaf = lax.axis_index("leaf") * clusters
    for target in range(clusters):
        for at in range(0, far_count, pack):
            side[target, :, at * rank : (at + pack) * rank] = jnp.concatenate(
                [couplings_ref[target, at + i] for i in range(pack)], axis=1
            )
    for order, part in enumerate(parts):
        for group in range(seg_size // pack):
            block = part[group * rank : (group + 1) * rank, :]
            for i in range(pack):
                skel[order * seg_size + group * pack + i] = block[:, i * columns : (i + 1) * columns]
    step = 256 // rank
    for target in range(clusters):
        coefficient = jnp.zeros((rank, columns), f32)
        for at in range(0, far_count, step):
            rows = [skel[far_ref[target, at + i]] for i in range(step)]
            coefficient = coefficient + jnp.dot(
                side[target, :, at * rank : (at + step) * rank],
                jnp.concatenate(rows, axis=0),
                preferred_element_type=f32,
            )
        held[target] = coefficient.astype(bf16)
    for target in range(clusters):
        far_sum(out_ref, basis_ref, target, leaf + target, held[target])


def on_device(points, charges, basis, couplings, near_src, far_src):
    blk_count = lax.axis_size("blk")
    mine = charges.T
    columns, seg_rows = mine.shape
    seg_size = seg_rows // LEAF
    rank = basis.shape[0]
    own_clusters, near_count = near_src.shape
    cluster_total = seg_size * blk_count
    pack = LEAF // columns
    skel_rows = seg_size // pack * rank
    own_list, load = pl.pallas_call(
        functools.partial(list_kernel, seg_size),
        out_shape=[
            jax.ShapeDtypeStruct((8, LEAF), jnp.int32),
            jax.ShapeDtypeStruct((skel_rows + 16, LEAF), bf16),
        ],
        in_specs=[HBM] * 3,
        out_specs=[VMEM] * 2,
        scratch_shapes=[
            pltpu.VMEM(near_src.shape, jnp.int32),
            pltpu.VMEM(basis.shape, bf16),
            pltpu.VMEM(mine.shape, bf16),
            pltpu.SemaphoreType.DMA((3,)),
        ],
        compiler_params=pltpu.CompilerParams(vmem_limit_bytes=63 * 2**20),
        cost_estimate=cost(3.0),
    )(near_src, basis, mine)

    points, load = lax.optimization_barrier((points, load))
    first_load = crossed(load, 1)
    target_rows, source_rows = pl.pallas_call(
        functools.partial(feature_kernel, seg_size, own_clusters),
        out_shape=[
            jax.ShapeDtypeStruct((2 * own_clusters + 1, DEPTH, LEAF), bf16),
            jax.ShapeDtypeStruct((seg_size, LEAF, DEPTH), bf16),
        ],
        in_specs=[VMEM],
        out_specs=[VMEM, VMEM],
        compiler_params=PARAMS,
        cost_estimate=cost(0.7),
    )(points)
    target_rows, later_charges, later_load = lax.optimization_barrier((target_rows, mine, load))
    other = shifted(later_charges, "rhs", 1)
    narrow = blk_count == 4 and cluster_total <= 256
    if narrow:
        loads = [load, crossed(later_load, -1), shifted(later_load, "blk", 2), first_load]
    else:
        loads = [lax.all_gather(later_load[:skel_rows], "blk", axis=0, tiled=True)]
    args = (target_rows, source_rows, mine, other)
    codes = first_load[skel_rows:].astype(jnp.int32)
    pairs = codes[:8] + 256 * codes[8:]
    partial = near_sum(0, own_clusters, pairs, *args, bf16)
    partial, own_list = lax.optimization_barrier((partial, own_list))
    returned = crossed(partial, -1)
    own_near = near_sum(own_clusters, own_clusters, own_list, *args, f32)
    own_near, loads = lax.optimization_barrier((own_near, loads))

    blk = lax.axis_index("blk")
    first = blk * seg_size + lax.axis_index("leaf") * own_clusters
    entries = lax.dynamic_slice_in_dim(far_src, first, own_clusters, 0)
    far_shape = jax.ShapeDtypeStruct((columns, own_clusters * LEAF), f32)
    if narrow:
        segment = lax.div(entries, seg_size)
        ahead = jnp.where(lax.axis_index("rhs") == 0, segment - blk, blk - segment)
        order = lax.rem(ahead + blk_count, blk_count)
        entries = entries + (order - segment) * seg_size
        far = pl.pallas_call(
            functools.partial(far_kernel_phased, seg_size),
            out_shape=far_shape,
            in_specs=[SMEM] + [VMEM] * 6,
            out_specs=VMEM,
            scratch_shapes=[
                pltpu.VMEM((cluster_total, rank, columns), bf16),
                pltpu.VMEM((own_clusters, rank, far_src.shape[1] * rank), bf16),
                pltpu.VMEM((own_clusters, rank, columns), bf16),
            ],
            compiler_params=PARAMS,
            cost_estimate=cost(0.01),
        )(entries, couplings, basis, *loads)
    else:
        far = pl.pallas_call(
            functools.partial(far_kernel, seg_size),
            out_shape=far_shape,
            in_specs=[SMEM] + [VMEM] * 3,
            out_specs=VMEM,
            scratch_shapes=[pltpu.VMEM((cluster_total, rank, columns), bf16)],
            compiler_params=PARAMS,
        )(entries, couplings, basis, *loads)

    far, returned = lax.optimization_barrier((far, returned))
    near = own_near + returned.astype(f32)
    got = shifted(near[columns:].astype(bf16), "rhs", 1)
    return (near[:columns] + got.astype(f32) + far).astype(bf16).T


def solution(mesh):
    in_specs = (
        P(None, "groups"),
        P(("groups", "blk"), "rhs"),
        P(None, ("groups", "blk")),
        P(("groups", "blk", "leaf"), None, None, None),
        P(("groups", "blk", "leaf"), None),
        P("groups", None),
    )
    out_specs = P(("groups", "blk", "leaf"), "rhs")
    return jax.shard_map(
        on_device, mesh=mesh, in_specs=in_specs, out_specs=out_specs, check_vma=False
    )
```

```python
import functools

import jax
import jax.numpy as jnp
from jax import lax
from jax.experimental import pallas as pl
from jax.experimental.pallas import tpu as pltpu
from jax.sharding import PartitionSpec as P

LEAF = 128
BATCH = 12
DEPTH = 48

kernel_scale = 0.0625 / (4.0 * 3.141592653589793)
soften = 0.001
inverse_sq = 1.0 / (kernel_scale * kernel_scale)

bf16 = jnp.bfloat16
f32 = jnp.float32
VMEM = pl.BlockSpec(memory_space=pltpu.VMEM)
HBM = pl.BlockSpec(memory_space=pltpu.HBM)
SMEM = pl.BlockSpec(memory_space=pltpu.SMEM)
PARAMS = pltpu.CompilerParams(vmem_limit_bytes=48 * 2**20)


def cost(microseconds):
    return pl.CostEstimate(flops=int(microseconds * 1e9), bytes_accessed=0, transcendentals=0)


def shifted(block, axis, shift):
    count = lax.axis_size(axis)
    return lax.ppermute(block, axis, [(i, (i + shift) % count) for i in range(count)])


def crossed(block, shift):
    count = lax.axis_size("blk")
    pairs = []
    for i in range(count):
        pairs.append((2 * i, (i + shift) % count * 2))
        pairs.append((2 * i + 1, (i - shift) % count * 2 + 1))
    return lax.ppermute(block, ("blk", "rhs"), pairs)


def cluster(index):
    return pl.ds(pl.multiple_of(index * LEAF, LEAF), LEAF)


def list_kernel(seg_size, near_hbm, basis_hbm, charges_hbm, own_ref, load_ref, near_ref, basis_ref, charges_ref, sems):
    copies = [
        pltpu.make_async_copy(near_hbm, near_ref, sems.at[0]),
        pltpu.make_async_copy(basis_hbm, basis_ref, sems.at[1]),
        pltpu.make_async_copy(charges_hbm, charges_ref, sems.at[2]),
    ]
    for copy in copies:
        copy.start()
    targets, near_count = near_ref.shape
    blk_count = lax.axis_size("blk")
    blk = lax.axis_index("blk")
    before = lax.rem(blk + blk_count - 1, blk_count)
    half = lax.axis_index("rhs")
    columns = charges_ref.shape[0]
    rank = basis_ref.shape[0]
    pack = LEAF // columns
    slots = 4 if near_count <= LEAF // 4 and targets % 4 == 0 else 1
    width = LEAF // slots
    lines = targets // slots

    def iota(shape, dim):
        return lax.broadcasted_iota(jnp.int32, shape, dim)

    def ones(condition):
        return jnp.where(condition, 1.0, 0.0).astype(bf16)

    lane = iota((lines, LEAF), 1)
    target = iota((lines, LEAF), 0) * slots + lane // width
    in_half = target // (targets // 2) == half
    earlier = ones(iota((LEAF, LEAF), 0) < iota((LEAF, LEAF), 1))
    whole = jnp.ones((LEAF, LEAF), bf16)
    above = ones(iota((lines, lines), 1) < iota((lines, lines), 0))
    row = iota((8, LEAF), 0)
    lower = iota((LEAF, LEAF), 0)
    filler = jnp.full((1, width - near_count), -1, jnp.int32)
    for copy in copies:
        copy.wait()
    packed = []
    for line in range(lines):
        pieces = []
        for i in range(slots):
            at = line * slots + i
            pieces += [near_ref[at : at + 1, :], filler]
        packed.append(jnp.concatenate(pieces, axis=1))
    sources = jnp.concatenate(packed, axis=0)
    if seg_size & (seg_size - 1) == 0:
        segment = lax.shift_right_arithmetic(sources, seg_size.bit_length() - 1)
    else:
        segment = lax.div(sources, seg_size)
    local = (sources - segment * seg_size).astype(f32)
    is_own = segment == blk
    is_prev = jnp.logical_and(segment == before, jnp.logical_not(is_own))
    is_next = jnp.logical_and(sources >= 0, jnp.logical_not(jnp.logical_or(is_own, is_prev)))
    is_own = jnp.logical_and(jnp.logical_and(is_own, in_half), sources >= 0)
    is_prev = jnp.logical_and(is_prev, sources >= 0)
    leaving = jnp.where(half == 0, jnp.where(is_next, 1, 0), jnp.where(is_prev, 1, 0))
    masks = (is_own, leaving == 1)
    place = jnp.zeros((lines, LEAF), f32)
    totals = []
    for mask in masks:
        within = jnp.dot(ones(mask), earlier, preferred_element_type=f32)
        count = jnp.dot(ones(mask), whole, preferred_element_type=f32)
        start = jnp.dot(above, count.astype(bf16), preferred_element_type=f32)
        place = jnp.where(mask, start + within, place)
        totals.append(start[lines - 1 :, :] + count[lines - 1 :, :])
    place = place.astype(jnp.int32)
    target = target.astype(f32)
    left, right = [], []
    for line in range(lines):
        at = place[line : line + 1, :]
        here = lax.shift_right_logical(at, 7) == row
        rows = []
        for mask in masks:
            chosen = jnp.logical_and(here, jnp.where(mask[line : line + 1, :], 1, 0) == 1)
            rows.append(jnp.where(chosen, local[line : line + 1, :], 0.0))
            rows.append(jnp.where(chosen, target[line : line + 1, :], 0.0))
        left.append(jnp.concatenate(rows, axis=0).astype(bf16))
        right.append(ones(lax.bitwise_and(at, LEAF - 1) == lower))
    lists = lax.dot_general(
        jnp.concatenate(left, axis=1),
        jnp.concatenate(right, axis=1),
        (((1,), (1,)), ((), ())),
        preferred_element_type=f32,
    )
    last = row * LEAF + iota((8, LEAF), 1) == 8 * LEAF - 1
    own = lists[:8] + 256.0 * lists[8:16]
    own_ref[...] = jnp.where(last, totals[0], own).astype(jnp.int32)
    high = jnp.floor(totals[1] * (1.0 / 256.0))
    away = jnp.concatenate(
        [jnp.where(last, totals[1] - 256.0 * high, lists[16:24]), jnp.where(last, high, lists[24:32])], axis=0
    )
    rows_end = seg_size // pack * rank
    load_ref[rows_end : rows_end + 16, :] = away.astype(bf16)

    blocks = []
    for group in range(seg_size // pack):
        rows = []
        for i in range(pack):
            at = (group * pack + i) * LEAF
            parts = [jnp.zeros((columns, LEAF), bf16)] * pack
            parts[i] = charges_ref[:, at : at + LEAF]
            rows.append(jnp.concatenate(parts, axis=1))
        at = group * pack * LEAF
        blocks.append(
            lax.dot_general(
                basis_ref[:, at : at + pack * LEAF],
                jnp.concatenate(rows, axis=0),
                (((1,), (1,)), ((), ())),
                preferred_element_type=f32,
            )
        )
    for group, block in enumerate(blocks):
        load_ref[group * rank : (group + 1) * rank, :] = block.astype(bf16)


def split(value):
    high = value.astype(bf16).astype(f32)
    rest = value - high
    middle = rest.astype(bf16).astype(f32)
    return high, middle, rest - middle


def coords_of(points_ref, at):
    block = points_ref[:, cluster(at)]
    zero, one, two = block[0:1, :], block[1:2, :], block[2:3, :]
    return zero, one, two, zero * zero + one * one + two * two


def rows_of(values):
    row = lax.broadcasted_iota(jnp.int32, (8, LEAF), 0)
    out = jnp.zeros((8, LEAF), f32)
    for i, value in enumerate(values):
        out = jnp.where(row == i, value, out)
    return out


def target_features(points_ref, at):
    zero, one, two, norm = coords_of(points_ref, at)
    slope = -2.0 * inverse_sq
    rows = rows_of((zero * slope, one * slope, two * slope, (norm + soften) * inverse_sq, 1.0))
    high, middle, low = split(rows)
    return jnp.concatenate([high, high, middle, middle, high, low], axis=0).astype(bf16)


def source_features(points_ref, at):
    zero, one, two, norm = coords_of(points_ref, at)
    rows = rows_of((zero, one, two, 1.0, norm * inverse_sq))
    high, middle, low = split(rows)
    stacked = jnp.concatenate([high, middle, high, middle, low, high], axis=0)
    return jnp.transpose(stacked).astype(bf16)


def feature_kernel(seg_size, targets, points_ref, target_ref, source_ref):
    blk_count = lax.axis_size("blk")
    blk = lax.axis_index("blk")
    first = lax.axis_index("leaf") * targets
    away = lax.rem(blk + 2 * lax.axis_index("rhs") + blk_count - 1, blk_count)
    for which, segment in enumerate((away, blk)):
        for i in range(targets):
            target_ref[which * targets + i] = target_features(points_ref, segment * seg_size + first + i)
    target_ref[2 * targets] = jnp.zeros((DEPTH, LEAF), bf16)

    def some_sources(step, carry):
        for u in range(8):
            at = step * 8 + u
            source_ref[at] = source_features(points_ref, blk * seg_size + at)
        return carry

    lax.fori_loop(0, seg_size // 8, some_sources, 0)


def near_kernel(base, list_ref, target_ref, source_ref, mine_ref, other_ref, out_ref, total, even, odd):
    targets = total.shape[0] - 1
    blank = target_ref.shape[0] - 1
    length = list_ref[7, LEAF - 1]
    batches = lax.div(length + (BATCH - 1), BATCH)
    total[...] = jnp.zeros_like(total)

    def pair(batch, u):
        at = batch * BATCH + u
        code = list_ref[lax.shift_right_logical(at, 7), lax.bitwise_and(at, 127)]
        code = jnp.where(at < length, code, targets * 256)
        return lax.shift_right_logical(code, 8), lax.bitwise_and(code, 255)

    def make(batch, slot):
        for u in range(BATCH):
            target, source = pair(batch, u)
            square = jnp.dot(source_ref[source], target_ref[jnp.minimum(base + target, blank)], preferred_element_type=f32)
            slot[u] = lax.rsqrt(square).astype(bf16)

    def use(batch, slot):
        sums = []
        for u in range(BATCH):
            target, source = pair(batch, u)
            charges = jnp.concatenate([mine_ref[:, cluster(source)], other_ref[:, cluster(source)]], axis=0)
            sums.append((target, jnp.dot(charges, slot[u], preferred_element_type=f32)))
        for target, value in sums:
            total[target] += value

    make(0, even)

    def body(step, carry):
        make(2 * step + 1, odd)
        use(2 * step, even)
        make(2 * step + 2, even)
        use(2 * step + 1, odd)
        return carry

    lax.fori_loop(0, lax.div(batches, 2), body, 0)

    @pl.when(lax.rem(batches, 2) == 1)
    def _():
        use(batches - 1, even)

    for i in range(targets):
        out_ref[:, i * LEAF : (i + 1) * LEAF] = total[i].astype(out_ref.dtype)


def near_sum(base, targets, pairs, target_rows, source_rows, mine, other, dtype):
    columns = 2 * mine.shape[0]
    return pl.pallas_call(
        functools.partial(near_kernel, base),
        out_shape=jax.ShapeDtypeStruct((columns, targets * LEAF), dtype),
        in_specs=[SMEM] + [VMEM] * 4,
        out_specs=VMEM,
        scratch_shapes=[
            pltpu.VMEM((targets + 1, columns, LEAF), f32),
            pltpu.VMEM((BATCH, LEAF, LEAF), bf16),
            pltpu.VMEM((BATCH, LEAF, LEAF), bf16),
        ],
        compiler_params=PARAMS,
        cost_estimate=cost(20.0),
    )(pairs, target_rows, source_rows, mine, other)


def far_sum(out_ref, basis_ref, target, at, coefficient):
    out_ref[:, target * LEAF : (target + 1) * LEAF] = lax.dot_general(
        coefficient.astype(bf16),
        basis_ref[:, cluster(at)],
        (((0,), (0,)), ((), ())),
        preferred_element_type=f32,
    )


def far_kernel(seg_size, far_ref, couplings_ref, basis_ref, part, out_ref, skel):
    leaf = lax.axis_index("leaf") * couplings_ref.shape[0]
    clusters, far_count, rank, _ = couplings_ref.shape
    columns = out_ref.shape[0]
    pack = LEAF // columns

    def unpack(group, carry):
        block = part[pl.ds(pl.multiple_of(group * rank, rank), rank), :]
        for i in range(pack):
            skel[group * pack + i] = block[:, i * columns : (i + 1) * columns]
        return carry

    lax.fori_loop(0, part.shape[0] // rank, unpack, 0)
    for target in range(clusters):
        coefficient = jnp.zeros((rank, columns), f32)
        step = 256 // rank
        for at in range(0, far_count, step):
            left = jnp.concatenate([couplings_ref[target, at + i] for i in range(step)], axis=1)
            rows = [skel[far_ref[target, at + i]] for i in range(step)]
            coefficient = coefficient + jnp.dot(
                left, jnp.concatenate(rows, axis=0), preferred_element_type=f32
            )
        far_sum(out_ref, basis_ref, target, leaf + target, coefficient)


def far_kernel_phased(seg_size, far_ref, couplings_ref, basis_ref, *refs):
    parts, (out_ref, skel, side, held) = refs[:-4], refs[-4:]
    clusters, far_count, rank, _ = couplings_ref.shape
    columns = out_ref.shape[0]
    pack = LEAF // columns
    leaf = lax.axis_index("leaf") * clusters
    for target in range(clusters):
        for at in range(0, far_count, pack):
            side[target, :, at * rank : (at + pack) * rank] = jnp.concatenate(
                [couplings_ref[target, at + i] for i in range(pack)], axis=1
            )
    for order, part in enumerate(parts):
        for group in range(seg_size // pack):
            block = part[group * rank : (group + 1) * rank, :]
            for i in range(pack):
                skel[order * seg_size + group * pack + i] = block[:, i * columns : (i + 1) * columns]
    step = 256 // rank
    for target in range(clusters):
        coefficient = jnp.zeros((rank, columns), f32)
        for at in range(0, far_count, step):
            rows = [skel[far_ref[target, at + i]] for i in range(step)]
            coefficient = coefficient + jnp.dot(
                side[target, :, at * rank : (at + step) * rank],
                jnp.concatenate(rows, axis=0),
                preferred_element_type=f32,
            )
        held[target] = coefficient.astype(bf16)
    for target in range(clusters):
        far_sum(out_ref, basis_ref, target, leaf + target, held[target])


def on_device(points, charges, basis, couplings, near_src, far_src):
    blk_count = lax.axis_size("blk")
    mine = charges.T
    columns, seg_rows = mine.shape
    seg_size = seg_rows // LEAF
    rank = basis.shape[0]
    own_clusters, near_count = near_src.shape
    cluster_total = seg_size * blk_count
    pack = LEAF // columns
    skel_rows = seg_size // pack * rank
    other = shifted(mine, "rhs", 1)
    own_list, load = pl.pallas_call(
        functools.partial(list_kernel, seg_size),
        out_shape=[
            jax.ShapeDtypeStruct((8, LEAF), jnp.int32),
            jax.ShapeDtypeStruct((skel_rows + 16, LEAF), bf16),
        ],
        in_specs=[HBM] * 3,
        out_specs=[VMEM] * 2,
        scratch_shapes=[
            pltpu.VMEM(near_src.shape, jnp.int32),
            pltpu.VMEM(basis.shape, bf16),
            pltpu.VMEM(mine.shape, bf16),
            pltpu.SemaphoreType.DMA((3,)),
        ],
        compiler_params=pltpu.CompilerParams(vmem_limit_bytes=63 * 2**20),
        cost_estimate=cost(3.0),
    )(near_src, basis, mine)

    points, load = lax.optimization_barrier((points, load))
    first_load = crossed(load, 1)
    target_rows, source_rows = pl.pallas_call(
        functools.partial(feature_kernel, seg_size, own_clusters),
        out_shape=[
            jax.ShapeDtypeStruct((2 * own_clusters + 1, DEPTH, LEAF), bf16),
            jax.ShapeDtypeStruct((seg_size, LEAF, DEPTH), bf16),
        ],
        in_specs=[VMEM],
        out_specs=[VMEM, VMEM],
        compiler_params=PARAMS,
        cost_estimate=cost(0.7),
    )(points)
    target_rows, later_load = lax.optimization_barrier((target_rows, load))
    narrow = blk_count == 4 and cluster_total <= 256
    if narrow:
        loads = [load, crossed(later_load, -1), shifted(later_load, "blk", 2), first_load]
    else:
        loads = [lax.all_gather(later_load[:skel_rows], "blk", axis=0, tiled=True)]
    args = (target_rows, source_rows, mine, other)
    codes = first_load[skel_rows:].astype(jnp.int32)
    pairs = codes[:8] + 256 * codes[8:]
    partial = near_sum(0, own_clusters, pairs, *args, bf16)
    partial, own_list = lax.optimization_barrier((partial, own_list))
    returned = crossed(partial, -1)
    own_near = near_sum(own_clusters, own_clusters, own_list, *args, f32)
    own_near, loads = lax.optimization_barrier((own_near, loads))

    blk = lax.axis_index("blk")
    first = blk * seg_size + lax.axis_index("leaf") * own_clusters
    entries = lax.dynamic_slice_in_dim(far_src, first, own_clusters, 0)
    far_shape = jax.ShapeDtypeStruct((columns, own_clusters * LEAF), f32)
    if narrow:
        segment = lax.div(entries, seg_size)
        ahead = jnp.where(lax.axis_index("rhs") == 0, segment - blk, blk - segment)
        order = lax.rem(ahead + blk_count, blk_count)
        entries = entries + (order - segment) * seg_size
        far = pl.pallas_call(
            functools.partial(far_kernel_phased, seg_size),
            out_shape=far_shape,
            in_specs=[SMEM] + [VMEM] * 6,
            out_specs=VMEM,
            scratch_shapes=[
                pltpu.VMEM((cluster_total, rank, columns), bf16),
                pltpu.VMEM((own_clusters, rank, far_src.shape[1] * rank), bf16),
                pltpu.VMEM((own_clusters, rank, columns), bf16),
            ],
            compiler_params=PARAMS,
            cost_estimate=cost(0.01),
        )(entries, couplings, basis, *loads)
    else:
        far = pl.pallas_call(
            functools.partial(far_kernel, seg_size),
            out_shape=far_shape,
            in_specs=[SMEM] + [VMEM] * 3,
            out_specs=VMEM,
            scratch_shapes=[pltpu.VMEM((cluster_total, rank, columns), bf16)],
            compiler_params=PARAMS,
        )(entries, couplings, basis, *loads)

    far, returned = lax.optimization_barrier((far, returned))
    near = own_near + returned.astype(f32)
    got = shifted(near[columns:].astype(bf16), "rhs", 1)
    return (near[:columns] + got.astype(f32) + far).astype(bf16).T


def solution(mesh):
    in_specs = (
        P(None, "groups"),
        P(("groups", "blk"), "rhs"),
        P(None, ("groups", "blk")),
        P(("groups", "blk", "leaf"), None, None, None),
        P(("groups", "blk", "leaf"), None),
        P("groups", None),
    )
    out_specs = P(("groups", "blk", "leaf"), "rhs")
    return jax.shard_map(
        on_device, mesh=mesh, in_specs=in_specs, out_specs=out_specs, check_vma=False
    )
```

```python
import functools

import jax
import jax.numpy as jnp
from jax import lax
from jax.experimental import pallas as pl
from jax.experimental.pallas import tpu as pltpu
from jax.sharding import PartitionSpec as P

LEAF = 128
BATCH = 12
DEPTH = 48

kernel_scale = 0.0625 / (4.0 * 3.141592653589793)
soften = 0.001
inverse_sq = 1.0 / (kernel_scale * kernel_scale)

bf16 = jnp.bfloat16
f32 = jnp.float32
VMEM = pl.BlockSpec(memory_space=pltpu.VMEM)
HBM = pl.BlockSpec(memory_space=pltpu.HBM)
SMEM = pl.BlockSpec(memory_space=pltpu.SMEM)
PARAMS = pltpu.CompilerParams(vmem_limit_bytes=48 * 2**20)


def cost(microseconds):
    return pl.CostEstimate(flops=int(microseconds * 1e9), bytes_accessed=0, transcendentals=0)


def shifted(block, axis, shift):
    count = lax.axis_size(axis)
    return lax.ppermute(block, axis, [(i, (i + shift) % count) for i in range(count)])


def crossed(block, shift):
    count = lax.axis_size("blk")
    pairs = []
    for i in range(count):
        pairs.append((2 * i, (i + shift) % count * 2))
        pairs.append((2 * i + 1, (i - shift) % count * 2 + 1))
    return lax.ppermute(block, ("blk", "rhs"), pairs)


def cluster(index):
    return pl.ds(pl.multiple_of(index * LEAF, LEAF), LEAF)


def list_kernel(seg_size, near_hbm, basis_hbm, charges_hbm, own_ref, load_ref, near_ref, basis_ref, charges_ref, sems):
    copies = [
        pltpu.make_async_copy(near_hbm, near_ref, sems.at[0]),
        pltpu.make_async_copy(basis_hbm, basis_ref, sems.at[1]),
        pltpu.make_async_copy(charges_hbm, charges_ref, sems.at[2]),
    ]
    for copy in copies:
        copy.start()
    targets, near_count = near_ref.shape
    blk_count = lax.axis_size("blk")
    blk = lax.axis_index("blk")
    before = lax.rem(blk + blk_count - 1, blk_count)
    half = lax.axis_index("rhs")
    columns = charges_ref.shape[0]
    rank = basis_ref.shape[0]
    pack = LEAF // columns
    slots = 4 if near_count <= LEAF // 4 and targets % 4 == 0 else 1
    width = LEAF // slots
    lines = targets // slots

    def iota(shape, dim):
        return lax.broadcasted_iota(jnp.int32, shape, dim)

    def ones(condition):
        return jnp.where(condition, 1.0, 0.0).astype(bf16)

    lane = iota((lines, LEAF), 1)
    target = iota((lines, LEAF), 0) * slots + lane // width
    in_half = target // (targets // 2) == half
    earlier = ones(iota((LEAF, LEAF), 0) < iota((LEAF, LEAF), 1))
    whole = jnp.ones((LEAF, LEAF), bf16)
    above = ones(iota((lines, lines), 1) < iota((lines, lines), 0))
    row = iota((8, LEAF), 0)
    lower = iota((LEAF, LEAF), 0)
    filler = jnp.full((1, width - near_count), -1, jnp.int32)
    for copy in copies:
        copy.wait()
    packed = []
    for line in range(lines):
        pieces = []
        for i in range(slots):
            at = line * slots + i
            pieces += [near_ref[at : at + 1, :], filler]
        packed.append(jnp.concatenate(pieces, axis=1))
    sources = jnp.concatenate(packed, axis=0)
    if seg_size & (seg_size - 1) == 0:
        segment = lax.shift_right_arithmetic(sources, seg_size.bit_length() - 1)
    else:
        segment = lax.div(sources, seg_size)
    local = (sources - segment * seg_size).astype(f32)
    is_own = segment == blk
    is_prev = jnp.logical_and(segment == before, jnp.logical_not(is_own))
    is_next = jnp.logical_and(sources >= 0, jnp.logical_not(jnp.logical_or(is_own, is_prev)))
    is_own = jnp.logical_and(jnp.logical_and(is_own, in_half), sources >= 0)
    is_prev = jnp.logical_and(is_prev, sources >= 0)
    leaving = jnp.where(half == 0, jnp.where(is_next, 1, 0), jnp.where(is_prev, 1, 0))
    masks = (is_own, leaving == 1)
    place = jnp.zeros((lines, LEAF), f32)
    totals, middles = [], []
    for mask in masks:
        within = jnp.dot(ones(mask), earlier, preferred_element_type=f32)
        count = jnp.dot(ones(mask), whole, preferred_element_type=f32)
        start = jnp.dot(above, count.astype(bf16), preferred_element_type=f32)
        place = jnp.where(mask, start + within, place)
        totals.append(start[lines - 1 :, :] + count[lines - 1 :, :])
        middles.append(start[lines // 2 : lines // 2 + 1, :])
    place = place.astype(jnp.int32)
    target = target.astype(f32)
    left, right = [], []
    for line in range(lines):
        at = place[line : line + 1, :]
        here = lax.shift_right_logical(at, 7) == row
        rows = []
        for mask in masks:
            chosen = jnp.logical_and(here, jnp.where(mask[line : line + 1, :], 1, 0) == 1)
            rows.append(jnp.where(chosen, local[line : line + 1, :], 0.0))
            rows.append(jnp.where(chosen, target[line : line + 1, :], 0.0))
        left.append(jnp.concatenate(rows, axis=0).astype(bf16))
        right.append(ones(lax.bitwise_and(at, LEAF - 1) == lower))
    lists = lax.dot_general(
        jnp.concatenate(left, axis=1),
        jnp.concatenate(right, axis=1),
        (((1,), (1,)), ((), ())),
        preferred_element_type=f32,
    )
    last = row * LEAF + iota((8, LEAF), 1) == 8 * LEAF - 1
    own = lists[:8] + 256.0 * lists[8:16]
    own_ref[...] = jnp.where(last, totals[0], own).astype(jnp.int32)
    prior = row * LEAF + iota((8, LEAF), 1) == 8 * LEAF - 2
    length = jnp.where(prior, middles[1], totals[1])
    high = jnp.floor(length * (1.0 / 256.0))
    ends = jnp.logical_or(last, prior)
    away = jnp.concatenate(
        [jnp.where(ends, length - 256.0 * high, lists[16:24]), jnp.where(ends, high, lists[24:32])], axis=0
    )
    rows_end = seg_size // pack * rank
    load_ref[rows_end : rows_end + 16, :] = away.astype(bf16)

    blocks = []
    for group in range(seg_size // pack):
        rows = []
        for i in range(pack):
            at = (group * pack + i) * LEAF
            parts = [jnp.zeros((columns, LEAF), bf16)] * pack
            parts[i] = charges_ref[:, at : at + LEAF]
            rows.append(jnp.concatenate(parts, axis=1))
        at = group * pack * LEAF
        blocks.append(
            lax.dot_general(
                basis_ref[:, at : at + pack * LEAF],
                jnp.concatenate(rows, axis=0),
                (((1,), (1,)), ((), ())),
                preferred_element_type=f32,
            )
        )
    for group, block in enumerate(blocks):
        load_ref[group * rank : (group + 1) * rank, :] = block.astype(bf16)


def split(value):
    high = value.astype(bf16).astype(f32)
    rest = value - high
    middle = rest.astype(bf16).astype(f32)
    return high, middle, rest - middle


def coords_of(points_ref, at):
    block = points_ref[:, cluster(at)]
    zero, one, two = block[0:1, :], block[1:2, :], block[2:3, :]
    return zero, one, two, zero * zero + one * one + two * two


def rows_of(values):
    row = lax.broadcasted_iota(jnp.int32, (8, LEAF), 0)
    out = jnp.zeros((8, LEAF), f32)
    for i, value in enumerate(values):
        out = jnp.where(row == i, value, out)
    return out


def target_features(points_ref, at):
    zero, one, two, norm = coords_of(points_ref, at)
    slope = -2.0 * inverse_sq
    rows = rows_of((zero * slope, one * slope, two * slope, (norm + soften) * inverse_sq, 1.0))
    high, middle, low = split(rows)
    return jnp.concatenate([high, high, middle, middle, high, low], axis=0).astype(bf16)


def source_features(points_ref, at):
    zero, one, two, norm = coords_of(points_ref, at)
    rows = rows_of((zero, one, two, 1.0, norm * inverse_sq))
    high, middle, low = split(rows)
    stacked = jnp.concatenate([high, middle, high, middle, low, high], axis=0)
    return jnp.transpose(stacked).astype(bf16)


def feature_kernel(seg_size, targets, points_ref, target_ref, source_ref):
    blk_count = lax.axis_size("blk")
    blk = lax.axis_index("blk")
    first = lax.axis_index("leaf") * targets
    away = lax.rem(blk + 2 * lax.axis_index("rhs") + blk_count - 1, blk_count)
    for which, segment in enumerate((away, blk)):
        for i in range(targets):
            target_ref[which * targets + i] = target_features(points_ref, segment * seg_size + first + i)
    target_ref[2 * targets] = jnp.zeros((DEPTH, LEAF), bf16)

    def some_sources(step, carry):
        for u in range(8):
            at = step * 8 + u
            source_ref[at] = source_features(points_ref, blk * seg_size + at)
        return carry

    lax.fori_loop(0, seg_size // 8, some_sources, 0)


def near_kernel(base, part, list_ref, target_ref, source_ref, mine_ref, other_ref, out_ref, total, even, odd):
    targets = total.shape[0] - 1
    blank = target_ref.shape[0] - 1
    skipped = targets if part == 1 else 0
    begin = list_ref[7, LEAF - 2] if part == 1 else 0
    end = list_ref[7, LEAF - 2] if part == 0 else list_ref[7, LEAF - 1]
    batches = lax.div(end - begin + (BATCH - 1), BATCH)
    total[...] = jnp.zeros_like(total)

    def pair(batch, u):
        at = begin + batch * BATCH + u
        code = list_ref[lax.shift_right_logical(at, 7), lax.bitwise_and(at, 127)]
        code = jnp.where(at < end, code, (skipped + targets) * 256)
        return lax.shift_right_logical(code, 8), lax.bitwise_and(code, 255)

    def make(batch, slot):
        for u in range(BATCH):
            target, source = pair(batch, u)
            square = jnp.dot(source_ref[source], target_ref[jnp.minimum(base + target, blank)], preferred_element_type=f32)
            slot[u] = lax.rsqrt(square).astype(bf16)

    def use(batch, slot):
        sums = []
        for u in range(BATCH):
            target, source = pair(batch, u)
            charges = jnp.concatenate([mine_ref[:, cluster(source)], other_ref[:, cluster(source)]], axis=0)
            sums.append((target, jnp.dot(charges, slot[u], preferred_element_type=f32)))
        for target, value in sums:
            total[target - skipped] += value

    make(0, even)

    def body(step, carry):
        make(2 * step + 1, odd)
        use(2 * step, even)
        make(2 * step + 2, even)
        use(2 * step + 1, odd)
        return carry

    lax.fori_loop(0, lax.div(batches, 2), body, 0)

    @pl.when(lax.rem(batches, 2) == 1)
    def _():
        use(batches - 1, even)

    for i in range(targets):
        out_ref[:, i * LEAF : (i + 1) * LEAF] = total[i].astype(out_ref.dtype)


def near_sum(base, part, microseconds, targets, pairs, target_rows, source_rows, mine, other, dtype):
    columns = 2 * mine.shape[0]
    return pl.pallas_call(
        functools.partial(near_kernel, base, part),
        out_shape=jax.ShapeDtypeStruct((columns, targets * LEAF), dtype),
        in_specs=[SMEM] + [VMEM] * 4,
        out_specs=VMEM,
        scratch_shapes=[
            pltpu.VMEM((targets + 1, columns, LEAF), f32),
            pltpu.VMEM((BATCH, LEAF, LEAF), bf16),
            pltpu.VMEM((BATCH, LEAF, LEAF), bf16),
        ],
        compiler_params=PARAMS,
        cost_estimate=cost(microseconds),
    )(pairs, target_rows, source_rows, mine, other)


def far_sum(out_ref, basis_ref, target, at, coefficient):
    out_ref[:, target * LEAF : (target + 1) * LEAF] = lax.dot_general(
        coefficient.astype(bf16),
        basis_ref[:, cluster(at)],
        (((0,), (0,)), ((), ())),
        preferred_element_type=f32,
    )


def far_kernel(seg_size, far_ref, couplings_ref, basis_ref, part, out_ref, skel):
    leaf = lax.axis_index("leaf") * couplings_ref.shape[0]
    clusters, far_count, rank, _ = couplings_ref.shape
    columns = out_ref.shape[0]
    pack = LEAF // columns

    def unpack(group, carry):
        block = part[pl.ds(pl.multiple_of(group * rank, rank), rank), :]
        for i in range(pack):
            skel[group * pack + i] = block[:, i * columns : (i + 1) * columns]
        return carry

    lax.fori_loop(0, part.shape[0] // rank, unpack, 0)
    for target in range(clusters):
        coefficient = jnp.zeros((rank, columns), f32)
        step = 256 // rank
        for at in range(0, far_count, step):
            left = jnp.concatenate([couplings_ref[target, at + i] for i in range(step)], axis=1)
            rows = [skel[far_ref[target, at + i]] for i in range(step)]
            coefficient = coefficient + jnp.dot(
                left, jnp.concatenate(rows, axis=0), preferred_element_type=f32
            )
        far_sum(out_ref, basis_ref, target, leaf + target, coefficient)


def far_kernel_phased(seg_size, far_ref, couplings_ref, basis_ref, *refs):
    parts, (out_ref, skel, side, held) = refs[:-4], refs[-4:]
    clusters, far_count, rank, _ = couplings_ref.shape
    columns = out_ref.shape[0]
    pack = LEAF // columns
    leaf = lax.axis_index("leaf") * clusters
    for target in range(clusters):
        for at in range(0, far_count, pack):
            side[target, :, at * rank : (at + pack) * rank] = jnp.concatenate(
                [couplings_ref[target, at + i] for i in range(pack)], axis=1
            )
    for order, part in enumerate(parts):
        for group in range(seg_size // pack):
            block = part[group * rank : (group + 1) * rank, :]
            for i in range(pack):
                skel[order * seg_size + group * pack + i] = block[:, i * columns : (i + 1) * columns]
    step = 256 // rank
    for target in range(clusters):
        coefficient = jnp.zeros((rank, columns), f32)
        for at in range(0, far_count, step):
            rows = [skel[far_ref[target, at + i]] for i in range(step)]
            coefficient = coefficient + jnp.dot(
                side[target, :, at * rank : (at + step) * rank],
                jnp.concatenate(rows, axis=0),
                preferred_element_type=f32,
            )
        held[target] = coefficient.astype(bf16)
    for target in range(clusters):
        far_sum(out_ref, basis_ref, target, leaf + target, held[target])


def on_device(points, charges, basis, couplings, near_src, far_src):
    blk_count = lax.axis_size("blk")
    mine = charges.T
    columns, seg_rows = mine.shape
    seg_size = seg_rows // LEAF
    rank = basis.shape[0]
    own_clusters, near_count = near_src.shape
    cluster_total = seg_size * blk_count
    pack = LEAF // columns
    skel_rows = seg_size // pack * rank
    other = shifted(mine, "rhs", 1)
    own_list, load = pl.pallas_call(
        functools.partial(list_kernel, seg_size),
        out_shape=[
            jax.ShapeDtypeStruct((8, LEAF), jnp.int32),
            jax.ShapeDtypeStruct((skel_rows + 16, LEAF), bf16),
        ],
        in_specs=[HBM] * 3,
        out_specs=[VMEM] * 2,
        scratch_shapes=[
            pltpu.VMEM(near_src.shape, jnp.int32),
            pltpu.VMEM(basis.shape, bf16),
            pltpu.VMEM(mine.shape, bf16),
            pltpu.SemaphoreType.DMA((3,)),
        ],
        compiler_params=pltpu.CompilerParams(vmem_limit_bytes=63 * 2**20),
        cost_estimate=cost(3.0),
    )(near_src, basis, mine)

    points, load = lax.optimization_barrier((points, load))
    first_load = crossed(load, 1)
    target_rows, source_rows = pl.pallas_call(
        functools.partial(feature_kernel, seg_size, own_clusters),
        out_shape=[
            jax.ShapeDtypeStruct((2 * own_clusters + 1, DEPTH, LEAF), bf16),
            jax.ShapeDtypeStruct((seg_size, LEAF, DEPTH), bf16),
        ],
        in_specs=[VMEM],
        out_specs=[VMEM, VMEM],
        compiler_params=PARAMS,
        cost_estimate=cost(0.7),
    )(points)
    target_rows, later_load = lax.optimization_barrier((target_rows, load))
    narrow = blk_count == 4 and cluster_total <= 256
    if narrow:
        loads = [load, crossed(later_load, -1), shifted(later_load, "blk", 2), first_load]
    else:
        loads = [lax.all_gather(later_load[:skel_rows], "blk", axis=0, tiled=True)]
    args = (target_rows, source_rows, mine, other)
    codes = first_load[skel_rows:].astype(jnp.int32)
    pairs = codes[:8] + 256 * codes[8:]
    low = near_sum(0, 0, 20.0, own_clusters // 2, pairs, *args, bf16)
    low, pairs = lax.optimization_barrier((low, pairs))
    low_back = crossed(low, -1)
    high = near_sum(0, 1, 20.0, own_clusters // 2, pairs, *args, bf16)
    high, own_list = lax.optimization_barrier((high, own_list))
    high_back = crossed(high, -1)
    low_back, high, own_list = lax.optimization_barrier((low_back, high, own_list))
    own_near = near_sum(own_clusters, None, 20.0, own_clusters, own_list, *args, f32)
    own_near, loads = lax.optimization_barrier((own_near, loads))

    blk = lax.axis_index("blk")
    first = blk * seg_size + lax.axis_index("leaf") * own_clusters
    entries = lax.dynamic_slice_in_dim(far_src, first, own_clusters, 0)
    far_shape = jax.ShapeDtypeStruct((columns, own_clusters * LEAF), f32)
    if narrow:
        segment = lax.div(entries, seg_size)
        ahead = jnp.where(lax.axis_index("rhs") == 0, segment - blk, blk - segment)
        order = lax.rem(ahead + blk_count, blk_count)
        entries = entries + (order - segment) * seg_size
        far = pl.pallas_call(
            functools.partial(far_kernel_phased, seg_size),
            out_shape=far_shape,
            in_specs=[SMEM] + [VMEM] * 6,
            out_specs=VMEM,
            scratch_shapes=[
                pltpu.VMEM((cluster_total, rank, columns), bf16),
                pltpu.VMEM((own_clusters, rank, far_src.shape[1] * rank), bf16),
                pltpu.VMEM((own_clusters, rank, columns), bf16),
            ],
            compiler_params=PARAMS,
            cost_estimate=cost(0.01),
        )(entries, couplings, basis, *loads)
    else:
        far = pl.pallas_call(
            functools.partial(far_kernel, seg_size),
            out_shape=far_shape,
            in_specs=[SMEM] + [VMEM] * 3,
            out_specs=VMEM,
            scratch_shapes=[pltpu.VMEM((cluster_total, rank, columns), bf16)],
            compiler_params=PARAMS,
        )(entries, couplings, basis, *loads)

    far, low_back, high_back = lax.optimization_barrier((far, low_back, high_back))
    near = own_near + jnp.concatenate([low_back, high_back], axis=1).astype(f32)
    got = shifted(near[columns:].astype(bf16), "rhs", 1)
    return (near[:columns] + got.astype(f32) + far).astype(bf16).T


def solution(mesh):
    in_specs = (
        P(None, "groups"),
        P(("groups", "blk"), "rhs"),
        P(None, ("groups", "blk")),
        P(("groups", "blk", "leaf"), None, None, None),
        P(("groups", "blk", "leaf"), None),
        P("groups", None),
    )
    out_specs = P(("groups", "blk", "leaf"), "rhs")
    return jax.shard_map(
        on_device, mesh=mesh, in_specs=in_specs, out_specs=out_specs, check_vma=False
    )
```

```python
import functools

import jax
import jax.numpy as jnp
from jax import lax
from jax.experimental import pallas as pl
from jax.experimental.pallas import tpu as pltpu
from jax.sharding import PartitionSpec as P

LEAF = 128
BATCH = 12
DEPTH = 48

kernel_scale = 0.0625 / (4.0 * 3.141592653589793)
soften = 0.001
inverse_sq = 1.0 / (kernel_scale * kernel_scale)

bf16 = jnp.bfloat16
f32 = jnp.float32
VMEM = pl.BlockSpec(memory_space=pltpu.VMEM)
HBM = pl.BlockSpec(memory_space=pltpu.HBM)
SMEM = pl.BlockSpec(memory_space=pltpu.SMEM)
PARAMS = pltpu.CompilerParams(vmem_limit_bytes=48 * 2**20)


def cost(microseconds):
    return pl.CostEstimate(flops=int(microseconds * 1e9), bytes_accessed=0, transcendentals=0)


def shifted(block, axis, shift):
    count = lax.axis_size(axis)
    return lax.ppermute(block, axis, [(i, (i + shift) % count) for i in range(count)])


def crossed(block, shift):
    count = lax.axis_size("blk")
    pairs = []
    for i in range(count):
        pairs.append((2 * i, (i + shift) % count * 2))
        pairs.append((2 * i + 1, (i - shift) % count * 2 + 1))
    return lax.ppermute(block, ("blk", "rhs"), pairs)


def cluster(index):
    return pl.ds(pl.multiple_of(index * LEAF, LEAF), LEAF)


def list_kernel(seg_size, near_hbm, basis_hbm, charges_hbm, own_ref, load_ref, near_ref, basis_ref, charges_ref, sems):
    copies = [
        pltpu.make_async_copy(near_hbm, near_ref, sems.at[0]),
        pltpu.make_async_copy(basis_hbm, basis_ref, sems.at[1]),
        pltpu.make_async_copy(charges_hbm, charges_ref, sems.at[2]),
    ]
    for copy in copies:
        copy.start()
    targets, near_count = near_ref.shape
    blk_count = lax.axis_size("blk")
    blk = lax.axis_index("blk")
    before = lax.rem(blk + blk_count - 1, blk_count)
    half = lax.axis_index("rhs")
    columns = charges_ref.shape[0]
    rank = basis_ref.shape[0]
    pack = LEAF // columns
    slots = 4 if near_count <= LEAF // 4 and targets % 4 == 0 else 1
    width = LEAF // slots
    lines = targets // slots

    def iota(shape, dim):
        return lax.broadcasted_iota(jnp.int32, shape, dim)

    def ones(condition):
        return jnp.where(condition, 1.0, 0.0).astype(bf16)

    lane = iota((lines, LEAF), 1)
    target = iota((lines, LEAF), 0) * slots + lane // width
    in_half = target // (targets // 2) == half
    earlier = ones(iota((LEAF, LEAF), 0) < iota((LEAF, LEAF), 1))
    whole = jnp.ones((LEAF, LEAF), bf16)
    above = ones(iota((lines, lines), 1) < iota((lines, lines), 0))
    row = iota((8, LEAF), 0)
    lower = iota((LEAF, LEAF), 0)
    filler = jnp.full((1, width - near_count), -1, jnp.int32)
    for copy in copies:
        copy.wait()
    packed = []
    for line in range(lines):
        pieces = []
        for i in range(slots):
            at = line * slots + i
            pieces += [near_ref[at : at + 1, :], filler]
        packed.append(jnp.concatenate(pieces, axis=1))
    sources = jnp.concatenate(packed, axis=0)
    if seg_size & (seg_size - 1) == 0:
        segment = lax.shift_right_arithmetic(sources, seg_size.bit_length() - 1)
    else:
        segment = lax.div(sources, seg_size)
    local = (sources - segment * seg_size).astype(f32)
    is_own = segment == blk
    is_prev = jnp.logical_and(segment == before, jnp.logical_not(is_own))
    is_next = jnp.logical_and(sources >= 0, jnp.logical_not(jnp.logical_or(is_own, is_prev)))
    is_own = jnp.logical_and(jnp.logical_and(is_own, in_half), sources >= 0)
    is_prev = jnp.logical_and(is_prev, sources >= 0)
    leaving = jnp.where(half == 0, jnp.where(is_next, 1, 0), jnp.where(is_prev, 1, 0))
    masks = (is_own, leaving == 1)
    place = jnp.zeros((lines, LEAF), f32)
    totals, middles = [], []
    for mask in masks:
        within = jnp.dot(ones(mask), earlier, preferred_element_type=f32)
        count = jnp.dot(ones(mask), whole, preferred_element_type=f32)
        start = jnp.dot(above, count.astype(bf16), preferred_element_type=f32)
        place = jnp.where(mask, start + within, place)
        totals.append(start[lines - 1 :, :] + count[lines - 1 :, :])
        middles.append(start[lines // 2 : lines // 2 + 1, :])
    place = place.astype(jnp.int32)
    target = target.astype(f32)
    left, right = [], []
    for line in range(lines):
        at = place[line : line + 1, :]
        here = lax.shift_right_logical(at, 7) == row
        rows = []
        for mask in masks:
            chosen = jnp.logical_and(here, jnp.where(mask[line : line + 1, :], 1, 0) == 1)
            rows.append(jnp.where(chosen, local[line : line + 1, :], 0.0))
            rows.append(jnp.where(chosen, target[line : line + 1, :], 0.0))
        left.append(jnp.concatenate(rows, axis=0).astype(bf16))
        right.append(ones(lax.bitwise_and(at, LEAF - 1) == lower))
    lists = lax.dot_general(
        jnp.concatenate(left, axis=1),
        jnp.concatenate(right, axis=1),
        (((1,), (1,)), ((), ())),
        preferred_element_type=f32,
    )
    last = row * LEAF + iota((8, LEAF), 1) == 8 * LEAF - 1
    own = lists[:8] + 256.0 * lists[8:16]
    own_ref[...] = jnp.where(last, totals[0], own).astype(jnp.int32)
    prior = row * LEAF + iota((8, LEAF), 1) == 8 * LEAF - 2
    length = jnp.where(prior, middles[1], totals[1])
    high = jnp.floor(length * (1.0 / 256.0))
    ends = jnp.logical_or(last, prior)
    away = jnp.concatenate(
        [jnp.where(ends, length - 256.0 * high, lists[16:24]), jnp.where(ends, high, lists[24:32])], axis=0
    )
    rows_end = seg_size // pack * rank
    load_ref[rows_end : rows_end + 16, :] = away.astype(bf16)

    blocks = []
    for group in range(seg_size // pack):
        rows = []
        for i in range(pack):
            at = (group * pack + i) * LEAF
            parts = [jnp.zeros((columns, LEAF), bf16)] * pack
            parts[i] = charges_ref[:, at : at + LEAF]
            rows.append(jnp.concatenate(parts, axis=1))
        at = group * pack * LEAF
        blocks.append(
            lax.dot_general(
                basis_ref[:, at : at + pack * LEAF],
                jnp.concatenate(rows, axis=0),
                (((1,), (1,)), ((), ())),
                preferred_element_type=f32,
            )
        )
    for group, block in enumerate(blocks):
        load_ref[group * rank : (group + 1) * rank, :] = block.astype(bf16)


def split(value):
    high = value.astype(bf16).astype(f32)
    rest = value - high
    middle = rest.astype(bf16).astype(f32)
    return high, middle, rest - middle


def coords_of(points_ref, at):
    block = points_ref[:, cluster(at)]
    zero, one, two = block[0:1, :], block[1:2, :], block[2:3, :]
    return zero, one, two, zero * zero + one * one + two * two


def rows_of(values):
    row = lax.broadcasted_iota(jnp.int32, (8, LEAF), 0)
    out = jnp.zeros((8, LEAF), f32)
    for i, value in enumerate(values):
        out = jnp.where(row == i, value, out)
    return out


def target_features(points_ref, at):
    zero, one, two, norm = coords_of(points_ref, at)
    slope = -2.0 * inverse_sq
    rows = rows_of((zero * slope, one * slope, two * slope, (norm + soften) * inverse_sq, 1.0))
    high, middle, low = split(rows)
    return jnp.concatenate([high, high, middle, middle, high, low], axis=0).astype(bf16)


def source_features(points_ref, at):
    zero, one, two, norm = coords_of(points_ref, at)
    rows = rows_of((zero, one, two, 1.0, norm * inverse_sq))
    high, middle, low = split(rows)
    stacked = jnp.concatenate([high, middle, high, middle, low, high], axis=0)
    return jnp.transpose(stacked).astype(bf16)


def feature_kernel(seg_size, targets, points_ref, target_ref, source_ref):
    blk_count = lax.axis_size("blk")
    blk = lax.axis_index("blk")
    first = lax.axis_index("leaf") * targets
    away = lax.rem(blk + 2 * lax.axis_index("rhs") + blk_count - 1, blk_count)
    for which, segment in enumerate((away, blk)):
        for i in range(targets):
            target_ref[which * targets + i] = target_features(points_ref, segment * seg_size + first + i)
    target_ref[2 * targets] = jnp.zeros((DEPTH, LEAF), bf16)

    def some_sources(step, carry):
        for u in range(8):
            at = step * 8 + u
            source_ref[at] = source_features(points_ref, blk * seg_size + at)
        return carry

    lax.fori_loop(0, seg_size // 8, some_sources, 0)


def near_kernel(base, part, list_ref, target_ref, source_ref, mine_ref, other_ref, out_ref, total, even, odd):
    targets = total.shape[0] - 1
    blank = target_ref.shape[0] - 1
    skipped = targets if part == 1 else 0
    begin = list_ref[7, LEAF - 2] if part == 1 else 0
    end = list_ref[7, LEAF - 2] if part == 0 else list_ref[7, LEAF - 1]
    batches = lax.div(end - begin + (BATCH - 1), BATCH)
    total[...] = jnp.zeros_like(total)

    def pair(batch, u):
        at = begin + batch * BATCH + u
        code = list_ref[lax.shift_right_logical(at, 7), lax.bitwise_and(at, 127)]
        code = jnp.where(at < end, code, (skipped + targets) * 256)
        return lax.shift_right_logical(code, 8), lax.bitwise_and(code, 255)

    def make(batch, slot):
        for u in range(BATCH):
            target, source = pair(batch, u)
            square = jnp.dot(source_ref[source], target_ref[jnp.minimum(base + target, blank)], preferred_element_type=f32)
            slot[u] = lax.rsqrt(square).astype(bf16)

    def use(batch, slot):
        sums = []
        for u in range(BATCH):
            target, source = pair(batch, u)
            charges = jnp.concatenate([mine_ref[:, cluster(source)], other_ref[:, cluster(source)]], axis=0)
            sums.append((target, jnp.dot(charges, slot[u], preferred_element_type=f32)))
        for target, value in sums:
            total[target - skipped] += value

    make(0, even)

    def body(step, carry):
        make(2 * step + 1, odd)
        use(2 * step, even)
        make(2 * step + 2, even)
        use(2 * step + 1, odd)
        return carry

    lax.fori_loop(0, lax.div(batches, 2), body, 0)

    @pl.when(lax.rem(batches, 2) == 1)
    def _():
        use(batches - 1, even)

    for i in range(targets):
        out_ref[:, i * LEAF : (i + 1) * LEAF] = total[i].astype(out_ref.dtype)


def near_sum(base, part, microseconds, targets, pairs, target_rows, source_rows, mine, other, dtype):
    columns = 2 * mine.shape[0]
    return pl.pallas_call(
        functools.partial(near_kernel, base, part),
        out_shape=jax.ShapeDtypeStruct((columns, targets * LEAF), dtype),
        in_specs=[SMEM] + [VMEM] * 4,
        out_specs=VMEM,
        scratch_shapes=[
            pltpu.VMEM((targets + 1, columns, LEAF), f32),
            pltpu.VMEM((BATCH, LEAF, LEAF), bf16),
            pltpu.VMEM((BATCH, LEAF, LEAF), bf16),
        ],
        compiler_params=PARAMS,
        cost_estimate=cost(microseconds),
    )(pairs, target_rows, source_rows, mine, other)


def far_sum(out_ref, basis_ref, target, at, coefficient):
    out_ref[:, target * LEAF : (target + 1) * LEAF] = lax.dot_general(
        coefficient.astype(bf16),
        basis_ref[:, cluster(at)],
        (((0,), (0,)), ((), ())),
        preferred_element_type=f32,
    )


def far_kernel(seg_size, far_ref, couplings_ref, basis_ref, part, out_ref, skel):
    leaf = lax.axis_index("leaf") * couplings_ref.shape[0]
    clusters, far_count, rank, _ = couplings_ref.shape
    columns = out_ref.shape[0]
    pack = LEAF // columns

    def unpack(group, carry):
        block = part[pl.ds(pl.multiple_of(group * rank, rank), rank), :]
        for i in range(pack):
            skel[group * pack + i] = block[:, i * columns : (i + 1) * columns]
        return carry

    lax.fori_loop(0, part.shape[0] // rank, unpack, 0)
    for target in range(clusters):
        coefficient = jnp.zeros((rank, columns), f32)
        step = 256 // rank
        for at in range(0, far_count, step):
            left = jnp.concatenate([couplings_ref[target, at + i] for i in range(step)], axis=1)
            rows = [skel[far_ref[target, at + i]] for i in range(step)]
            coefficient = coefficient + jnp.dot(
                left, jnp.concatenate(rows, axis=0), preferred_element_type=f32
            )
        far_sum(out_ref, basis_ref, target, leaf + target, coefficient)


def far_kernel_phased(seg_size, far_ref, couplings_ref, basis_ref, *refs):
    parts, (out_ref, skel, side, held) = refs[:-4], refs[-4:]
    clusters, far_count, rank, _ = couplings_ref.shape
    columns = out_ref.shape[0]
    pack = LEAF // columns
    leaf = lax.axis_index("leaf") * clusters
    for target in range(clusters):
        for at in range(0, far_count, pack):
            side[target, :, at * rank : (at + pack) * rank] = jnp.concatenate(
                [couplings_ref[target, at + i] for i in range(pack)], axis=1
            )
    for order, part in enumerate(parts):
        for group in range(seg_size // pack):
            block = part[group * rank : (group + 1) * rank, :]
            for i in range(pack):
                skel[order * seg_size + group * pack + i] = block[:, i * columns : (i + 1) * columns]
    step = 256 // rank
    for target in range(clusters):
        coefficient = jnp.zeros((rank, columns), f32)
        for at in range(0, far_count, step):
            rows = [skel[far_ref[target, at + i]] for i in range(step)]
            coefficient = coefficient + jnp.dot(
                side[target, :, at * rank : (at + step) * rank],
                jnp.concatenate(rows, axis=0),
                preferred_element_type=f32,
            )
        held[target] = coefficient.astype(bf16)
    for target in range(clusters):
        far_sum(out_ref, basis_ref, target, leaf + target, held[target])


def on_device(points, charges, basis, couplings, near_src, far_src):
    blk_count = lax.axis_size("blk")
    mine = charges.T
    columns, seg_rows = mine.shape
    seg_size = seg_rows // LEAF
    rank = basis.shape[0]
    own_clusters, near_count = near_src.shape
    cluster_total = seg_size * blk_count
    pack = LEAF // columns
    skel_rows = seg_size // pack * rank
    other = shifted(mine, "rhs", 1)
    own_list, load = pl.pallas_call(
        functools.partial(list_kernel, seg_size),
        out_shape=[
            jax.ShapeDtypeStruct((8, LEAF), jnp.int32),
            jax.ShapeDtypeStruct((skel_rows + 16, LEAF), bf16),
        ],
        in_specs=[HBM] * 3,
        out_specs=[VMEM] * 2,
        scratch_shapes=[
            pltpu.VMEM(near_src.shape, jnp.int32),
            pltpu.VMEM(basis.shape, bf16),
            pltpu.VMEM(mine.shape, bf16),
            pltpu.SemaphoreType.DMA((3,)),
        ],
        compiler_params=pltpu.CompilerParams(vmem_limit_bytes=63 * 2**20),
        cost_estimate=cost(3.0),
    )(near_src, basis, mine)

    points, load = lax.optimization_barrier((points, load))
    first_load = crossed(load, 1)
    target_rows, source_rows = pl.pallas_call(
        functools.partial(feature_kernel, seg_size, own_clusters),
        out_shape=[
            jax.ShapeDtypeStruct((2 * own_clusters + 1, DEPTH, LEAF), bf16),
            jax.ShapeDtypeStruct((seg_size, LEAF, DEPTH), bf16),
        ],
        in_specs=[VMEM],
        out_specs=[VMEM, VMEM],
        compiler_params=PARAMS,
        cost_estimate=cost(0.7),
    )(points)
    target_rows, later_load = lax.optimization_barrier((target_rows, load))
    narrow = blk_count == 4 and cluster_total <= 256
    if narrow:
        loads = [load, crossed(later_load, -1), shifted(later_load, "blk", 2), first_load]
    else:
        loads = [lax.all_gather(later_load[:skel_rows], "blk", axis=0, tiled=True)]
    args = (target_rows, source_rows, mine, other)
    codes = first_load[skel_rows:].astype(jnp.int32)
    pairs = codes[:8] + 256 * codes[8:]
    low = near_sum(0, 0, 20.0, own_clusters // 2, pairs, *args, bf16)
    low, pairs = lax.optimization_barrier((low, pairs))
    low_back = crossed(low, -1)
    high = near_sum(0, 1, 20.0, own_clusters // 2, pairs, *args, bf16)
    high, own_list = lax.optimization_barrier((high, own_list))
    high_back = crossed(high, -1)
    own_near = near_sum(own_clusters, None, 0.5, own_clusters, own_list, *args, f32)
    own_near, loads, low_back = lax.optimization_barrier((own_near, loads, low_back))

    blk = lax.axis_index("blk")
    first = blk * seg_size + lax.axis_index("leaf") * own_clusters
    entries = lax.dynamic_slice_in_dim(far_src, first, own_clusters, 0)
    far_shape = jax.ShapeDtypeStruct((columns, own_clusters * LEAF), f32)
    if narrow:
        segment = lax.div(entries, seg_size)
        ahead = jnp.where(lax.axis_index("rhs") == 0, segment - blk, blk - segment)
        order = lax.rem(ahead + blk_count, blk_count)
        entries = entries + (order - segment) * seg_size
        far = pl.pallas_call(
            functools.partial(far_kernel_phased, seg_size),
            out_shape=far_shape,
            in_specs=[SMEM] + [VMEM] * 6,
            out_specs=VMEM,
            scratch_shapes=[
                pltpu.VMEM((cluster_total, rank, columns), bf16),
                pltpu.VMEM((own_clusters, rank, far_src.shape[1] * rank), bf16),
                pltpu.VMEM((own_clusters, rank, columns), bf16),
            ],
            compiler_params=PARAMS,
            cost_estimate=cost(20.0),
        )(entries, couplings, basis, *loads)
    else:
        far = pl.pallas_call(
            functools.partial(far_kernel, seg_size),
            out_shape=far_shape,
            in_specs=[SMEM] + [VMEM] * 3,
            out_specs=VMEM,
            scratch_shapes=[pltpu.VMEM((cluster_total, rank, columns), bf16)],
            compiler_params=PARAMS,
        )(entries, couplings, basis, *loads)

    far, low_back, high_back = lax.optimization_barrier((far, low_back, high_back))
    near = own_near + jnp.concatenate([low_back, high_back], axis=1).astype(f32)
    got = shifted(near[columns:].astype(bf16), "rhs", 1)
    return (near[:columns] + got.astype(f32) + far).astype(bf16).T


def solution(mesh):
    in_specs = (
        P(None, "groups"),
        P(("groups", "blk"), "rhs"),
        P(None, ("groups", "blk")),
        P(("groups", "blk", "leaf"), None, None, None),
        P(("groups", "blk", "leaf"), None),
        P("groups", None),
    )
    out_specs = P(("groups", "blk", "leaf"), "rhs")
    return jax.shard_map(
        on_device, mesh=mesh, in_specs=in_specs, out_specs=out_specs, check_vma=False
    )
```

```python
import functools

import jax
import jax.numpy as jnp
from jax import lax
from jax.experimental import pallas as pl
from jax.experimental.pallas import tpu as pltpu
from jax.sharding import PartitionSpec as P

LEAF = 128
BATCH = 12
DEPTH = 48

kernel_scale = 0.0625 / (4.0 * 3.141592653589793)
soften = 0.001
inverse_sq = 1.0 / (kernel_scale * kernel_scale)

bf16 = jnp.bfloat16
f32 = jnp.float32
VMEM = pl.BlockSpec(memory_space=pltpu.VMEM)
HBM = pl.BlockSpec(memory_space=pltpu.HBM)
SMEM = pl.BlockSpec(memory_space=pltpu.SMEM)
PARAMS = pltpu.CompilerParams(vmem_limit_bytes=48 * 2**20)


def cost(microseconds):
    return pl.CostEstimate(flops=int(microseconds * 1e9), bytes_accessed=0, transcendentals=0)


def shifted(block, axis, shift):
    count = lax.axis_size(axis)
    return lax.ppermute(block, axis, [(i, (i + shift) % count) for i in range(count)])


def crossed(block, shift):
    count = lax.axis_size("blk")
    pairs = []
    for i in range(count):
        pairs.append((2 * i, (i + shift) % count * 2))
        pairs.append((2 * i + 1, (i - shift) % count * 2 + 1))
    return lax.ppermute(block, ("blk", "rhs"), pairs)


def cluster(index):
    return pl.ds(pl.multiple_of(index * LEAF, LEAF), LEAF)


def list_kernel(seg_size, near_hbm, basis_hbm, charges_hbm, own_ref, load_ref, near_ref, basis_ref, charges_ref, sems):
    copies = [
        pltpu.make_async_copy(near_hbm, near_ref, sems.at[0]),
        pltpu.make_async_copy(basis_hbm, basis_ref, sems.at[1]),
        pltpu.make_async_copy(charges_hbm, charges_ref, sems.at[2]),
    ]
    for copy in copies:
        copy.start()
    targets, near_count = near_ref.shape
    blk_count = lax.axis_size("blk")
    blk = lax.axis_index("blk")
    before = lax.rem(blk + blk_count - 1, blk_count)
    half = lax.axis_index("rhs")
    columns = charges_ref.shape[0]
    rank = basis_ref.shape[0]
    pack = LEAF // columns
    slots = 4 if near_count <= LEAF // 4 and targets % 4 == 0 else 1
    width = LEAF // slots
    lines = targets // slots

    def iota(shape, dim):
        return lax.broadcasted_iota(jnp.int32, shape, dim)

    def ones(condition):
        return jnp.where(condition, 1.0, 0.0).astype(bf16)

    lane = iota((lines, LEAF), 1)
    target = iota((lines, LEAF), 0) * slots + lane // width
    in_half = target // (targets // 2) == half
    earlier = ones(iota((LEAF, LEAF), 0) < iota((LEAF, LEAF), 1))
    whole = jnp.ones((LEAF, LEAF), bf16)
    above = ones(iota((lines, lines), 1) < iota((lines, lines), 0))
    row = iota((8, LEAF), 0)
    lower = iota((LEAF, LEAF), 0)
    filler = jnp.full((1, width - near_count), -1, jnp.int32)
    for copy in copies:
        copy.wait()
    packed = []
    for line in range(lines):
        pieces = []
        for i in range(slots):
            at = line * slots + i
            pieces += [near_ref[at : at + 1, :], filler]
        packed.append(jnp.concatenate(pieces, axis=1))
    sources = jnp.concatenate(packed, axis=0)
    if seg_size & (seg_size - 1) == 0:
        segment = lax.shift_right_arithmetic(sources, seg_size.bit_length() - 1)
    else:
        segment = lax.div(sources, seg_size)
    local = (sources - segment * seg_size).astype(f32)
    is_own = segment == blk
    is_prev = jnp.logical_and(segment == before, jnp.logical_not(is_own))
    is_next = jnp.logical_and(sources >= 0, jnp.logical_not(jnp.logical_or(is_own, is_prev)))
    is_own = jnp.logical_and(jnp.logical_and(is_own, in_half), sources >= 0)
    is_prev = jnp.logical_and(is_prev, sources >= 0)
    leaving = jnp.where(half == 0, jnp.where(is_next, 1, 0), jnp.where(is_prev, 1, 0))
    masks = (is_own, leaving == 1)
    place = jnp.zeros((lines, LEAF), f32)
    totals, middles = [], []
    for mask in masks:
        within = jnp.dot(ones(mask), earlier, preferred_element_type=f32)
        count = jnp.dot(ones(mask), whole, preferred_element_type=f32)
        start = jnp.dot(above, count.astype(bf16), preferred_element_type=f32)
        place = jnp.where(mask, start + within, place)
        totals.append(start[lines - 1 :, :] + count[lines - 1 :, :])
        middles.append(start[lines // 2 : lines // 2 + 1, :])
    place = place.astype(jnp.int32)
    target = target.astype(f32)
    left, right = [], []
    for line in range(lines):
        at = place[line : line + 1, :]
        here = lax.shift_right_logical(at, 7) == row
        rows = []
        for mask in masks:
            chosen = jnp.logical_and(here, jnp.where(mask[line : line + 1, :], 1, 0) == 1)
            rows.append(jnp.where(chosen, local[line : line + 1, :], 0.0))
            rows.append(jnp.where(chosen, target[line : line + 1, :], 0.0))
        left.append(jnp.concatenate(rows, axis=0).astype(bf16))
        right.append(ones(lax.bitwise_and(at, LEAF - 1) == lower))
    lists = lax.dot_general(
        jnp.concatenate(left, axis=1),
        jnp.concatenate(right, axis=1),
        (((1,), (1,)), ((), ())),
        preferred_element_type=f32,
    )
    last = row * LEAF + iota((8, LEAF), 1) == 8 * LEAF - 1
    own = lists[:8] + 256.0 * lists[8:16]
    own_ref[...] = jnp.where(last, totals[0], own).astype(jnp.int32)
    prior = row * LEAF + iota((8, LEAF), 1) == 8 * LEAF - 2
    length = jnp.where(prior, middles[1], totals[1])
    high = jnp.floor(length * (1.0 / 256.0))
    ends = jnp.logical_or(last, prior)
    away = jnp.concatenate(
        [jnp.where(ends, length - 256.0 * high, lists[16:24]), jnp.where(ends, high, lists[24:32])], axis=0
    )
    rows_end = seg_size // pack * rank
    load_ref[rows_end : rows_end + 16, :] = away.astype(bf16)

    blocks = []
    for group in range(seg_size // pack):
        rows = []
        for i in range(pack):
            at = (group * pack + i) * LEAF
            parts = [jnp.zeros((columns, LEAF), bf16)] * pack
            parts[i] = charges_ref[:, at : at + LEAF]
            rows.append(jnp.concatenate(parts, axis=1))
        at = group * pack * LEAF
        blocks.append(
            lax.dot_general(
                basis_ref[:, at : at + pack * LEAF],
                jnp.concatenate(rows, axis=0),
                (((1,), (1,)), ((), ())),
                preferred_element_type=f32,
            )
        )
    for group, block in enumerate(blocks):
        load_ref[group * rank : (group + 1) * rank, :] = block.astype(bf16)


def split(value):
    high = value.astype(bf16).astype(f32)
    rest = value - high
    middle = rest.astype(bf16).astype(f32)
    return high, middle, rest - middle


def coords_of(points_ref, at):
    block = points_ref[:, cluster(at)]
    zero, one, two = block[0:1, :], block[1:2, :], block[2:3, :]
    return zero, one, two, zero * zero + one * one + two * two


def rows_of(values):
    row = lax.broadcasted_iota(jnp.int32, (8, LEAF), 0)
    out = jnp.zeros((8, LEAF), f32)
    for i, value in enumerate(values):
        out = jnp.where(row == i, value, out)
    return out


def target_features(points_ref, at):
    zero, one, two, norm = coords_of(points_ref, at)
    slope = -2.0 * inverse_sq
    rows = rows_of((zero * slope, one * slope, two * slope, (norm + soften) * inverse_sq, 1.0))
    high, middle, low = split(rows)
    return jnp.concatenate([high, high, middle, middle, high, low], axis=0).astype(bf16)


def source_features(points_ref, at):
    zero, one, two, norm = coords_of(points_ref, at)
    rows = rows_of((zero, one, two, 1.0, norm * inverse_sq))
    high, middle, low = split(rows)
    stacked = jnp.concatenate([high, middle, high, middle, low, high], axis=0)
    return jnp.transpose(stacked).astype(bf16)


def feature_kernel(seg_size, targets, points_ref, target_ref, source_ref):
    blk_count = lax.axis_size("blk")
    blk = lax.axis_index("blk")
    first = lax.axis_index("leaf") * targets
    away = lax.rem(blk + 2 * lax.axis_index("rhs") + blk_count - 1, blk_count)
    for which, segment in enumerate((away, blk)):
        for i in range(targets):
            target_ref[which * targets + i] = target_features(points_ref, segment * seg_size + first + i)
    target_ref[2 * targets] = jnp.zeros((DEPTH, LEAF), bf16)

    def some_sources(step, carry):
        for u in range(8):
            at = step * 8 + u
            source_ref[at] = source_features(points_ref, blk * seg_size + at)
        return carry

    lax.fori_loop(0, seg_size // 8, some_sources, 0)


def near_kernel(base, part, list_ref, target_ref, source_ref, mine_ref, other_ref, out_ref, total, even, odd):
    targets = total.shape[0] - 1
    blank = target_ref.shape[0] - 1
    skipped = targets if part == 1 else 0
    begin = list_ref[7, LEAF - 2] if part == 1 else 0
    end = list_ref[7, LEAF - 2] if part == 0 else list_ref[7, LEAF - 1]
    batches = lax.div(end - begin + (BATCH - 1), BATCH)
    total[...] = jnp.zeros_like(total)

    def pair(batch, u):
        at = begin + batch * BATCH + u
        code = list_ref[lax.shift_right_logical(at, 7), lax.bitwise_and(at, 127)]
        code = jnp.where(at < end, code, (skipped + targets) * 256)
        return lax.shift_right_logical(code, 8), lax.bitwise_and(code, 255)

    def make(batch, slot):
        for u in range(BATCH):
            target, source = pair(batch, u)
            square = jnp.dot(source_ref[source], target_ref[jnp.minimum(base + target, blank)], preferred_element_type=f32)
            slot[u] = lax.rsqrt(square).astype(bf16)

    def use(batch, slot):
        sums = []
        for u in range(BATCH):
            target, source = pair(batch, u)
            charges = jnp.concatenate([mine_ref[:, cluster(source)], other_ref[:, cluster(source)]], axis=0)
            sums.append((target, jnp.dot(charges, slot[u], preferred_element_type=f32)))
        for target, value in sums:
            total[target - skipped] += value

    make(0, even)

    def body(step, carry):
        make(2 * step + 1, odd)
        use(2 * step, even)
        make(2 * step + 2, even)
        use(2 * step + 1, odd)
        return carry

    lax.fori_loop(0, lax.div(batches, 2), body, 0)

    @pl.when(lax.rem(batches, 2) == 1)
    def _():
        use(batches - 1, even)

    for i in range(targets):
        out_ref[:, i * LEAF : (i + 1) * LEAF] = total[i].astype(out_ref.dtype)


def near_sum(base, part, microseconds, targets, pairs, target_rows, source_rows, mine, other, dtype):
    columns = 2 * mine.shape[0]
    return pl.pallas_call(
        functools.partial(near_kernel, base, part),
        out_shape=jax.ShapeDtypeStruct((columns, targets * LEAF), dtype),
        in_specs=[SMEM] + [VMEM] * 4,
        out_specs=VMEM,
        scratch_shapes=[
            pltpu.VMEM((targets + 1, columns, LEAF), f32),
            pltpu.VMEM((BATCH, LEAF, LEAF), bf16),
            pltpu.VMEM((BATCH, LEAF, LEAF), bf16),
        ],
        compiler_params=PARAMS,
        cost_estimate=cost(microseconds),
    )(pairs, target_rows, source_rows, mine, other)


def far_sum(out_ref, basis_ref, target, at, coefficient):
    out_ref[:, target * LEAF : (target + 1) * LEAF] = lax.dot_general(
        coefficient.astype(bf16),
        basis_ref[:, cluster(at)],
        (((0,), (0,)), ((), ())),
        preferred_element_type=f32,
    )


def far_kernel(seg_size, far_ref, couplings_ref, basis_ref, part, out_ref, skel):
    leaf = lax.axis_index("leaf") * couplings_ref.shape[0]
    clusters, far_count, rank, _ = couplings_ref.shape
    columns = out_ref.shape[0]
    pack = LEAF // columns

    def unpack(group, carry):
        block = part[pl.ds(pl.multiple_of(group * rank, rank), rank), :]
        for i in range(pack):
            skel[group * pack + i] = block[:, i * columns : (i + 1) * columns]
        return carry

    lax.fori_loop(0, part.shape[0] // rank, unpack, 0)
    for target in range(clusters):
        coefficient = jnp.zeros((rank, columns), f32)
        step = 256 // rank
        for at in range(0, far_count, step):
            left = jnp.concatenate([couplings_ref[target, at + i] for i in range(step)], axis=1)
            rows = [skel[far_ref[target, at + i]] for i in range(step)]
            coefficient = coefficient + jnp.dot(
                left, jnp.concatenate(rows, axis=0), preferred_element_type=f32
            )
        far_sum(out_ref, basis_ref, target, leaf + target, coefficient)


def far_kernel_phased(seg_size, far_ref, couplings_ref, basis_ref, *refs):
    parts, (out_ref, skel, side, held) = refs[:-4], refs[-4:]
    clusters, far_count, rank, _ = couplings_ref.shape
    columns = out_ref.shape[0]
    pack = LEAF // columns
    leaf = lax.axis_index("leaf") * clusters
    for target in range(clusters):
        for at in range(0, far_count, pack):
            side[target, :, at * rank : (at + pack) * rank] = jnp.concatenate(
                [couplings_ref[target, at + i] for i in range(pack)], axis=1
            )
    for order, part in enumerate(parts):
        for group in range(seg_size // pack):
            block = part[group * rank : (group + 1) * rank, :]
            for i in range(pack):
                skel[order * seg_size + group * pack + i] = block[:, i * columns : (i + 1) * columns]
    step = 256 // rank
    for target in range(clusters):
        coefficient = jnp.zeros((rank, columns), f32)
        for at in range(0, far_count, step):
            rows = [skel[far_ref[target, at + i]] for i in range(step)]
            coefficient = coefficient + jnp.dot(
                side[target, :, at * rank : (at + step) * rank],
                jnp.concatenate(rows, axis=0),
                preferred_element_type=f32,
            )
        held[target] = coefficient.astype(bf16)
    for target in range(clusters):
        far_sum(out_ref, basis_ref, target, leaf + target, held[target])


def on_device(points, charges, basis, couplings, near_src, far_src):
    blk_count = lax.axis_size("blk")
    mine = charges.T
    columns, seg_rows = mine.shape
    seg_size = seg_rows // LEAF
    rank = basis.shape[0]
    own_clusters, near_count = near_src.shape
    cluster_total = seg_size * blk_count
    pack = LEAF // columns
    skel_rows = seg_size // pack * rank
    other = shifted(mine, "rhs", 1)
    own_list, load = pl.pallas_call(
        functools.partial(list_kernel, seg_size),
        out_shape=[
            jax.ShapeDtypeStruct((8, LEAF), jnp.int32),
            jax.ShapeDtypeStruct((skel_rows + 16, LEAF), bf16),
        ],
        in_specs=[HBM] * 3,
        out_specs=[VMEM] * 2,
        scratch_shapes=[
            pltpu.VMEM(near_src.shape, jnp.int32),
            pltpu.VMEM(basis.shape, bf16),
            pltpu.VMEM(mine.shape, bf16),
            pltpu.SemaphoreType.DMA((3,)),
        ],
        compiler_params=pltpu.CompilerParams(vmem_limit_bytes=63 * 2**20),
        cost_estimate=cost(3.0),
    )(near_src, basis, mine)

    points, load = lax.optimization_barrier((points, load))
    first_load = crossed(load, 1)
    target_rows, source_rows = pl.pallas_call(
        functools.partial(feature_kernel, seg_size, own_clusters),
        out_shape=[
            jax.ShapeDtypeStruct((2 * own_clusters + 1, DEPTH, LEAF), bf16),
            jax.ShapeDtypeStruct((seg_size, LEAF, DEPTH), bf16),
        ],
        in_specs=[VMEM],
        out_specs=[VMEM, VMEM],
        compiler_params=PARAMS,
        cost_estimate=cost(0.7),
    )(points)
    args = (target_rows, source_rows, mine, other)
    own_near = near_sum(own_clusters, None, 2.6, own_clusters, own_list, *args, f32)
    own_near, first_load = lax.optimization_barrier((own_near, first_load))
    codes = first_load[skel_rows:].astype(jnp.int32)
    pairs = codes[:8] + 256 * codes[8:]
    low = near_sum(0, 0, 20.0, own_clusters // 2, pairs, *args, bf16)
    low, pairs, later_load = lax.optimization_barrier((low, pairs, load))
    low_back = crossed(low, -1)
    narrow = blk_count == 4 and cluster_total <= 256
    if narrow:
        loads = [load, crossed(later_load, -1), shifted(later_load, "blk", 2), first_load]
    else:
        loads = [lax.all_gather(later_load[:skel_rows], "blk", axis=0, tiled=True)]
    high = near_sum(0, 1, 20.0, own_clusters // 2, pairs, *args, bf16)
    high_back = crossed(high, -1)
    _, loads, low_back = lax.optimization_barrier((high, loads, low_back))

    blk = lax.axis_index("blk")
    first = blk * seg_size + lax.axis_index("leaf") * own_clusters
    entries = lax.dynamic_slice_in_dim(far_src, first, own_clusters, 0)
    far_shape = jax.ShapeDtypeStruct((columns, own_clusters * LEAF), f32)
    if narrow:
        segment = lax.div(entries, seg_size)
        ahead = jnp.where(lax.axis_index("rhs") == 0, segment - blk, blk - segment)
        order = lax.rem(ahead + blk_count, blk_count)
        entries = entries + (order - segment) * seg_size
        far = pl.pallas_call(
            functools.partial(far_kernel_phased, seg_size),
            out_shape=far_shape,
            in_specs=[SMEM] + [VMEM] * 6,
            out_specs=VMEM,
            scratch_shapes=[
                pltpu.VMEM((cluster_total, rank, columns), bf16),
                pltpu.VMEM((own_clusters, rank, far_src.shape[1] * rank), bf16),
                pltpu.VMEM((own_clusters, rank, columns), bf16),
            ],
            compiler_params=PARAMS,
            cost_estimate=cost(20.0),
        )(entries, couplings, basis, *loads)
    else:
        far = pl.pallas_call(
            functools.partial(far_kernel, seg_size),
            out_shape=far_shape,
            in_specs=[SMEM] + [VMEM] * 3,
            out_specs=VMEM,
            scratch_shapes=[pltpu.VMEM((cluster_total, rank, columns), bf16)],
            compiler_params=PARAMS,
        )(entries, couplings, basis, *loads)

    far, low_back, high_back = lax.optimization_barrier((far, low_back, high_back))
    near = own_near + jnp.concatenate([low_back, high_back], axis=1).astype(f32)
    got = shifted(near[columns:].astype(bf16), "rhs", 1)
    return (near[:columns] + got.astype(f32) + far).astype(bf16).T


def solution(mesh):
    in_specs = (
        P(None, "groups"),
        P(("groups", "blk"), "rhs"),
        P(None, ("groups", "blk")),
        P(("groups", "blk", "leaf"), None, None, None),
        P(("groups", "blk", "leaf"), None),
        P("groups", None),
    )
    out_specs = P(("groups", "blk", "leaf"), "rhs")
    return jax.shard_map(
        on_device, mesh=mesh, in_specs=in_specs, out_specs=out_specs, check_vma=False
    )
```

```python
import functools

import jax
import jax.numpy as jnp
from jax import lax
from jax.experimental import pallas as pl
from jax.experimental.pallas import tpu as pltpu
from jax.sharding import PartitionSpec as P

LEAF = 128
BATCH = 12
DEPTH = 48

kernel_scale = 0.0625 / (4.0 * 3.141592653589793)
soften = 0.001
inverse_sq = 1.0 / (kernel_scale * kernel_scale)

bf16 = jnp.bfloat16
f32 = jnp.float32
VMEM = pl.BlockSpec(memory_space=pltpu.VMEM)
HBM = pl.BlockSpec(memory_space=pltpu.HBM)
SMEM = pl.BlockSpec(memory_space=pltpu.SMEM)
PARAMS = pltpu.CompilerParams(vmem_limit_bytes=48 * 2**20)


def cost(microseconds):
    return pl.CostEstimate(flops=int(microseconds * 1e9), bytes_accessed=0, transcendentals=0)


def shifted(block, axis, shift):
    count = lax.axis_size(axis)
    return lax.ppermute(block, axis, [(i, (i + shift) % count) for i in range(count)])


def crossed(block, shift):
    count = lax.axis_size("blk")
    pairs = []
    for i in range(count):
        pairs.append((2 * i, (i + shift) % count * 2))
        pairs.append((2 * i + 1, (i - shift) % count * 2 + 1))
    return lax.ppermute(block, ("blk", "rhs"), pairs)


def cluster(index):
    return pl.ds(pl.multiple_of(index * LEAF, LEAF), LEAF)


def list_kernel(seg_size, near_hbm, basis_hbm, charges_hbm, own_ref, load_ref, near_ref, basis_ref, charges_ref, sems):
    copies = [
        pltpu.make_async_copy(near_hbm, near_ref, sems.at[0]),
        pltpu.make_async_copy(basis_hbm, basis_ref, sems.at[1]),
        pltpu.make_async_copy(charges_hbm, charges_ref, sems.at[2]),
    ]
    for copy in copies:
        copy.start()
    targets, near_count = near_ref.shape
    blk_count = lax.axis_size("blk")
    blk = lax.axis_index("blk")
    before = lax.rem(blk + blk_count - 1, blk_count)
    half = lax.axis_index("rhs")
    columns = charges_ref.shape[0]
    rank = basis_ref.shape[0]
    pack = LEAF // columns
    slots = 4 if near_count <= LEAF // 4 and targets % 4 == 0 else 1
    width = LEAF // slots
    lines = targets // slots

    def iota(shape, dim):
        return lax.broadcasted_iota(jnp.int32, shape, dim)

    def ones(condition):
        return jnp.where(condition, 1.0, 0.0).astype(bf16)

    lane = iota((lines, LEAF), 1)
    target = iota((lines, LEAF), 0) * slots + lane // width
    in_half = target // (targets // 2) == half
    earlier = ones(iota((LEAF, LEAF), 0) < iota((LEAF, LEAF), 1))
    whole = jnp.ones((LEAF, LEAF), bf16)
    above = ones(iota((lines, lines), 1) < iota((lines, lines), 0))
    row = iota((8, LEAF), 0)
    lower = iota((LEAF, LEAF), 0)
    filler = jnp.full((1, width - near_count), -1, jnp.int32)
    for copy in copies:
        copy.wait()
    packed = []
    for line in range(lines):
        pieces = []
        for i in range(slots):
            at = line * slots + i
            pieces += [near_ref[at : at + 1, :], filler]
        packed.append(jnp.concatenate(pieces, axis=1))
    sources = jnp.concatenate(packed, axis=0)
    if seg_size & (seg_size - 1) == 0:
        segment = lax.shift_right_arithmetic(sources, seg_size.bit_length() - 1)
    else:
        segment = lax.div(sources, seg_size)
    local = (sources - segment * seg_size).astype(f32)
    is_own = segment == blk
    is_prev = jnp.logical_and(segment == before, jnp.logical_not(is_own))
    is_next = jnp.logical_and(sources >= 0, jnp.logical_not(jnp.logical_or(is_own, is_prev)))
    is_own = jnp.logical_and(jnp.logical_and(is_own, in_half), sources >= 0)
    is_prev = jnp.logical_and(is_prev, sources >= 0)
    leaving = jnp.where(half == 0, jnp.where(is_next, 1, 0), jnp.where(is_prev, 1, 0))
    masks = (is_own, leaving == 1)
    place = jnp.zeros((lines, LEAF), f32)
    totals, middles = [], []
    for mask in masks:
        within = jnp.dot(ones(mask), earlier, preferred_element_type=f32)
        count = jnp.dot(ones(mask), whole, preferred_element_type=f32)
        start = jnp.dot(above, count.astype(bf16), preferred_element_type=f32)
        place = jnp.where(mask, start + within, place)
        totals.append(start[lines - 1 :, :] + count[lines - 1 :, :])
        middles.append(start[lines // 2 : lines // 2 + 1, :])
    place = place.astype(jnp.int32)
    target = target.astype(f32)
    left, right = [], []
    for line in range(lines):
        at = place[line : line + 1, :]
        here = lax.shift_right_logical(at, 7) == row
        rows = []
        for mask in masks:
            chosen = jnp.logical_and(here, jnp.where(mask[line : line + 1, :], 1, 0) == 1)
            rows.append(jnp.where(chosen, local[line : line + 1, :], 0.0))
            rows.append(jnp.where(chosen, target[line : line + 1, :], 0.0))
        left.append(jnp.concatenate(rows, axis=0).astype(bf16))
        right.append(ones(lax.bitwise_and(at, LEAF - 1) == lower))
    lists = lax.dot_general(
        jnp.concatenate(left, axis=1),
        jnp.concatenate(right, axis=1),
        (((1,), (1,)), ((), ())),
        preferred_element_type=f32,
    )
    last = row * LEAF + iota((8, LEAF), 1) == 8 * LEAF - 1
    own = lists[:8] + 256.0 * lists[8:16]
    own_ref[...] = jnp.where(last, totals[0], own).astype(jnp.int32)
    prior = row * LEAF + iota((8, LEAF), 1) == 8 * LEAF - 2
    length = jnp.where(prior, middles[1], totals[1])
    high = jnp.floor(length * (1.0 / 256.0))
    ends = jnp.logical_or(last, prior)
    away = jnp.concatenate(
        [jnp.where(ends, length - 256.0 * high, lists[16:24]), jnp.where(ends, high, lists[24:32])], axis=0
    )
    rows_end = seg_size // pack * rank
    load_ref[rows_end : rows_end + 16, :] = away.astype(bf16)

    singles = []
    for index in range(seg_size):
        at = index * LEAF
        singles.append(
            lax.dot_general(
                basis_ref[:, at : at + LEAF],
                charges_ref[:, at : at + LEAF],
                (((1,), (1,)), ((), ())),
                preferred_element_type=f32,
            )
        )
    blocks = [jnp.concatenate(singles[i : i + pack], axis=1) for i in range(0, seg_size, pack)]
    for group, block in enumerate(blocks):
        load_ref[group * rank : (group + 1) * rank, :] = block.astype(bf16)


def split(value):
    high = value.astype(bf16).astype(f32)
    rest = value - high
    middle = rest.astype(bf16).astype(f32)
    return high, middle, rest - middle


def coords_of(points_ref, at):
    block = points_ref[:, cluster(at)]
    zero, one, two = block[0:1, :], block[1:2, :], block[2:3, :]
    return zero, one, two, zero * zero + one * one + two * two


def rows_of(values):
    row = lax.broadcasted_iota(jnp.int32, (8, LEAF), 0)
    out = jnp.zeros((8, LEAF), f32)
    for i, value in enumerate(values):
        out = jnp.where(row == i, value, out)
    return out


def target_features(points_ref, at):
    zero, one, two, norm = coords_of(points_ref, at)
    slope = -2.0 * inverse_sq
    rows = rows_of((zero * slope, one * slope, two * slope, (norm + soften) * inverse_sq, 1.0))
    high, middle, low = split(rows)
    return jnp.concatenate([high, high, middle, middle, high, low], axis=0).astype(bf16)


def source_features(points_ref, at):
    zero, one, two, norm = coords_of(points_ref, at)
    rows = rows_of((zero, one, two, 1.0, norm * inverse_sq))
    high, middle, low = split(rows)
    stacked = jnp.concatenate([high, middle, high, middle, low, high], axis=0)
    return jnp.transpose(stacked).astype(bf16)


def feature_kernel(seg_size, targets, points_ref, target_ref, source_ref):
    blk_count = lax.axis_size("blk")
    blk = lax.axis_index("blk")
    first = lax.axis_index("leaf") * targets
    away = lax.rem(blk + 2 * lax.axis_index("rhs") + blk_count - 1, blk_count)
    for which, segment in enumerate((away, blk)):
        for i in range(targets):
            target_ref[which * targets + i] = target_features(points_ref, segment * seg_size + first + i)
    target_ref[2 * targets] = jnp.zeros((DEPTH, LEAF), bf16)

    def some_sources(step, carry):
        for u in range(8):
            at = step * 8 + u
            source_ref[at] = source_features(points_ref, blk * seg_size + at)
        return carry

    lax.fori_loop(0, seg_size // 8, some_sources, 0)


def near_kernel(base, part, list_ref, target_ref, source_ref, mine_ref, other_ref, out_ref, total, even, odd):
    targets = total.shape[0] - 1
    blank = target_ref.shape[0] - 1
    skipped = targets if part == 1 else 0
    begin = list_ref[7, LEAF - 2] if part == 1 else 0
    end = list_ref[7, LEAF - 2] if part == 0 else list_ref[7, LEAF - 1]
    batches = lax.div(end - begin + (BATCH - 1), BATCH)
    total[...] = jnp.zeros_like(total)

    def pair(batch, u):
        at = begin + batch * BATCH + u
        code = list_ref[lax.shift_right_logical(at, 7), lax.bitwise_and(at, 127)]
        code = jnp.where(at < end, code, (skipped + targets) * 256)
        return lax.shift_right_logical(code, 8), lax.bitwise_and(code, 255)

    def make(batch, slot):
        for u in range(BATCH):
            target, source = pair(batch, u)
            square = jnp.dot(source_ref[source], target_ref[jnp.minimum(base + target, blank)], preferred_element_type=f32)
            slot[u] = lax.rsqrt(square).astype(bf16)

    def use(batch, slot):
        sums = []
        for u in range(BATCH):
            target, source = pair(batch, u)
            charges = jnp.concatenate([mine_ref[:, cluster(source)], other_ref[:, cluster(source)]], axis=0)
            sums.append((target, jnp.dot(charges, slot[u], preferred_element_type=f32)))
        for target, value in sums:
            total[target - skipped] += value

    make(0, even)

    def body(step, carry):
        make(2 * step + 1, odd)
        use(2 * step, even)
        make(2 * step + 2, even)
        use(2 * step + 1, odd)
        return carry

    lax.fori_loop(0, lax.div(batches, 2), body, 0)

    @pl.when(lax.rem(batches, 2) == 1)
    def _():
        use(batches - 1, even)

    for i in range(targets):
        out_ref[:, i * LEAF : (i + 1) * LEAF] = total[i].astype(out_ref.dtype)


def near_sum(base, part, microseconds, targets, pairs, target_rows, source_rows, mine, other, dtype):
    columns = 2 * mine.shape[0]
    return pl.pallas_call(
        functools.partial(near_kernel, base, part),
        out_shape=jax.ShapeDtypeStruct((columns, targets * LEAF), dtype),
        in_specs=[SMEM] + [VMEM] * 4,
        out_specs=VMEM,
        scratch_shapes=[
            pltpu.VMEM((targets + 1, columns, LEAF), f32),
            pltpu.VMEM((BATCH, LEAF, LEAF), bf16),
            pltpu.VMEM((BATCH, LEAF, LEAF), bf16),
        ],
        compiler_params=PARAMS,
        cost_estimate=cost(microseconds),
    )(pairs, target_rows, source_rows, mine, other)


def far_sum(out_ref, basis_ref, target, at, coefficient):
    out_ref[:, target * LEAF : (target + 1) * LEAF] = lax.dot_general(
        coefficient.astype(bf16),
        basis_ref[:, cluster(at)],
        (((0,), (0,)), ((), ())),
        preferred_element_type=f32,
    )


def far_kernel(seg_size, far_ref, couplings_ref, basis_ref, part, out_ref, skel):
    leaf = lax.axis_index("leaf") * couplings_ref.shape[0]
    clusters, far_count, rank, _ = couplings_ref.shape
    columns = out_ref.shape[0]
    pack = LEAF // columns

    def unpack(group, carry):
        block = part[pl.ds(pl.multiple_of(group * rank, rank), rank), :]
        for i in range(pack):
            skel[group * pack + i] = block[:, i * columns : (i + 1) * columns]
        return carry

    lax.fori_loop(0, part.shape[0] // rank, unpack, 0)
    for target in range(clusters):
        coefficient = jnp.zeros((rank, columns), f32)
        step = 256 // rank
        for at in range(0, far_count, step):
            left = jnp.concatenate([couplings_ref[target, at + i] for i in range(step)], axis=1)
            rows = [skel[far_ref[target, at + i]] for i in range(step)]
            coefficient = coefficient + jnp.dot(
                left, jnp.concatenate(rows, axis=0), preferred_element_type=f32
            )
        far_sum(out_ref, basis_ref, target, leaf + target, coefficient)


def far_kernel_phased(seg_size, far_ref, couplings_ref, basis_ref, *refs):
    parts, (out_ref, skel, side, held) = refs[:-4], refs[-4:]
    clusters, far_count, rank, _ = couplings_ref.shape
    columns = out_ref.shape[0]
    pack = LEAF // columns
    leaf = lax.axis_index("leaf") * clusters
    for target in range(clusters):
        for at in range(0, far_count, pack):
            side[target, :, at * rank : (at + pack) * rank] = jnp.concatenate(
                [couplings_ref[target, at + i] for i in range(pack)], axis=1
            )
    for order, part in enumerate(parts):
        for group in range(seg_size // pack):
            block = part[group * rank : (group + 1) * rank, :]
            for i in range(pack):
                skel[order * seg_size + group * pack + i] = block[:, i * columns : (i + 1) * columns]
    step = 256 // rank
    for target in range(clusters):
        coefficient = jnp.zeros((rank, columns), f32)
        for at in range(0, far_count, step):
            rows = [skel[far_ref[target, at + i]] for i in range(step)]
            coefficient = coefficient + jnp.dot(
                side[target, :, at * rank : (at + step) * rank],
                jnp.concatenate(rows, axis=0),
                preferred_element_type=f32,
            )
        held[target] = coefficient.astype(bf16)
    for target in range(clusters):
        far_sum(out_ref, basis_ref, target, leaf + target, held[target])


def on_device(points, charges, basis, couplings, near_src, far_src):
    blk_count = lax.axis_size("blk")
    mine = charges.T
    columns, seg_rows = mine.shape
    seg_size = seg_rows // LEAF
    rank = basis.shape[0]
    own_clusters, near_count = near_src.shape
    cluster_total = seg_size * blk_count
    pack = LEAF // columns
    skel_rows = seg_size // pack * rank
    other = shifted(mine, "rhs", 1)
    own_list, load = pl.pallas_call(
        functools.partial(list_kernel, seg_size),
        out_shape=[
            jax.ShapeDtypeStruct((8, LEAF), jnp.int32),
            jax.ShapeDtypeStruct((skel_rows + 16, LEAF), bf16),
        ],
        in_specs=[HBM] * 3,
        out_specs=[VMEM] * 2,
        scratch_shapes=[
            pltpu.VMEM(near_src.shape, jnp.int32),
            pltpu.VMEM(basis.shape, bf16),
            pltpu.VMEM(mine.shape, bf16),
            pltpu.SemaphoreType.DMA((3,)),
        ],
        compiler_params=pltpu.CompilerParams(vmem_limit_bytes=63 * 2**20),
        cost_estimate=cost(3.0),
    )(near_src, basis, mine)

    points, load = lax.optimization_barrier((points, load))
    first_load = crossed(load, 1)
    target_rows, source_rows = pl.pallas_call(
        functools.partial(feature_kernel, seg_size, own_clusters),
        out_shape=[
            jax.ShapeDtypeStruct((2 * own_clusters + 1, DEPTH, LEAF), bf16),
            jax.ShapeDtypeStruct((seg_size, LEAF, DEPTH), bf16),
        ],
        in_specs=[VMEM],
        out_specs=[VMEM, VMEM],
        compiler_params=PARAMS,
        cost_estimate=cost(0.7),
    )(points)
    target_rows, later_load = lax.optimization_barrier((target_rows, load))
    narrow = blk_count == 4 and cluster_total <= 256
    if narrow:
        loads = [load, crossed(later_load, -1), shifted(later_load, "blk", 2), first_load]
    else:
        loads = [lax.all_gather(later_load[:skel_rows], "blk", axis=0, tiled=True)]
    args = (target_rows, source_rows, mine, other)
    codes = first_load[skel_rows:].astype(jnp.int32)
    pairs = codes[:8] + 256 * codes[8:]
    low = near_sum(0, 0, 20.0, own_clusters // 2, pairs, *args, bf16)
    low, pairs = lax.optimization_barrier((low, pairs))
    low_back = crossed(low, -1)
    high = near_sum(0, 1, 20.0, own_clusters // 2, pairs, *args, bf16)
    high, own_list = lax.optimization_barrier((high, own_list))
    high_back = crossed(high, -1)
    own_near = near_sum(own_clusters, None, 0.5, own_clusters, own_list, *args, f32)
    own_near, loads, low_back = lax.optimization_barrier((own_near, loads, low_back))

    blk = lax.axis_index("blk")
    first = blk * seg_size + lax.axis_index("leaf") * own_clusters
    entries = lax.dynamic_slice_in_dim(far_src, first, own_clusters, 0)
    far_shape = jax.ShapeDtypeStruct((columns, own_clusters * LEAF), f32)
    if narrow:
        segment = lax.div(entries, seg_size)
        ahead = jnp.where(lax.axis_index("rhs") == 0, segment - blk, blk - segment)
        order = lax.rem(ahead + blk_count, blk_count)
        entries = entries + (order - segment) * seg_size
        far = pl.pallas_call(
            functools.partial(far_kernel_phased, seg_size),
            out_shape=far_shape,
            in_specs=[SMEM] + [VMEM] * 6,
            out_specs=VMEM,
            scratch_shapes=[
                pltpu.VMEM((cluster_total, rank, columns), bf16),
                pltpu.VMEM((own_clusters, rank, far_src.shape[1] * rank), bf16),
                pltpu.VMEM((own_clusters, rank, columns), bf16),
            ],
            compiler_params=PARAMS,
            cost_estimate=cost(20.0),
        )(entries, couplings, basis, *loads)
    else:
        far = pl.pallas_call(
            functools.partial(far_kernel, seg_size),
            out_shape=far_shape,
            in_specs=[SMEM] + [VMEM] * 3,
            out_specs=VMEM,
            scratch_shapes=[pltpu.VMEM((cluster_total, rank, columns), bf16)],
            compiler_params=PARAMS,
        )(entries, couplings, basis, *loads)

    far, low_back, high_back = lax.optimization_barrier((far, low_back, high_back))
    near = own_near + jnp.concatenate([low_back, high_back], axis=1).astype(f32)
    got = shifted(near[columns:].astype(bf16), "rhs", 1)
    return (near[:columns] + got.astype(f32) + far).astype(bf16).T


def solution(mesh):
    in_specs = (
        P(None, "groups"),
        P(("groups", "blk"), "rhs"),
        P(None, ("groups", "blk")),
        P(("groups", "blk", "leaf"), None, None, None),
        P(("groups", "blk", "leaf"), None),
        P("groups", None),
    )
    out_specs = P(("groups", "blk", "leaf"), "rhs")
    return jax.shard_map(
        on_device, mesh=mesh, in_specs=in_specs, out_specs=out_specs, check_vma=False
    )
```

```python
import functools

import jax
import jax.numpy as jnp
from jax import lax
from jax.experimental import pallas as pl
from jax.experimental.pallas import tpu as pltpu
from jax.sharding import PartitionSpec as P

LEAF = 128
BATCH = 16
DEPTH = 48

kernel_scale = 0.0625 / (4.0 * 3.141592653589793)
soften = 0.001
inverse_sq = 1.0 / (kernel_scale * kernel_scale)

bf16 = jnp.bfloat16
f32 = jnp.float32
VMEM = pl.BlockSpec(memory_space=pltpu.VMEM)
HBM = pl.BlockSpec(memory_space=pltpu.HBM)
SMEM = pl.BlockSpec(memory_space=pltpu.SMEM)
PARAMS = pltpu.CompilerParams(vmem_limit_bytes=48 * 2**20)


def cost(microseconds):
    return pl.CostEstimate(flops=int(microseconds * 1e9), bytes_accessed=0, transcendentals=0)


def shifted(block, axis, shift):
    count = lax.axis_size(axis)
    return lax.ppermute(block, axis, [(i, (i + shift) % count) for i in range(count)])


def crossed(block, shift):
    count = lax.axis_size("blk")
    pairs = []
    for i in range(count):
        pairs.append((2 * i, (i + shift) % count * 2))
        pairs.append((2 * i + 1, (i - shift) % count * 2 + 1))
    return lax.ppermute(block, ("blk", "rhs"), pairs)


def cluster(index):
    return pl.ds(pl.multiple_of(index * LEAF, LEAF), LEAF)


def list_kernel(seg_size, near_hbm, basis_hbm, charges_hbm, own_ref, load_ref, near_ref, basis_ref, charges_ref, sems):
    copies = [
        pltpu.make_async_copy(near_hbm, near_ref, sems.at[0]),
        pltpu.make_async_copy(basis_hbm, basis_ref, sems.at[1]),
        pltpu.make_async_copy(charges_hbm, charges_ref, sems.at[2]),
    ]
    for copy in copies:
        copy.start()
    targets, near_count = near_ref.shape
    blk_count = lax.axis_size("blk")
    blk = lax.axis_index("blk")
    before = lax.rem(blk + blk_count - 1, blk_count)
    half = lax.axis_index("rhs")
    columns = charges_ref.shape[0]
    rank = basis_ref.shape[0]
    pack = LEAF // columns
    slots = 4 if near_count <= LEAF // 4 and targets % 4 == 0 else 1
    width = LEAF // slots
    lines = targets // slots

    def iota(shape, dim):
        return lax.broadcasted_iota(jnp.int32, shape, dim)

    def ones(condition):
        return jnp.where(condition, 1.0, 0.0).astype(bf16)

    lane = iota((lines, LEAF), 1)
    target = iota((lines, LEAF), 0) * slots + lane // width
    in_half = target // (targets // 2) == half
    earlier = ones(iota((LEAF, LEAF), 0) < iota((LEAF, LEAF), 1))
    whole = jnp.ones((LEAF, LEAF), bf16)
    above = ones(iota((lines, lines), 1) < iota((lines, lines), 0))
    row = iota((8, LEAF), 0)
    lower = iota((LEAF, LEAF), 0)
    filler = jnp.full((1, width - near_count), -1, jnp.int32)
    for copy in copies:
        copy.wait()
    packed = []
    for line in range(lines):
        pieces = []
        for i in range(slots):
            at = line * slots + i
            pieces += [near_ref[at : at + 1, :], filler]
        packed.append(jnp.concatenate(pieces, axis=1))
    sources = jnp.concatenate(packed, axis=0)
    if seg_size & (seg_size - 1) == 0:
        segment = lax.shift_right_arithmetic(sources, seg_size.bit_length() - 1)
    else:
        segment = lax.div(sources, seg_size)
    local = (sources - segment * seg_size).astype(f32)
    is_own = segment == blk
    is_prev = jnp.logical_and(segment == before, jnp.logical_not(is_own))
    is_next = jnp.logical_and(sources >= 0, jnp.logical_not(jnp.logical_or(is_own, is_prev)))
    is_own = jnp.logical_and(jnp.logical_and(is_own, in_half), sources >= 0)
    is_prev = jnp.logical_and(is_prev, sources >= 0)
    leaving = jnp.where(half == 0, jnp.where(is_next, 1, 0), jnp.where(is_prev, 1, 0))
    masks = (is_own, leaving == 1)
    place = jnp.zeros((lines, LEAF), f32)
    totals, middles = [], []
    for mask in masks:
        within = jnp.dot(ones(mask), earlier, preferred_element_type=f32)
        count = jnp.dot(ones(mask), whole, preferred_element_type=f32)
        start = jnp.dot(above, count.astype(bf16), preferred_element_type=f32)
        place = jnp.where(mask, start + within, place)
        totals.append(start[lines - 1 :, :] + count[lines - 1 :, :])
        middles.append(start[lines // 2 : lines // 2 + 1, :])
    place = place.astype(jnp.int32)
    target = target.astype(f32)
    left, right = [], []
    for line in range(lines):
        at = place[line : line + 1, :]
        here = lax.shift_right_logical(at, 7) == row
        rows = []
        for mask in masks:
            chosen = jnp.logical_and(here, jnp.where(mask[line : line + 1, :], 1, 0) == 1)
            rows.append(jnp.where(chosen, local[line : line + 1, :], 0.0))
            rows.append(jnp.where(chosen, target[line : line + 1, :], 0.0))
        left.append(jnp.concatenate(rows, axis=0).astype(bf16))
        right.append(ones(lax.bitwise_and(at, LEAF - 1) == lower))
    lists = lax.dot_general(
        jnp.concatenate(left, axis=1),
        jnp.concatenate(right, axis=1),
        (((1,), (1,)), ((), ())),
        preferred_element_type=f32,
    )
    last = row * LEAF + iota((8, LEAF), 1) == 8 * LEAF - 1
    own = lists[:8] + 256.0 * lists[8:16]
    own_ref[...] = jnp.where(last, totals[0], own).astype(jnp.int32)
    prior = row * LEAF + iota((8, LEAF), 1) == 8 * LEAF - 2
    length = jnp.where(prior, middles[1], totals[1])
    high = jnp.floor(length * (1.0 / 256.0))
    ends = jnp.logical_or(last, prior)
    away = jnp.concatenate(
        [jnp.where(ends, length - 256.0 * high, lists[16:24]), jnp.where(ends, high, lists[24:32])], axis=0
    )
    rows_end = seg_size // pack * rank
    load_ref[rows_end : rows_end + 16, :] = away.astype(bf16)

    singles = []
    for index in range(seg_size):
        at = index * LEAF
        singles.append(
            lax.dot_general(
                basis_ref[:, at : at + LEAF],
                charges_ref[:, at : at + LEAF],
                (((1,), (1,)), ((), ())),
                preferred_element_type=f32,
            )
        )
    blocks = [jnp.concatenate(singles[i : i + pack], axis=1) for i in range(0, seg_size, pack)]
    for group, block in enumerate(blocks):
        load_ref[group * rank : (group + 1) * rank, :] = block.astype(bf16)


def split(value):
    high = value.astype(bf16).astype(f32)
    rest = value - high
    middle = rest.astype(bf16).astype(f32)
    return high, middle, rest - middle


def coords_of(points_ref, at):
    block = points_ref[:, cluster(at)]
    zero, one, two = block[0:1, :], block[1:2, :], block[2:3, :]
    return zero, one, two, zero * zero + one * one + two * two


def rows_of(values):
    row = lax.broadcasted_iota(jnp.int32, (8, LEAF), 0)
    out = jnp.zeros((8, LEAF), f32)
    for i, value in enumerate(values):
        out = jnp.where(row == i, value, out)
    return out


def target_features(points_ref, at):
    zero, one, two, norm = coords_of(points_ref, at)
    slope = -2.0 * inverse_sq
    rows = rows_of((zero * slope, one * slope, two * slope, (norm + soften) * inverse_sq, 1.0))
    high, middle, low = split(rows)
    return jnp.concatenate([high, high, middle, middle, high, low], axis=0).astype(bf16)


def source_features(points_ref, at):
    zero, one, two, norm = coords_of(points_ref, at)
    rows = rows_of((zero, one, two, 1.0, norm * inverse_sq))
    high, middle, low = split(rows)
    stacked = jnp.concatenate([high, middle, high, middle, low, high], axis=0)
    return jnp.transpose(stacked).astype(bf16)


def feature_kernel(seg_size, targets, points_ref, target_ref, source_ref):
    blk_count = lax.axis_size("blk")
    blk = lax.axis_index("blk")
    first = lax.axis_index("leaf") * targets
    away = lax.rem(blk + 2 * lax.axis_index("rhs") + blk_count - 1, blk_count)
    for which, segment in enumerate((away, blk)):
        for i in range(targets):
            target_ref[which * targets + i] = target_features(points_ref, segment * seg_size + first + i)
    target_ref[2 * targets] = jnp.zeros((DEPTH, LEAF), bf16)

    def some_sources(step, carry):
        for u in range(8):
            at = step * 8 + u
            source_ref[at] = source_features(points_ref, blk * seg_size + at)
        return carry

    lax.fori_loop(0, seg_size // 8, some_sources, 0)


def near_kernel(base, part, list_ref, target_ref, source_ref, mine_ref, other_ref, out_ref, total, even, odd):
    targets = total.shape[0] - 1
    blank = target_ref.shape[0] - 1
    skipped = targets if part == 1 else 0
    begin = list_ref[7, LEAF - 2] if part == 1 else 0
    end = list_ref[7, LEAF - 2] if part == 0 else list_ref[7, LEAF - 1]
    batches = lax.div(end - begin + (BATCH - 1), BATCH)
    total[...] = jnp.zeros_like(total)

    def pair(batch, u):
        at = begin + batch * BATCH + u
        code = list_ref[lax.shift_right_logical(at, 7), lax.bitwise_and(at, 127)]
        code = jnp.where(at < end, code, (skipped + targets) * 256)
        return lax.shift_right_logical(code, 8), lax.bitwise_and(code, 255)

    def make(batch, slot):
        for u in range(BATCH):
            target, source = pair(batch, u)
            square = jnp.dot(source_ref[source], target_ref[jnp.minimum(base + target, blank)], preferred_element_type=f32)
            slot[u] = lax.rsqrt(square).astype(bf16)

    def use(batch, slot):
        sums = []
        for u in range(BATCH):
            target, source = pair(batch, u)
            charges = jnp.concatenate([mine_ref[:, cluster(source)], other_ref[:, cluster(source)]], axis=0)
            sums.append((target, jnp.dot(charges, slot[u], preferred_element_type=f32)))
        for target, value in sums:
            total[target - skipped] += value

    make(0, even)

    def body(step, carry):
        make(2 * step + 1, odd)
        use(2 * step, even)
        make(2 * step + 2, even)
        use(2 * step + 1, odd)
        return carry

    lax.fori_loop(0, lax.div(batches, 2), body, 0)

    @pl.when(lax.rem(batches, 2) == 1)
    def _():
        use(batches - 1, even)

    for i in range(targets):
        out_ref[:, i * LEAF : (i + 1) * LEAF] = total[i].astype(out_ref.dtype)


def near_sum(base, part, microseconds, targets, pairs, target_rows, source_rows, mine, other, dtype):
    columns = 2 * mine.shape[0]
    return pl.pallas_call(
        functools.partial(near_kernel, base, part),
        out_shape=jax.ShapeDtypeStruct((columns, targets * LEAF), dtype),
        in_specs=[SMEM] + [VMEM] * 4,
        out_specs=VMEM,
        scratch_shapes=[
            pltpu.VMEM((targets + 1, columns, LEAF), f32),
            pltpu.VMEM((BATCH, LEAF, LEAF), bf16),
            pltpu.VMEM((BATCH, LEAF, LEAF), bf16),
        ],
        compiler_params=PARAMS,
        cost_estimate=cost(microseconds),
    )(pairs, target_rows, source_rows, mine, other)


def far_sum(out_ref, basis_ref, target, at, coefficient):
    out_ref[:, target * LEAF : (target + 1) * LEAF] = lax.dot_general(
        coefficient.astype(bf16),
        basis_ref[:, cluster(at)],
        (((0,), (0,)), ((), ())),
        preferred_element_type=f32,
    )


def far_kernel(seg_size, far_ref, couplings_ref, basis_ref, part, out_ref, skel):
    leaf = lax.axis_index("leaf") * couplings_ref.shape[0]
    clusters, far_count, rank, _ = couplings_ref.shape
    columns = out_ref.shape[0]
    pack = LEAF // columns

    def unpack(group, carry):
        block = part[pl.ds(pl.multiple_of(group * rank, rank), rank), :]
        for i in range(pack):
            skel[group * pack + i] = block[:, i * columns : (i + 1) * columns]
        return carry

    lax.fori_loop(0, part.shape[0] // rank, unpack, 0)
    for target in range(clusters):
        coefficient = jnp.zeros((rank, columns), f32)
        step = 256 // rank
        for at in range(0, far_count, step):
            left = jnp.concatenate([couplings_ref[target, at + i] for i in range(step)], axis=1)
            rows = [skel[far_ref[target, at + i]] for i in range(step)]
            coefficient = coefficient + jnp.dot(
                left, jnp.concatenate(rows, axis=0), preferred_element_type=f32
            )
        far_sum(out_ref, basis_ref, target, leaf + target, coefficient)


def far_kernel_phased(seg_size, far_ref, couplings_ref, basis_ref, *refs):
    parts, (out_ref, skel, side, held) = refs[:-4], refs[-4:]
    clusters, far_count, rank, _ = couplings_ref.shape
    columns = out_ref.shape[0]
    pack = LEAF // columns
    leaf = lax.axis_index("leaf") * clusters
    for target in range(clusters):
        for at in range(0, far_count, pack):
            side[target, :, at * rank : (at + pack) * rank] = jnp.concatenate(
                [couplings_ref[target, at + i] for i in range(pack)], axis=1
            )
    for order, part in enumerate(parts):
        for group in range(seg_size // pack):
            block = part[group * rank : (group + 1) * rank, :]
            for i in range(pack):
                skel[order * seg_size + group * pack + i] = block[:, i * columns : (i + 1) * columns]
    step = 256 // rank
    for target in range(clusters):
        coefficient = jnp.zeros((rank, columns), f32)
        for at in range(0, far_count, step):
            rows = [skel[far_ref[target, at + i]] for i in range(step)]
            coefficient = coefficient + jnp.dot(
                side[target, :, at * rank : (at + step) * rank],
                jnp.concatenate(rows, axis=0),
                preferred_element_type=f32,
            )
        held[target] = coefficient.astype(bf16)
    for target in range(clusters):
        far_sum(out_ref, basis_ref, target, leaf + target, held[target])


def on_device(points, charges, basis, couplings, near_src, far_src):
    blk_count = lax.axis_size("blk")
    mine = charges.T
    columns, seg_rows = mine.shape
    seg_size = seg_rows // LEAF
    rank = basis.shape[0]
    own_clusters, near_count = near_src.shape
    cluster_total = seg_size * blk_count
    pack = LEAF // columns
    skel_rows = seg_size // pack * rank
    other = shifted(mine, "rhs", 1)
    own_list, load = pl.pallas_call(
        functools.partial(list_kernel, seg_size),
        out_shape=[
            jax.ShapeDtypeStruct((8, LEAF), jnp.int32),
            jax.ShapeDtypeStruct((skel_rows + 16, LEAF), bf16),
        ],
        in_specs=[HBM] * 3,
        out_specs=[VMEM] * 2,
        scratch_shapes=[
            pltpu.VMEM(near_src.shape, jnp.int32),
            pltpu.VMEM(basis.shape, bf16),
            pltpu.VMEM(mine.shape, bf16),
            pltpu.SemaphoreType.DMA((3,)),
        ],
        compiler_params=pltpu.CompilerParams(vmem_limit_bytes=63 * 2**20),
        cost_estimate=cost(3.0),
    )(near_src, basis, mine)

    points, load = lax.optimization_barrier((points, load))
    first_load = crossed(load, 1)
    target_rows, source_rows = pl.pallas_call(
        functools.partial(feature_kernel, seg_size, own_clusters),
        out_shape=[
            jax.ShapeDtypeStruct((2 * own_clusters + 1, DEPTH, LEAF), bf16),
            jax.ShapeDtypeStruct((seg_size, LEAF, DEPTH), bf16),
        ],
        in_specs=[VMEM],
        out_specs=[VMEM, VMEM],
        compiler_params=PARAMS,
        cost_estimate=cost(0.7),
    )(points)
    target_rows, later_load = lax.optimization_barrier((target_rows, load))
    narrow = blk_count == 4 and cluster_total <= 256
    if narrow:
        loads = [load, crossed(later_load, -1), shifted(later_load, "blk", 2), first_load]
    else:
        loads = [lax.all_gather(later_load[:skel_rows], "blk", axis=0, tiled=True)]
    args = (target_rows, source_rows, mine, other)
    codes = first_load[skel_rows:].astype(jnp.int32)
    pairs = codes[:8] + 256 * codes[8:]
    low = near_sum(0, 0, 20.0, own_clusters // 2, pairs, *args, bf16)
    low, pairs = lax.optimization_barrier((low, pairs))
    low_back = crossed(low, -1)
    high = near_sum(0, 1, 20.0, own_clusters // 2, pairs, *args, bf16)
    high, own_list = lax.optimization_barrier((high, own_list))
    high_back = crossed(high, -1)
    own_near = near_sum(own_clusters, None, 0.5, own_clusters, own_list, *args, f32)
    own_near, loads, low_back = lax.optimization_barrier((own_near, loads, low_back))

    blk = lax.axis_index("blk")
    first = blk * seg_size + lax.axis_index("leaf") * own_clusters
    entries = lax.dynamic_slice_in_dim(far_src, first, own_clusters, 0)
    far_shape = jax.ShapeDtypeStruct((columns, own_clusters * LEAF), f32)
    if narrow:
        segment = lax.div(entries, seg_size)
        ahead = jnp.where(lax.axis_index("rhs") == 0, segment - blk, blk - segment)
        order = lax.rem(ahead + blk_count, blk_count)
        entries = entries + (order - segment) * seg_size
        far = pl.pallas_call(
            functools.partial(far_kernel_phased, seg_size),
            out_shape=far_shape,
            in_specs=[SMEM] + [VMEM] * 6,
            out_specs=VMEM,
            scratch_shapes=[
                pltpu.VMEM((cluster_total, rank, columns), bf16),
                pltpu.VMEM((own_clusters, rank, far_src.shape[1] * rank), bf16),
                pltpu.VMEM((own_clusters, rank, columns), bf16),
            ],
            compiler_params=PARAMS,
            cost_estimate=cost(20.0),
        )(entries, couplings, basis, *loads)
    else:
        far = pl.pallas_call(
            functools.partial(far_kernel, seg_size),
            out_shape=far_shape,
            in_specs=[SMEM] + [VMEM] * 3,
            out_specs=VMEM,
            scratch_shapes=[pltpu.VMEM((cluster_total, rank, columns), bf16)],
            compiler_params=PARAMS,
        )(entries, couplings, basis, *loads)

    far, low_back, high_back = lax.optimization_barrier((far, low_back, high_back))
    near = own_near + jnp.concatenate([low_back, high_back], axis=1).astype(f32)
    got = shifted(near[columns:].astype(bf16), "rhs", 1)
    return (near[:columns] + got.astype(f32) + far).astype(bf16).T


def solution(mesh):
    in_specs = (
        P(None, "groups"),
        P(("groups", "blk"), "rhs"),
        P(None, ("groups", "blk")),
        P(("groups", "blk", "leaf"), None, None, None),
        P(("groups", "blk", "leaf"), None),
        P("groups", None),
    )
    out_specs = P(("groups", "blk", "leaf"), "rhs")
    return jax.shard_map(
        on_device, mesh=mesh, in_specs=in_specs, out_specs=out_specs, check_vma=False
    )
```

```python
import functools

import jax
import jax.numpy as jnp
from jax import lax
from jax.experimental import pallas as pl
from jax.experimental.pallas import tpu as pltpu
from jax.sharding import PartitionSpec as P

LEAF = 128
BATCH = 16
DEPTH = 48

kernel_scale = 0.0625 / (4.0 * 3.141592653589793)
soften = 0.001
inverse_sq = 1.0 / (kernel_scale * kernel_scale)

bf16 = jnp.bfloat16
f32 = jnp.float32
VMEM = pl.BlockSpec(memory_space=pltpu.VMEM)
HBM = pl.BlockSpec(memory_space=pltpu.HBM)
SMEM = pl.BlockSpec(memory_space=pltpu.SMEM)
PARAMS = pltpu.CompilerParams(vmem_limit_bytes=48 * 2**20)


def cost(microseconds):
    return pl.CostEstimate(flops=int(microseconds * 1e9), bytes_accessed=0, transcendentals=0)


def shifted(block, axis, shift):
    count = lax.axis_size(axis)
    return lax.ppermute(block, axis, [(i, (i + shift) % count) for i in range(count)])


def crossed(block, shift):
    count = lax.axis_size("blk")
    pairs = []
    for i in range(count):
        pairs.append((2 * i, (i + shift) % count * 2))
        pairs.append((2 * i + 1, (i - shift) % count * 2 + 1))
    return lax.ppermute(block, ("blk", "rhs"), pairs)


def cluster(index):
    return pl.ds(pl.multiple_of(index * LEAF, LEAF), LEAF)


def list_kernel(seg_size, near_hbm, basis_hbm, charges_hbm, own_ref, load_ref, near_ref, basis_ref, charges_ref, sems):
    copies = [
        pltpu.make_async_copy(near_hbm, near_ref, sems.at[0]),
        pltpu.make_async_copy(basis_hbm, basis_ref, sems.at[1]),
        pltpu.make_async_copy(charges_hbm, charges_ref, sems.at[2]),
    ]
    for copy in copies:
        copy.start()
    targets, near_count = near_ref.shape
    blk_count = lax.axis_size("blk")
    blk = lax.axis_index("blk")
    before = lax.rem(blk + blk_count - 1, blk_count)
    half = lax.axis_index("rhs")
    columns = charges_ref.shape[0]
    rank = basis_ref.shape[0]
    pack = LEAF // columns
    slots = 4 if near_count <= LEAF // 4 and targets % 4 == 0 else 1
    width = LEAF // slots
    lines = targets // slots

    def iota(shape, dim):
        return lax.broadcasted_iota(jnp.int32, shape, dim)

    def ones(condition):
        return jnp.where(condition, 1.0, 0.0).astype(bf16)

    lane = iota((lines, LEAF), 1)
    target = iota((lines, LEAF), 0) * slots + lane // width
    in_half = target // (targets // 2) == half
    earlier = ones(iota((LEAF, LEAF), 0) < iota((LEAF, LEAF), 1))
    whole = jnp.ones((LEAF, LEAF), bf16)
    above = ones(iota((lines, lines), 1) < iota((lines, lines), 0))
    row = iota((8, LEAF), 0)
    lower = iota((LEAF, LEAF), 0)
    filler = jnp.full((1, width - near_count), -1, jnp.int32)
    copies[0].wait()
    packed = []
    for line in range(lines):
        pieces = []
        for i in range(slots):
            at = line * slots + i
            pieces += [near_ref[at : at + 1, :], filler]
        packed.append(jnp.concatenate(pieces, axis=1))
    sources = jnp.concatenate(packed, axis=0)
    if seg_size & (seg_size - 1) == 0:
        segment = lax.shift_right_arithmetic(sources, seg_size.bit_length() - 1)
    else:
        segment = lax.div(sources, seg_size)
    local = (sources - segment * seg_size).astype(f32)
    is_own = segment == blk
    is_prev = jnp.logical_and(segment == before, jnp.logical_not(is_own))
    is_next = jnp.logical_and(sources >= 0, jnp.logical_not(jnp.logical_or(is_own, is_prev)))
    is_own = jnp.logical_and(jnp.logical_and(is_own, in_half), sources >= 0)
    is_prev = jnp.logical_and(is_prev, sources >= 0)
    leaving = jnp.where(half == 0, jnp.where(is_next, 1, 0), jnp.where(is_prev, 1, 0))
    masks = (is_own, leaving == 1)
    place = jnp.zeros((lines, LEAF), f32)
    totals, middles = [], []
    for mask in masks:
        within = jnp.dot(ones(mask), earlier, preferred_element_type=f32)
        count = jnp.dot(ones(mask), whole, preferred_element_type=f32)
        start = jnp.dot(above, count.astype(bf16), preferred_element_type=f32)
        place = jnp.where(mask, start + within, place)
        totals.append(start[lines - 1 :, :] + count[lines - 1 :, :])
        middles.append(start[lines // 2 : lines // 2 + 1, :])
    place = place.astype(jnp.int32)
    target = target.astype(f32)
    left, right = [], []
    for line in range(lines):
        at = place[line : line + 1, :]
        here = lax.shift_right_logical(at, 7) == row
        rows = []
        for mask in masks:
            chosen = jnp.logical_and(here, jnp.where(mask[line : line + 1, :], 1, 0) == 1)
            rows.append(jnp.where(chosen, local[line : line + 1, :], 0.0))
            rows.append(jnp.where(chosen, target[line : line + 1, :], 0.0))
        left.append(jnp.concatenate(rows, axis=0).astype(bf16))
        right.append(ones(lax.bitwise_and(at, LEAF - 1) == lower))
    lists = lax.dot_general(
        jnp.concatenate(left, axis=1),
        jnp.concatenate(right, axis=1),
        (((1,), (1,)), ((), ())),
        preferred_element_type=f32,
    )
    last = row * LEAF + iota((8, LEAF), 1) == 8 * LEAF - 1
    own = lists[:8] + 256.0 * lists[8:16]
    own_ref[...] = jnp.where(last, totals[0], own).astype(jnp.int32)
    prior = row * LEAF + iota((8, LEAF), 1) == 8 * LEAF - 2
    length = jnp.where(prior, middles[1], totals[1])
    high = jnp.floor(length * (1.0 / 256.0))
    ends = jnp.logical_or(last, prior)
    away = jnp.concatenate(
        [jnp.where(ends, length - 256.0 * high, lists[16:24]), jnp.where(ends, high, lists[24:32])], axis=0
    )
    rows_end = seg_size // pack * rank
    load_ref[rows_end : rows_end + 16, :] = away.astype(bf16)

    copies[1].wait()
    copies[2].wait()
    singles = []
    for index in range(seg_size):
        at = index * LEAF
        singles.append(
            lax.dot_general(
                basis_ref[:, at : at + LEAF],
                charges_ref[:, at : at + LEAF],
                (((1,), (1,)), ((), ())),
                preferred_element_type=f32,
            )
        )
    blocks = [jnp.concatenate(singles[i : i + pack], axis=1) for i in range(0, seg_size, pack)]
    for group, block in enumerate(blocks):
        load_ref[group * rank : (group + 1) * rank, :] = block.astype(bf16)


def split(value):
    high = value.astype(bf16).astype(f32)
    rest = value - high
    middle = rest.astype(bf16).astype(f32)
    return high, middle, rest - middle


def coords_of(points_ref, at):
    block = points_ref[:, cluster(at)]
    zero, one, two = block[0:1, :], block[1:2, :], block[2:3, :]
    return zero, one, two, zero * zero + one * one + two * two


def rows_of(values):
    row = lax.broadcasted_iota(jnp.int32, (8, LEAF), 0)
    out = jnp.zeros((8, LEAF), f32)
    for i, value in enumerate(values):
        out = jnp.where(row == i, value, out)
    return out


def target_features(points_ref, at):
    zero, one, two, norm = coords_of(points_ref, at)
    slope = -2.0 * inverse_sq
    rows = rows_of((zero * slope, one * slope, two * slope, (norm + soften) * inverse_sq, 1.0))
    high, middle, low = split(rows)
    return jnp.concatenate([high, high, middle, middle, high, low], axis=0).astype(bf16)


def source_features(points_ref, at):
    zero, one, two, norm = coords_of(points_ref, at)
    rows = rows_of((zero, one, two, 1.0, norm * inverse_sq))
    high, middle, low = split(rows)
    stacked = jnp.concatenate([high, middle, high, middle, low, high], axis=0)
    return jnp.transpose(stacked).astype(bf16)


def feature_kernel(seg_size, targets, points_ref, target_ref, source_ref):
    blk_count = lax.axis_size("blk")
    blk = lax.axis_index("blk")
    first = lax.axis_index("leaf") * targets
    away = lax.rem(blk + 2 * lax.axis_index("rhs") + blk_count - 1, blk_count)
    for which, segment in enumerate((away, blk)):
        for i in range(targets):
            target_ref[which * targets + i] = target_features(points_ref, segment * seg_size + first + i)
    target_ref[2 * targets] = jnp.zeros((DEPTH, LEAF), bf16)

    def some_sources(step, carry):
        for u in range(8):
            at = step * 8 + u
            source_ref[at] = source_features(points_ref, blk * seg_size + at)
        return carry

    lax.fori_loop(0, seg_size // 8, some_sources, 0)


def near_kernel(base, part, list_ref, target_ref, source_ref, mine_ref, other_ref, out_ref, total, even, odd):
    targets = total.shape[0] - 1
    blank = target_ref.shape[0] - 1
    skipped = targets if part == 1 else 0
    begin = list_ref[7, LEAF - 2] if part == 1 else 0
    end = list_ref[7, LEAF - 2] if part == 0 else list_ref[7, LEAF - 1]
    batches = lax.div(end - begin + (BATCH - 1), BATCH)
    total[...] = jnp.zeros_like(total)

    def pair(batch, u):
        at = begin + batch * BATCH + u
        code = list_ref[lax.shift_right_logical(at, 7), lax.bitwise_and(at, 127)]
        code = jnp.where(at < end, code, (skipped + targets) * 256)
        return lax.shift_right_logical(code, 8), lax.bitwise_and(code, 255)

    def make(batch, slot):
        for u in range(BATCH):
            target, source = pair(batch, u)
            square = jnp.dot(source_ref[source], target_ref[jnp.minimum(base + target, blank)], preferred_element_type=f32)
            slot[u] = lax.rsqrt(square).astype(bf16)

    def use(batch, slot):
        sums = []
        for u in range(BATCH):
            target, source = pair(batch, u)
            charges = jnp.concatenate([mine_ref[:, cluster(source)], other_ref[:, cluster(source)]], axis=0)
            sums.append((target, jnp.dot(charges, slot[u], preferred_element_type=f32)))
        for target, value in sums:
            total[target - skipped] += value

    make(0, even)

    def body(step, carry):
        make(2 * step + 1, odd)
        use(2 * step, even)
        make(2 * step + 2, even)
        use(2 * step + 1, odd)
        return carry

    lax.fori_loop(0, lax.div(batches, 2), body, 0)

    @pl.when(lax.rem(batches, 2) == 1)
    def _():
        use(batches - 1, even)

    for i in range(targets):
        out_ref[:, i * LEAF : (i + 1) * LEAF] = total[i].astype(out_ref.dtype)


def near_sum(base, part, microseconds, targets, pairs, target_rows, source_rows, mine, other, dtype):
    columns = 2 * mine.shape[0]
    return pl.pallas_call(
        functools.partial(near_kernel, base, part),
        out_shape=jax.ShapeDtypeStruct((columns, targets * LEAF), dtype),
        in_specs=[SMEM] + [VMEM] * 4,
        out_specs=VMEM,
        scratch_shapes=[
            pltpu.VMEM((targets + 1, columns, LEAF), f32),
            pltpu.VMEM((BATCH, LEAF, LEAF), bf16),
            pltpu.VMEM((BATCH, LEAF, LEAF), bf16),
        ],
        compiler_params=PARAMS,
        cost_estimate=cost(microseconds),
    )(pairs, target_rows, source_rows, mine, other)


def far_sum(out_ref, basis_ref, target, at, coefficient):
    out_ref[:, target * LEAF : (target + 1) * LEAF] = lax.dot_general(
        coefficient.astype(bf16),
        basis_ref[:, cluster(at)],
        (((0,), (0,)), ((), ())),
        preferred_element_type=f32,
    )


def far_kernel(seg_size, far_ref, couplings_ref, basis_ref, part, out_ref, skel):
    leaf = lax.axis_index("leaf") * couplings_ref.shape[0]
    clusters, far_count, rank, _ = couplings_ref.shape
    columns = out_ref.shape[0]
    pack = LEAF // columns

    def unpack(group, carry):
        block = part[pl.ds(pl.multiple_of(group * rank, rank), rank), :]
        for i in range(pack):
            skel[group * pack + i] = block[:, i * columns : (i + 1) * columns]
        return carry

    lax.fori_loop(0, part.shape[0] // rank, unpack, 0)
    for target in range(clusters):
        coefficient = jnp.zeros((rank, columns), f32)
        step = 256 // rank
        for at in range(0, far_count, step):
            left = jnp.concatenate([couplings_ref[target, at + i] for i in range(step)], axis=1)
            rows = [skel[far_ref[target, at + i]] for i in range(step)]
            coefficient = coefficient + jnp.dot(
                left, jnp.concatenate(rows, axis=0), preferred_element_type=f32
            )
        far_sum(out_ref, basis_ref, target, leaf + target, coefficient)


def far_kernel_phased(seg_size, far_ref, couplings_ref, basis_ref, *refs):
    parts, (out_ref, skel, side, held) = refs[:-4], refs[-4:]
    clusters, far_count, rank, _ = couplings_ref.shape
    columns = out_ref.shape[0]
    pack = LEAF // columns
    leaf = lax.axis_index("leaf") * clusters
    for target in range(clusters):
        for at in range(0, far_count, pack):
            side[target, :, at * rank : (at + pack) * rank] = jnp.concatenate(
                [couplings_ref[target, at + i] for i in range(pack)], axis=1
            )
    for order, part in enumerate(parts):
        for group in range(seg_size // pack):
            block = part[group * rank : (group + 1) * rank, :]
            for i in range(pack):
                skel[order * seg_size + group * pack + i] = block[:, i * columns : (i + 1) * columns]
    step = 256 // rank
    for target in range(clusters):
        coefficient = jnp.zeros((rank, columns), f32)
        for at in range(0, far_count, step):
            rows = [skel[far_ref[target, at + i]] for i in range(step)]
            coefficient = coefficient + jnp.dot(
                side[target, :, at * rank : (at + step) * rank],
                jnp.concatenate(rows, axis=0),
                preferred_element_type=f32,
            )
        held[target] = coefficient.astype(bf16)
    for target in range(clusters):
        far_sum(out_ref, basis_ref, target, leaf + target, held[target])


def on_device(points, charges, basis, couplings, near_src, far_src):
    blk_count = lax.axis_size("blk")
    mine = charges.T
    columns, seg_rows = mine.shape
    seg_size = seg_rows // LEAF
    rank = basis.shape[0]
    own_clusters, near_count = near_src.shape
    cluster_total = seg_size * blk_count
    pack = LEAF // columns
    skel_rows = seg_size // pack * rank
    other = shifted(mine, "rhs", 1)
    own_list, load = pl.pallas_call(
        functools.partial(list_kernel, seg_size),
        out_shape=[
            jax.ShapeDtypeStruct((8, LEAF), jnp.int32),
            jax.ShapeDtypeStruct((skel_rows + 16, LEAF), bf16),
        ],
        in_specs=[HBM] * 3,
        out_specs=[VMEM] * 2,
        scratch_shapes=[
            pltpu.VMEM(near_src.shape, jnp.int32),
            pltpu.VMEM(basis.shape, bf16),
            pltpu.VMEM(mine.shape, bf16),
            pltpu.SemaphoreType.DMA((3,)),
        ],
        compiler_params=pltpu.CompilerParams(vmem_limit_bytes=63 * 2**20),
        cost_estimate=cost(3.0),
    )(near_src, basis, mine)

    points, load = lax.optimization_barrier((points, load))
    first_load = crossed(load, 1)
    target_rows, source_rows = pl.pallas_call(
        functools.partial(feature_kernel, seg_size, own_clusters),
        out_shape=[
            jax.ShapeDtypeStruct((2 * own_clusters + 1, DEPTH, LEAF), bf16),
            jax.ShapeDtypeStruct((seg_size, LEAF, DEPTH), bf16),
        ],
        in_specs=[VMEM],
        out_specs=[VMEM, VMEM],
        compiler_params=PARAMS,
        cost_estimate=cost(0.7),
    )(points)
    target_rows, later_load = lax.optimization_barrier((target_rows, load))
    narrow = blk_count == 4 and cluster_total <= 256
    if narrow:
        loads = [load, crossed(later_load, -1), shifted(later_load, "blk", 2), first_load]
    else:
        loads = [lax.all_gather(later_load[:skel_rows], "blk", axis=0, tiled=True)]
    args = (target_rows, source_rows, mine, other)
    codes = first_load[skel_rows:].astype(jnp.int32)
    pairs = codes[:8] + 256 * codes[8:]
    low = near_sum(0, 0, 20.0, own_clusters // 2, pairs, *args, bf16)
    low, pairs = lax.optimization_barrier((low, pairs))
    low_back = crossed(low, -1)
    high = near_sum(0, 1, 20.0, own_clusters // 2, pairs, *args, bf16)
    high, own_list = lax.optimization_barrier((high, own_list))
    high_back = crossed(high, -1)
    own_near = near_sum(own_clusters, None, 0.5, own_clusters, own_list, *args, f32)
    own_near, loads, low_back = lax.optimization_barrier((own_near, loads, low_back))

    blk = lax.axis_index("blk")
    first = blk * seg_size + lax.axis_index("leaf") * own_clusters
    entries = lax.dynamic_slice_in_dim(far_src, first, own_clusters, 0)
    far_shape = jax.ShapeDtypeStruct((columns, own_clusters * LEAF), f32)
    if narrow:
        segment = lax.div(entries, seg_size)
        ahead = jnp.where(lax.axis_index("rhs") == 0, segment - blk, blk - segment)
        order = lax.rem(ahead + blk_count, blk_count)
        entries = entries + (order - segment) * seg_size
        far = pl.pallas_call(
            functools.partial(far_kernel_phased, seg_size),
            out_shape=far_shape,
            in_specs=[SMEM] + [VMEM] * 6,
            out_specs=VMEM,
            scratch_shapes=[
                pltpu.VMEM((cluster_total, rank, columns), bf16),
                pltpu.VMEM((own_clusters, rank, far_src.shape[1] * rank), bf16),
                pltpu.VMEM((own_clusters, rank, columns), bf16),
            ],
            compiler_params=PARAMS,
            cost_estimate=cost(20.0),
        )(entries, couplings, basis, *loads)
    else:
        far = pl.pallas_call(
            functools.partial(far_kernel, seg_size),
            out_shape=far_shape,
            in_specs=[SMEM] + [VMEM] * 3,
            out_specs=VMEM,
            scratch_shapes=[pltpu.VMEM((cluster_total, rank, columns), bf16)],
            compiler_params=PARAMS,
        )(entries, couplings, basis, *loads)

    far, low_back, high_back = lax.optimization_barrier((far, low_back, high_back))
    near = own_near + jnp.concatenate([low_back, high_back], axis=1).astype(f32)
    got = shifted(near[columns:].astype(bf16), "rhs", 1)
    return (near[:columns] + got.astype(f32) + far).astype(bf16).T


def solution(mesh):
    in_specs = (
        P(None, "groups"),
        P(("groups", "blk"), "rhs"),
        P(None, ("groups", "blk")),
        P(("groups", "blk", "leaf"), None, None, None),
        P(("groups", "blk", "leaf"), None),
        P("groups", None),
    )
    out_specs = P(("groups", "blk", "leaf"), "rhs")
    return jax.shard_map(
        on_device, mesh=mesh, in_specs=in_specs, out_specs=out_specs, check_vma=False
    )
```

```python
import functools

import jax
import jax.numpy as jnp
from jax import lax
from jax.experimental import pallas as pl
from jax.experimental.pallas import tpu as pltpu
from jax.sharding import PartitionSpec as P

LEAF = 128
BATCH = 18
DEPTH = 48

kernel_scale = 0.0625 / (4.0 * 3.141592653589793)
soften = 0.001
inverse_sq = 1.0 / (kernel_scale * kernel_scale)

bf16 = jnp.bfloat16
f32 = jnp.float32
VMEM = pl.BlockSpec(memory_space=pltpu.VMEM)
HBM = pl.BlockSpec(memory_space=pltpu.HBM)
SMEM = pl.BlockSpec(memory_space=pltpu.SMEM)
PARAMS = pltpu.CompilerParams(vmem_limit_bytes=48 * 2**20)


def cost(microseconds):
    return pl.CostEstimate(flops=int(microseconds * 1e9), bytes_accessed=0, transcendentals=0)


def shifted(block, axis, shift):
    count = lax.axis_size(axis)
    return lax.ppermute(block, axis, [(i, (i + shift) % count) for i in range(count)])


def crossed(block, shift):
    count = lax.axis_size("blk")
    pairs = []
    for i in range(count):
        pairs.append((2 * i, (i + shift) % count * 2))
        pairs.append((2 * i + 1, (i - shift) % count * 2 + 1))
    return lax.ppermute(block, ("blk", "rhs"), pairs)


def cluster(index):
    return pl.ds(pl.multiple_of(index * LEAF, LEAF), LEAF)


def list_kernel(seg_size, near_hbm, basis_hbm, charges_hbm, own_ref, load_ref, near_ref, basis_ref, charges_ref, sems):
    copies = [
        pltpu.make_async_copy(near_hbm, near_ref, sems.at[0]),
        pltpu.make_async_copy(basis_hbm, basis_ref, sems.at[1]),
        pltpu.make_async_copy(charges_hbm, charges_ref, sems.at[2]),
    ]
    for copy in copies:
        copy.start()
    targets, near_count = near_ref.shape
    blk_count = lax.axis_size("blk")
    blk = lax.axis_index("blk")
    before = lax.rem(blk + blk_count - 1, blk_count)
    half = lax.axis_index("rhs")
    columns = charges_ref.shape[0]
    rank = basis_ref.shape[0]
    pack = LEAF // columns
    slots = 4 if near_count <= LEAF // 4 and targets % 4 == 0 else 1
    width = LEAF // slots
    lines = targets // slots

    def iota(shape, dim):
        return lax.broadcasted_iota(jnp.int32, shape, dim)

    def ones(condition):
        return jnp.where(condition, 1.0, 0.0).astype(bf16)

    lane = iota((lines, LEAF), 1)
    target = iota((lines, LEAF), 0) * slots + lane // width
    in_half = target // (targets // 2) == half
    earlier = ones(iota((LEAF, LEAF), 0) < iota((LEAF, LEAF), 1))
    whole = jnp.ones((LEAF, LEAF), bf16)
    above = ones(iota((lines, lines), 1) < iota((lines, lines), 0))
    row = iota((8, LEAF), 0)
    lower = iota((LEAF, LEAF), 0)
    filler = jnp.full((1, width - near_count), -1, jnp.int32)
    copies[0].wait()
    packed = []
    for line in range(lines):
        pieces = []
        for i in range(slots):
            at = line * slots + i
            pieces += [near_ref[at : at + 1, :], filler]
        packed.append(jnp.concatenate(pieces, axis=1))
    sources = jnp.concatenate(packed, axis=0)
    if seg_size & (seg_size - 1) == 0:
        segment = lax.shift_right_arithmetic(sources, seg_size.bit_length() - 1)
    else:
        segment = lax.div(sources, seg_size)
    local = (sources - segment * seg_size).astype(f32)
    is_own = segment == blk
    is_prev = jnp.logical_and(segment == before, jnp.logical_not(is_own))
    is_next = jnp.logical_and(sources >= 0, jnp.logical_not(jnp.logical_or(is_own, is_prev)))
    is_own = jnp.logical_and(jnp.logical_and(is_own, in_half), sources >= 0)
    is_prev = jnp.logical_and(is_prev, sources >= 0)
    leaving = jnp.where(half == 0, jnp.where(is_next, 1, 0), jnp.where(is_prev, 1, 0))
    masks = (is_own, leaving == 1)
    place = jnp.zeros((lines, LEAF), f32)
    totals, middles = [], []
    for mask in masks:
        within = jnp.dot(ones(mask), earlier, preferred_element_type=f32)
        count = jnp.dot(ones(mask), whole, preferred_element_type=f32)
        start = jnp.dot(above, count.astype(bf16), preferred_element_type=f32)
        place = jnp.where(mask, start + within, place)
        totals.append(start[lines - 1 :, :] + count[lines - 1 :, :])
        middles.append(start[lines // 2 : lines // 2 + 1, :])
    place = place.astype(jnp.int32)
    target = target.astype(f32)
    left, right = [], []
    for line in range(lines):
        at = place[line : line + 1, :]
        here = lax.shift_right_logical(at, 7) == row
        rows = []
        for mask in masks:
            chosen = jnp.logical_and(here, jnp.where(mask[line : line + 1, :], 1, 0) == 1)
            rows.append(jnp.where(chosen, local[line : line + 1, :], 0.0))
            rows.append(jnp.where(chosen, target[line : line + 1, :], 0.0))
        left.append(jnp.concatenate(rows, axis=0).astype(bf16))
        right.append(ones(lax.bitwise_and(at, LEAF - 1) == lower))
    lists = lax.dot_general(
        jnp.concatenate(left, axis=1),
        jnp.concatenate(right, axis=1),
        (((1,), (1,)), ((), ())),
        preferred_element_type=f32,
    )
    last = row * LEAF + iota((8, LEAF), 1) == 8 * LEAF - 1
    own = lists[:8] + 256.0 * lists[8:16]
    own_ref[...] = jnp.where(last, totals[0], own).astype(jnp.int32)
    prior = row * LEAF + iota((8, LEAF), 1) == 8 * LEAF - 2
    length = jnp.where(prior, middles[1], totals[1])
    high = jnp.floor(length * (1.0 / 256.0))
    ends = jnp.logical_or(last, prior)
    away = jnp.concatenate(
        [jnp.where(ends, length - 256.0 * high, lists[16:24]), jnp.where(ends, high, lists[24:32])], axis=0
    )
    rows_end = seg_size // pack * rank
    load_ref[rows_end : rows_end + 16, :] = away.astype(bf16)

    copies[1].wait()
    copies[2].wait()
    singles = []
    for index in range(seg_size):
        at = index * LEAF
        singles.append(
            lax.dot_general(
                basis_ref[:, at : at + LEAF],
                charges_ref[:, at : at + LEAF],
                (((1,), (1,)), ((), ())),
                preferred_element_type=f32,
            )
        )
    blocks = [jnp.concatenate(singles[i : i + pack], axis=1) for i in range(0, seg_size, pack)]
    for group, block in enumerate(blocks):
        load_ref[group * rank : (group + 1) * rank, :] = block.astype(bf16)


def split(value):
    high = value.astype(bf16).astype(f32)
    rest = value - high
    middle = rest.astype(bf16).astype(f32)
    return high, middle, rest - middle


def coords_of(points_ref, at):
    block = points_ref[:, cluster(at)]
    zero, one, two = block[0:1, :], block[1:2, :], block[2:3, :]
    return zero, one, two, zero * zero + one * one + two * two


def rows_of(values):
    row = lax.broadcasted_iota(jnp.int32, (8, LEAF), 0)
    out = jnp.zeros((8, LEAF), f32)
    for i, value in enumerate(values):
        out = jnp.where(row == i, value, out)
    return out


def target_features(points_ref, at):
    zero, one, two, norm = coords_of(points_ref, at)
    slope = -2.0 * inverse_sq
    rows = rows_of((zero * slope, one * slope, two * slope, (norm + soften) * inverse_sq, 1.0))
    high, middle, low = split(rows)
    return jnp.concatenate([high, high, middle, middle, high, low], axis=0).astype(bf16)


def source_features(points_ref, at):
    zero, one, two, norm = coords_of(points_ref, at)
    rows = rows_of((zero, one, two, 1.0, norm * inverse_sq))
    high, middle, low = split(rows)
    stacked = jnp.concatenate([high, middle, high, middle, low, high], axis=0)
    return jnp.transpose(stacked).astype(bf16)


def feature_kernel(seg_size, targets, points_ref, target_ref, source_ref):
    blk_count = lax.axis_size("blk")
    blk = lax.axis_index("blk")
    first = lax.axis_index("leaf") * targets
    away = lax.rem(blk + 2 * lax.axis_index("rhs") + blk_count - 1, blk_count)
    for which, segment in enumerate((away, blk)):
        for i in range(targets):
            target_ref[which * targets + i] = target_features(points_ref, segment * seg_size + first + i)
    target_ref[2 * targets] = jnp.zeros((DEPTH, LEAF), bf16)

    def some_sources(step, carry):
        for u in range(8):
            at = step * 8 + u
            source_ref[at] = source_features(points_ref, blk * seg_size + at)
        return carry

    lax.fori_loop(0, seg_size // 8, some_sources, 0)


def near_kernel(base, part, list_ref, target_ref, source_ref, mine_ref, other_ref, out_ref, total, even, odd):
    targets = total.shape[0] - 1
    blank = target_ref.shape[0] - 1
    skipped = targets if part == 1 else 0
    begin = list_ref[7, LEAF - 2] if part == 1 else 0
    end = list_ref[7, LEAF - 2] if part == 0 else list_ref[7, LEAF - 1]
    batches = lax.div(end - begin + (BATCH - 1), BATCH)
    total[...] = jnp.zeros_like(total)

    def pair(batch, u):
        at = begin + batch * BATCH + u
        code = list_ref[lax.shift_right_logical(at, 7), lax.bitwise_and(at, 127)]
        code = jnp.where(at < end, code, (skipped + targets) * 256)
        return lax.shift_right_logical(code, 8), lax.bitwise_and(code, 255)

    def make(batch, slot):
        for u in range(BATCH):
            target, source = pair(batch, u)
            square = jnp.dot(source_ref[source], target_ref[jnp.minimum(base + target, blank)], preferred_element_type=f32)
            slot[u] = lax.rsqrt(square).astype(bf16)

    def use(batch, slot):
        sums = []
        for u in range(BATCH):
            target, source = pair(batch, u)
            charges = jnp.concatenate([mine_ref[:, cluster(source)], other_ref[:, cluster(source)]], axis=0)
            sums.append((target, jnp.dot(charges, slot[u], preferred_element_type=f32)))
        for target, value in sums:
            total[target - skipped] += value

    make(0, even)

    def body(step, carry):
        make(2 * step + 1, odd)
        use(2 * step, even)
        make(2 * step + 2, even)
        use(2 * step + 1, odd)
        return carry

    lax.fori_loop(0, lax.div(batches, 2), body, 0)

    @pl.when(lax.rem(batches, 2) == 1)
    def _():
        use(batches - 1, even)

    for i in range(targets):
        out_ref[:, i * LEAF : (i + 1) * LEAF] = total[i].astype(out_ref.dtype)


def near_sum(base, part, microseconds, targets, pairs, target_rows, source_rows, mine, other, dtype):
    columns = 2 * mine.shape[0]
    return pl.pallas_call(
        functools.partial(near_kernel, base, part),
        out_shape=jax.ShapeDtypeStruct((columns, targets * LEAF), dtype),
        in_specs=[SMEM] + [VMEM] * 4,
        out_specs=VMEM,
        scratch_shapes=[
            pltpu.VMEM((targets + 1, columns, LEAF), f32),
            pltpu.VMEM((BATCH, LEAF, LEAF), bf16),
            pltpu.VMEM((BATCH, LEAF, LEAF), bf16),
        ],
        compiler_params=PARAMS,
        cost_estimate=cost(microseconds),
    )(pairs, target_rows, source_rows, mine, other)


def far_sum(out_ref, basis_ref, target, at, coefficient):
    out_ref[:, target * LEAF : (target + 1) * LEAF] = lax.dot_general(
        coefficient.astype(bf16),
        basis_ref[:, cluster(at)],
        (((0,), (0,)), ((), ())),
        preferred_element_type=f32,
    )


def far_kernel(seg_size, far_ref, couplings_ref, basis_ref, part, out_ref, skel):
    leaf = lax.axis_index("leaf") * couplings_ref.shape[0]
    clusters, far_count, rank, _ = couplings_ref.shape
    columns = out_ref.shape[0]
    pack = LEAF // columns

    def unpack(group, carry):
        block = part[pl.ds(pl.multiple_of(group * rank, rank), rank), :]
        for i in range(pack):
            skel[group * pack + i] = block[:, i * columns : (i + 1) * columns]
        return carry

    lax.fori_loop(0, part.shape[0] // rank, unpack, 0)
    for target in range(clusters):
        coefficient = jnp.zeros((rank, columns), f32)
        step = 256 // rank
        for at in range(0, far_count, step):
            left = jnp.concatenate([couplings_ref[target, at + i] for i in range(step)], axis=1)
            rows = [skel[far_ref[target, at + i]] for i in range(step)]
            coefficient = coefficient + jnp.dot(
                left, jnp.concatenate(rows, axis=0), preferred_element_type=f32
            )
        far_sum(out_ref, basis_ref, target, leaf + target, coefficient)


def far_kernel_phased(seg_size, far_ref, couplings_ref, basis_ref, *refs):
    parts, (out_ref, skel, side, held) = refs[:-4], refs[-4:]
    clusters, far_count, rank, _ = couplings_ref.shape
    columns = out_ref.shape[0]
    pack = LEAF // columns
    leaf = lax.axis_index("leaf") * clusters
    for target in range(clusters):
        for at in range(0, far_count, pack):
            side[target, :, at * rank : (at + pack) * rank] = jnp.concatenate(
                [couplings_ref[target, at + i] for i in range(pack)], axis=1
            )
    for order, part in enumerate(parts):
        for group in range(seg_size // pack):
            block = part[group * rank : (group + 1) * rank, :]
            for i in range(pack):
                skel[order * seg_size + group * pack + i] = block[:, i * columns : (i + 1) * columns]
    step = 256 // rank
    for target in range(clusters):
        coefficient = jnp.zeros((rank, columns), f32)
        for at in range(0, far_count, step):
            rows = [skel[far_ref[target, at + i]] for i in range(step)]
            coefficient = coefficient + jnp.dot(
                side[target, :, at * rank : (at + step) * rank],
                jnp.concatenate(rows, axis=0),
                preferred_element_type=f32,
            )
        held[target] = coefficient.astype(bf16)
    for target in range(clusters):
        far_sum(out_ref, basis_ref, target, leaf + target, held[target])


def on_device(points, charges, basis, couplings, near_src, far_src):
    blk_count = lax.axis_size("blk")
    mine = charges.T
    columns, seg_rows = mine.shape
    seg_size = seg_rows // LEAF
    rank = basis.shape[0]
    own_clusters, near_count = near_src.shape
    cluster_total = seg_size * blk_count
    pack = LEAF // columns
    skel_rows = seg_size // pack * rank
    other = shifted(mine, "rhs", 1)
    own_list, load = pl.pallas_call(
        functools.partial(list_kernel, seg_size),
        out_shape=[
            jax.ShapeDtypeStruct((8, LEAF), jnp.int32),
            jax.ShapeDtypeStruct((skel_rows + 16, LEAF), bf16),
        ],
        in_specs=[HBM] * 3,
        out_specs=[VMEM] * 2,
        scratch_shapes=[
            pltpu.VMEM(near_src.shape, jnp.int32),
            pltpu.VMEM(basis.shape, bf16),
            pltpu.VMEM(mine.shape, bf16),
            pltpu.SemaphoreType.DMA((3,)),
        ],
        compiler_params=pltpu.CompilerParams(vmem_limit_bytes=63 * 2**20),
        cost_estimate=cost(3.0),
    )(near_src, basis, mine)

    points, load = lax.optimization_barrier((points, load))
    first_load = crossed(load, 1)
    target_rows, source_rows = pl.pallas_call(
        functools.partial(feature_kernel, seg_size, own_clusters),
        out_shape=[
            jax.ShapeDtypeStruct((2 * own_clusters + 1, DEPTH, LEAF), bf16),
            jax.ShapeDtypeStruct((seg_size, LEAF, DEPTH), bf16),
        ],
        in_specs=[VMEM],
        out_specs=[VMEM, VMEM],
        compiler_params=PARAMS,
        cost_estimate=cost(0.7),
    )(points)
    target_rows, later_load = lax.optimization_barrier((target_rows, load))
    narrow = blk_count == 4 and cluster_total <= 256
    if narrow:
        loads = [load, crossed(later_load, -1), shifted(later_load, "blk", 2), first_load]
    else:
        loads = [lax.all_gather(later_load[:skel_rows], "blk", axis=0, tiled=True)]
    args = (target_rows, source_rows, mine, other)
    codes = first_load[skel_rows:].astype(jnp.int32)
    pairs = codes[:8] + 256 * codes[8:]
    low = near_sum(0, 0, 20.0, own_clusters // 2, pairs, *args, bf16)
    low, pairs = lax.optimization_barrier((low, pairs))
    low_back = crossed(low, -1)
    high = near_sum(0, 1, 20.0, own_clusters // 2, pairs, *args, bf16)
    high, own_list = lax.optimization_barrier((high, own_list))
    high_back = crossed(high, -1)
    own_near = near_sum(own_clusters, None, 0.5, own_clusters, own_list, *args, f32)
    own_near, loads, low_back = lax.optimization_barrier((own_near, loads, low_back))

    blk = lax.axis_index("blk")
    first = blk * seg_size + lax.axis_index("leaf") * own_clusters
    entries = lax.dynamic_slice_in_dim(far_src, first, own_clusters, 0)
    far_shape = jax.ShapeDtypeStruct((columns, own_clusters * LEAF), f32)
    if narrow:
        segment = lax.div(entries, seg_size)
        ahead = jnp.where(lax.axis_index("rhs") == 0, segment - blk, blk - segment)
        order = lax.rem(ahead + blk_count, blk_count)
        entries = entries + (order - segment) * seg_size
        far = pl.pallas_call(
            functools.partial(far_kernel_phased, seg_size),
            out_shape=far_shape,
            in_specs=[SMEM] + [VMEM] * 6,
            out_specs=VMEM,
            scratch_shapes=[
                pltpu.VMEM((cluster_total, rank, columns), bf16),
                pltpu.VMEM((own_clusters, rank, far_src.shape[1] * rank), bf16),
                pltpu.VMEM((own_clusters, rank, columns), bf16),
            ],
            compiler_params=PARAMS,
            cost_estimate=cost(20.0),
        )(entries, couplings, basis, *loads)
    else:
        far = pl.pallas_call(
            functools.partial(far_kernel, seg_size),
            out_shape=far_shape,
            in_specs=[SMEM] + [VMEM] * 3,
            out_specs=VMEM,
            scratch_shapes=[pltpu.VMEM((cluster_total, rank, columns), bf16)],
            compiler_params=PARAMS,
        )(entries, couplings, basis, *loads)

    far, low_back, high_back = lax.optimization_barrier((far, low_back, high_back))
    near = own_near + jnp.concatenate([low_back, high_back], axis=1).astype(f32)
    got = shifted(near[columns:].astype(bf16), "rhs", 1)
    return (near[:columns] + got.astype(f32) + far).astype(bf16).T


def solution(mesh):
    in_specs = (
        P(None, "groups"),
        P(("groups", "blk"), "rhs"),
        P(None, ("groups", "blk")),
        P(("groups", "blk", "leaf"), None, None, None),
        P(("groups", "blk", "leaf"), None),
        P("groups", None),
    )
    out_specs = P(("groups", "blk", "leaf"), "rhs")
    return jax.shard_map(
        on_device, mesh=mesh, in_specs=in_specs, out_specs=out_specs, check_vma=False
    )
```
